128 devices in a mesh: head: 16 (over y, z), qblk: 8 (over x, core).
Axes of the slice: x: 4, y: 4, z: 4, core: 2. Of those that a mesh axis runs over, the one named last changes fastest.
Arguments:
- residual: bfloat16 [4096, 2048], P(('qblk', 'head')), may hold values from -6 to 6
- queries: bfloat16 [4096, 4096], P('qblk', 'head'), may hold values from -30 to 30
- key_cache: bfloat16 [4, 2048, 128], P(None, 'qblk'), may hold values from -6 to 6
- value_cache: bfloat16 [4, 2048, 128], P(None, 'qblk'), may hold values from -6 to 6
- visible_len: int32 [4096], P('qblk'), may hold values from 256 to 2048
- out_weight: bfloat16 [4096, 2048], P('head'), may hold values from -0.5 to 0.5
- norm_gain: float32 [2048], replicated, may hold values from 0.1 to 1.9
- expert_ids: int32 [4096, 8], P(('qblk', 'head')), may hold values from 0 to 127, all different within a row; in each aligned block of 32 rows (0 to 31, 32 to 63, ...) at most 4 rows name the same one
- route_weights: float32 [4096, 8], P(('qblk', 'head')), may hold values from 0.02 to 0.3
- w_gate: bfloat16 [128, 2048, 768], P(('head', 'qblk')), may hold values from -0.125 to 0.125
- w_up: bfloat16 [128, 2048, 768], P(('head', 'qblk')), may hold values from -0.125 to 0.125
- w_down: bfloat16 [128, 768, 2048], P(('head', 'qblk')), may hold values from -0.21875 to 0.21875
Outputs:
- layer_out: bfloat16 [4096, 2048], P(('qblk', 'head'))
The draws below stay inside these ranges and needn't reach their ends.
Inputs may be any that keep to these rules, and one draw needn't show every extreme that they name: `expert_ids`: each row names 8 different experts; in each aligned block of 32 rows (the rows of one device) no expert is named more than 4 times, and some block names some expert exactly 4 times.
All inputs are finite; a program needn't handle non-finite values.
Results may differ from the reference program's by a relative error of at most 0.012.
Values may be sent and summed in bfloat16 or wider, within the bound.
A program may use at most 64 MiB of HBM per device.

```python
import math
import jax
import jax.numpy as jnp
import numpy as np
from jax import lax

D = 2048
QH = 32
KVH = 4
HD = 128
FF = 768
TOPK = 8
EXPERTS = 128
KEYS = 2048
TOK_DEV = 32
TOKENS = 4096
CAP = 4


def base_keys(key):
    raw = jnp.clip(jax.random.normal(jax.random.fold_in(key, 11), (KVH, KEYS, HD), jnp.float32), -6.0, 6.0)
    return raw.astype(jnp.bfloat16)


def draw_key_cache(key, part):
    return base_keys(key)


def draw_queries(key, part):
    drawn = jnp.clip(jax.random.normal(jax.random.fold_in(key, 23), (TOKENS, QH, HD), jnp.float32), -6.0, 6.0)
    return drawn.reshape(TOKENS, QH * HD).astype(jnp.bfloat16)


def set_ends(values, stream_key, least, largest):
    longest = values.shape.index(max(values.shape))
    spots = []
    for shift in (0, 1):
        where = [jax.random.randint(jax.random.fold_in(stream_key, axis), (), 0, length) for axis, length in enumerate(values.shape)]
        where[longest] = (where[longest] + shift) % values.shape[longest]
        spots.append(tuple(where))
    return values.at[spots[0]].set(least).at[spots[1]].set(largest)


def block_scale(stream_key, shape, pieces, smallest, top_value):
    def one(dim, parts):
        draws = jax.random.uniform(jax.random.fold_in(jax.random.fold_in(stream_key, 6), dim), (parts,), jnp.float32, smallest / len(pieces), top_value / len(pieces))
        return jnp.repeat(jnp.exp(draws), shape[dim] // parts).reshape((-1,) + (1,) * (len(shape) - dim - 1))

    factor_of = one(*pieces[0])
    for cut in pieces[1:]:
        factor_of = factor_of * one(*cut)
    return factor_of


def routed_block(key, own, number, rows, count, top, most, slope):
    sequence = jax.random.permutation(key, count)
    heavy_load, ordinary = load_shares(count, rows * top, most, slope, True), load_shares(count, rows * top, most, slope, False)
    places = jnp.arange(count)

    def named(sizes, rotation):
        used = int((sizes > 0).sum())
        fixed = max(1, used // 4)
        moved = fixed + (places - fixed + rotation * (used - fixed)) % max(1, count - fixed)
        return jnp.zeros((count,), jnp.int32).at[sequence[jnp.where(places < fixed, places, moved)]].set(jnp.asarray(sizes, jnp.int32))

    sizes = jnp.where(number % 4 == 0, named(heavy_load, number // 4), named(ordinary, number - number // 4 - 1))
    mixed = jax.random.permutation(jax.random.fold_in(own, 3), count)
    giver, receiver = mixed[0:count // 2 * 2:2], mixed[1:count // 2 * 2:2]
    room = jnp.minimum(sizes[giver] - 1, most - sizes[receiver]) // 2
    room = jnp.where((giver == sequence[0]) | (receiver == sequence[0]) | (sizes[receiver] == 0), 0, jnp.maximum(room, 0))
    moved = jax.random.randint(jax.random.fold_in(own, 4), (count // 2,), 0, 1 << 20) % (room + 1)
    sizes = sizes.at[giver].add(-moved).at[receiver].add(moved)
    items = jnp.searchsorted(jnp.cumsum(sizes), jnp.arange(rows * top), side="right").astype(jnp.int32)
    table = items.reshape(top, rows).T
    table = table[jax.random.permutation(jax.random.fold_in(own, 1), rows)]
    rotation = jax.random.randint(jax.random.fold_in(own, 2), (rows, 1), 0, top)
    return jnp.take_along_axis(table, (jnp.arange(top)[None, :] + rotation) % top, axis=1)


def load_shares(number_of, total, reach, skew, full):
    portions = [(1 << 20) // math.isqrt(standing ** skew) + 1 for standing in range(1, number_of + 1)]
    largest = reach if full else min(reach, max(-(-total // number_of), total * portions[0] // sum(portions)))
    least = 1 if total - largest >= number_of - 1 else 0
    holding, rest = [largest] + [least] * (number_of - 1), total - largest - least * (number_of - 1)
    while rest > 0:
        candidates = [i for i in range(1, number_of) if holding[i] < largest] or [i for i in range(1, number_of) if holding[i] < reach]
        pool, left = sum([portions[i] for i in candidates]), rest
        for i in candidates:
            more = min(reach - holding[i], max(1, left * portions[i] // pool), rest)
            holding[i] = holding[i] + more
            rest = rest - more
    return np.array(holding)


def centred(key, shape, width, bound, cuts=(), kind=jnp.bfloat16):
    result = jax.random.normal(key, shape, jnp.float32) * width
    if len(cuts) > 0:
        result = block_scale(key, shape, cuts, -0.22, 0.18) * result
    return jnp.clip(result, min=-bound, max=bound).astype(kind)


def setup_inputs(seed: int = 0) -> dict:
    key_list = jax.random.split(jax.random.key(seed), 13)
    residual = centred(key_list[0], (TOKENS, D), 1.0, 6.0, ((0, 128),))
    queries = draw_queries(jax.random.fold_in(key_list[12], 71), 0)
    key_cache = draw_key_cache(jax.random.fold_in(key_list[12], 71), 0)
    value_cache = centred(key_list[3], (KVH, KEYS, HD), 1.0, 6.0, ((1, 8),))
    visible_len = set_ends(jax.random.randint(key_list[4], (TOKENS,), KEYS // 8, KEYS + 1), jax.random.fold_in(key_list[4], 1), KEYS // 8, KEYS).astype(jnp.int32)
    out_weight = centred(key_list[5], (QH * HD, D), HD ** -0.5, 0.5, ((0, 16),))
    norm_gain = jnp.clip(1.0 + 0.18 * jax.random.normal(key_list[6], (D,), jnp.float32), 0.1, 1.9)
    expert_ids_keys = jax.random.split(jax.random.fold_in(key_list[7], 1), TOKENS // TOK_DEV)
    expert_ids_turns = jax.random.permutation(jax.random.fold_in(key_list[7], 3), TOKENS // TOK_DEV)
    expert_ids = jax.vmap(lambda own, number: routed_block(jax.random.fold_in(key_list[7], 2), own, number, TOK_DEV, EXPERTS, TOPK, CAP, 2))(expert_ids_keys, expert_ids_turns).reshape((TOKENS, TOPK))
    route_weights = jnp.clip(0.02 + 0.28 * jax.random.uniform(key_list[8], (TOKENS, TOPK), jnp.float32) ** block_scale(key_list[8], (TOKENS, TOPK), ((0, 128),), -0.2, 0.2), 0.02, 0.3)
    w_gate = centred(key_list[9], (EXPERTS, D, FF), D ** -0.5, 0.125, ((0, 128),))
    w_up = centred(key_list[10], (EXPERTS, D, FF), D ** -0.5, 0.125, ((0, 128),))
    w_down = centred(key_list[11], (EXPERTS, FF, D), FF ** -0.5, 0.21875, ((0, 128),))
    return dict(residual=residual, queries=queries, key_cache=key_cache, value_cache=value_cache, visible_len=visible_len, out_weight=out_weight, norm_gain=norm_gain, expert_ids=expert_ids, route_weights=route_weights, w_gate=w_gate, w_up=w_up, w_down=w_down)


def reference(residual, queries, key_cache, value_cache, visible_len, out_weight, norm_gain, expert_ids, route_weights, w_gate, w_up, w_down):
    group_size = QH // KVH
    score_scale = HD ** (-0.5)
    key_pos = jnp.arange(KEYS, dtype=jnp.int32)
    visible = key_pos[None, :] < visible_len[:, None]

    def one_head(head_idx):
        head_query = lax.dynamic_slice_in_dim(queries, head_idx * HD, HD, 1)
        kv_idx = head_idx // group_size
        head_keys = key_cache[kv_idx]
        head_values = value_cache[kv_idx]
        scores = jnp.dot(head_query, head_keys.T, preferred_element_type=jnp.float32) * score_scale
        scores = jnp.where(visible, scores, -jnp.inf)
        row_max = lax.optimization_barrier(jnp.max(scores, axis=1, keepdims=True))
        exp_scores = jnp.where(visible, jnp.exp(scores - row_max), 0.0)
        row_sum = lax.optimization_barrier(jnp.sum(exp_scores, axis=1, keepdims=True))
        head_out = jnp.dot(exp_scores.astype(jnp.bfloat16), head_values, preferred_element_type=jnp.float32) / row_sum
        return head_out.astype(jnp.bfloat16)
    stacked = lax.map(one_head, jnp.arange(QH, dtype=jnp.int32))
    attended = jnp.transpose(stacked, (1, 0, 2)).reshape(TOKENS, QH * HD)
    hidden_state = residual.astype(jnp.float32) + jnp.dot(attended, out_weight, preferred_element_type=jnp.float32)
    mean_square = lax.optimization_barrier(jnp.mean(hidden_state * hidden_state, axis=1, keepdims=True))
    normed = (hidden_state * lax.rsqrt(mean_square + 1e-06) * norm_gain).astype(jnp.bfloat16)
    blocks = TOKENS // TOK_DEV
    entries = TOK_DEV * TOPK
    flat_ids = expert_ids.reshape(blocks, entries)
    expert_range = jnp.arange(EXPERTS, dtype=jnp.int32)
    onehot = (flat_ids[:, :, None] == expert_range[None, None, :]).astype(jnp.int32)
    running_rank = (jnp.cumsum(onehot, axis=1) - 1).astype(jnp.int32)
    slot_pos = lax.optimization_barrier(jnp.sum(onehot * running_rank, axis=2)).astype(jnp.int32)
    block_idx = jnp.arange(blocks, dtype=jnp.int32)[:, None]
    entry_idx = jnp.arange(entries, dtype=jnp.int32)[None, :]
    token_idx = (block_idx * TOK_DEV + entry_idx // TOPK).astype(jnp.int32)
    column = (block_idx * CAP + slot_pos).astype(jnp.int32)
    table = jnp.full((EXPERTS, blocks * CAP), TOKENS, jnp.int32).at[flat_ids, column].set(token_idx)
    weight_table = jnp.zeros((EXPERTS, blocks * CAP), jnp.float32).at[flat_ids, column].set(route_weights.reshape(blocks, entries))
    padded = jnp.concatenate([normed, jnp.zeros((1, D), jnp.bfloat16)], axis=0)

    def serve(total, items):
        rows_idx, row_weight, gate_matrix, up_matrix, down_matrix = items
        chosen = padded[rows_idx]
        gate_act = jnp.dot(chosen, gate_matrix, preferred_element_type=jnp.float32)
        up_act = jnp.dot(chosen, up_matrix, preferred_element_type=jnp.float32)
        hidden = (jax.nn.silu(gate_act) * up_act).astype(jnp.bfloat16)
        expert_out = jnp.dot(hidden, down_matrix, preferred_element_type=jnp.float32).astype(jnp.bfloat16)
        total = total.at[rows_idx].add(row_weight[:, None] * expert_out.astype(jnp.float32))
        return (total, None)
    start_total = jnp.zeros((TOKENS + 1, D), jnp.float32)
    mixed, unused = lax.scan(serve, start_total, (table, weight_table, w_gate, w_up, w_down))
    return (hidden_state + mixed[:TOKENS]).astype(jnp.bfloat16)
```

```python
import jax
import jax.numpy as jnp
from jax import lax
from jax.experimental import pallas as pl
from jax.experimental.pallas import tpu as pltpu
from jax.sharding import PartitionSpec as P

MESH = pl.DeviceIdType.MESH
F32, BF16 = jnp.float32, jnp.bfloat16
D = 2048
HD = 128
FF = 768
HALF = D // 2
NEG = -1e30
QSCALE = HD ** (-0.5) * 1.4426950408889634
VMEM_LIMIT = 58 * 1024 * 1024


def dot(a, b):
    return jnp.dot(a, b, preferred_element_type=F32)


def dot_nt(a, b):
    return lax.dot_general(a, b, (((1,), (1,)), ((), ())), preferred_element_type=F32)


def dot_tn(a, b):
    return lax.dot_general(a, b, (((0,), (0,)), ((), ())), preferred_element_type=F32)


def wait_bytes(ref, sem):
    pltpu.make_async_copy(ref, ref, sem).wait()


def attention_kernel(
    q_ref, key_ref, value_ref, vis_ref, res_ref, gain_ref, w_ref,
    hid_ref, normed_ref,
    kv, w_buf, vt, top, den, acc, att, part, got, mid, got2,
    own_sem, w_sem, kv_send, kv_recv, send1, recv1, send2, recv2,
):
    head, qblk = lax.axis_index("head"), lax.axis_index("qblk")
    yy, zz = head // 4, lax.rem(head, 4)
    xx, core = qblk // 2, lax.rem(qblk, 2)
    sibling = 2 * xx + 1 - core

    def remote(src, dst, ssem, rsem, h, q):
        c = pltpu.make_async_remote_copy(
            src_ref=src, dst_ref=dst, send_sem=ssem, recv_sem=rsem,
            device_id=(h, q), device_id_type=MESH,
        )
        c.start()

    w_copy = pltpu.make_async_copy(w_ref, w_buf, w_sem)
    w_copy.start()
    for j, src in enumerate((key_ref, value_ref)):
        remote(src.at[yy], kv.at[qblk, j], kv_send, kv_recv.at[qblk], head, sibling)
        for dx in (1, 3, 2):
            peer = 2 * lax.rem(xx + dx, 4) + core
            remote(src.at[yy], kv.at[qblk, j], kv_send, kv_recv.at[qblk], head, peer)
    for j, src in enumerate((key_ref, value_ref)):
        pltpu.make_async_copy(src.at[yy], kv.at[qblk, j], own_sem).start()
    wait_bytes(kv.at[qblk], own_sem)

    top[...] = jnp.full(top.shape, NEG, F32)
    den[...] = jnp.zeros(den.shape, F32)
    acc[...] = jnp.zeros(acc.shape, F32)

    for dx in (0, 1, 3, 2):
        chip = lax.rem(xx + dx, 4)
        if dx:
            mine = 2 * chip + core
            wait_bytes(kv.at[mine], kv_recv.at[mine])
            remote(kv.at[mine], kv.at[mine], kv_send, kv_recv.at[mine], head, sibling)
        other = 2 * chip + 1 - core
        wait_bytes(kv.at[other], kv_recv.at[other])
        keys = kv[pl.ds(2 * chip, 2), 0].reshape(512, HD)
        vt[...] = kv[pl.ds(2 * chip, 2), 1].reshape(512, HD).astype(F32).T.astype(BF16)
        base = chip * 512

        def rows(i, carry, keys=keys, base=base):
            h, t0 = i // 2, pl.multiple_of(lax.rem(i, 2) * 256, 256)
            q = q_ref[pl.ds(t0, 256), pl.ds(pl.multiple_of(h * HD, HD), HD)]
            cols = pl.ds(pl.multiple_of(i * 256, 256), 256)
            s = dot_nt(keys, q)
            seen = vis_ref[:, pl.ds(t0, 256)] - base
            s = jnp.where(lax.broadcasted_iota(jnp.int32, s.shape, 0) < seen, s, NEG)
            old = top[:, cols]
            new = jnp.maximum(old, jnp.max(s, axis=0, keepdims=True))
            p = jnp.exp2((s - new) * QSCALE)
            scale = jnp.exp2((old - new) * QSCALE)
            top[:, cols] = new
            den[:, cols] = den[:, cols] * scale + jnp.sum(p, axis=0, keepdims=True)
            acc[:, cols] = acc[:, cols] * scale + dot(vt[...], p.astype(BF16))
            return carry

        lax.fori_loop(0, 4, rows, 0)

    for h in range(2):
        cols = slice(h * 512, (h + 1) * 512)
        att[:, h * HD:(h + 1) * HD] = (acc[:, cols] / den[:, cols]).T.astype(BF16)

    w_copy.wait()
    for d in (2, 1, 3, 0):
        z2, y2 = lax.rem(zz + d, 4), lax.rem(yy + d, 4)
        a0 = jnp.concatenate(
            [att[pl.ds(pl.multiple_of((i * 4 + z2) * 32, 32), 32), :] for i in range(4)], axis=0
        )
        part[0, z2] = dot(a0, w_buf[:, :HALF]).astype(BF16)
        if d:
            remote(part.at[0, z2], got.at[0, zz], send1, recv1.at[0, zz], yy * 4 + z2, qblk)
        a1 = att[pl.ds(pl.multiple_of(y2 * 128, 128), 128), :]
        part[1, y2] = dot(a1, w_buf[:, HALF:]).astype(BF16)
        if d:
            remote(part.at[1, y2], got.at[1, yy], send1, recv1.at[1, yy], y2 * 4 + zz, qblk)

    sum0 = part[0, zz].astype(F32)
    sum1 = part[1, yy].astype(F32)
    for d in (1, 3, 2):
        z2, y2 = lax.rem(zz + d, 4), lax.rem(yy + d, 4)
        wait_bytes(got.at[0, z2], recv1.at[0, z2])
        sum0 += got[0, z2].astype(F32)
        wait_bytes(got.at[1, y2], recv1.at[1, y2])
        sum1 += got[1, y2].astype(F32)
    mid[0] = sum0.reshape(4, 32, HALF).astype(BF16)
    mid[1] = sum1.reshape(4, 32, HALF).astype(BF16)
    for d in (2, 1, 3):
        z2, y2 = lax.rem(zz + d, 4), lax.rem(yy + d, 4)
        remote(mid.at[0, y2], got2.at[0, yy], send2, recv2.at[0, yy], y2 * 4 + zz, qblk)
        remote(mid.at[1, z2], got2.at[1, zz], send2, recv2.at[1, zz], yy * 4 + z2, qblk)
    h0 = res_ref[:, :HALF].astype(F32) + mid[0, yy].astype(F32)
    h1 = res_ref[:, HALF:].astype(F32) + mid[1, zz].astype(F32)
    for d in (1, 3, 2):
        z2, y2 = lax.rem(zz + d, 4), lax.rem(yy + d, 4)
        wait_bytes(got2.at[0, y2], recv2.at[0, y2])
        h0 += got2[0, y2].astype(F32)
        wait_bytes(got2.at[1, z2], recv2.at[1, z2])
        h1 += got2[1, z2].astype(F32)
    square = jnp.sum(h0 * h0, axis=1, keepdims=True) + jnp.sum(h1 * h1, axis=1, keepdims=True)
    rs = lax.rsqrt(square * (1.0 / D) + 1e-6)
    hid_ref[:, :HALF] = h0
    hid_ref[:, HALF:] = h1
    normed_ref[:, :HALF] = (h0 * rs * gain_ref[:, :HALF]).astype(BF16)
    normed_ref[:, HALF:] = (h1 * rs * gain_ref[:, HALF:]).astype(BF16)

    wait_bytes(kv.at[pl.ds(0, 7)], kv_send)
    wait_bytes(part.at[:, pl.ds(0, 3)], send1)
    wait_bytes(mid.at[:, pl.ds(0, 3)], send2)


def iota(shape, axis):
    return lax.broadcasted_iota(jnp.int32, shape, axis)


def expert_kernel(
    ids_ref, rw_ref, hid_ref, normed_ref, wg_ref, wu_ref, wd_ref,
    out_ref,
    wg, wu, wd, outbox, inbox, ybox, backbox, mix, x_buf, y_buf,
    w_sem, send1, recv1, send2, recv2,
):
    head, qblk = lax.axis_index("head"), lax.axis_index("qblk")
    me = head * 8 + qblk
    w_copies = [
        pltpu.make_async_copy(src.at[0], dst, w_sem.at[i])
        for i, (src, dst) in enumerate(((wg_ref, wg), (wu_ref, wu), (wd_ref, wd)))
    ]
    for c in w_copies:
        c.start()

    expert = iota((32, 128), 1)
    named = jnp.zeros((32, 128), F32)
    weight = jnp.zeros((32, 128), F32)
    for k in range(8):
        hit = ids_ref[:, k:k + 1] == expert
        named = jnp.where(hit, 1.0, named)
        weight = jnp.where(hit, rw_ref[:, k:k + 1], weight)
    earlier = jnp.where(iota((32, 32), 1) < iota((32, 32), 0), 1.0, 0.0).astype(BF16)
    rank = jnp.where(named > 0.0, dot(earlier, named.astype(BF16)), -1.0)
    rank4 = jnp.concatenate([rank] * 4, axis=0)

    spread = jnp.where(iota((2048, 128), 0) // 16 == iota((2048, 128), 1), 1.0, 0.0).astype(BF16)
    at = dot(spread, rank4.T.astype(BF16))
    j = iota((2048, 128), 0)
    take = (at == lax.rem(j, 4).astype(F32)) & (lax.rem(j // 4, 4) == iota((2048, 128), 1) // 32)
    pick = jnp.where(take, 1.0, 0.0).astype(BF16)
    x4 = jnp.concatenate([normed_ref[:, c * 512:(c + 1) * 512] for c in range(4)], axis=0)
    outbox[...] = dot(pick, x4).astype(BF16)

    def rows16(i):
        return pl.ds(pl.multiple_of(i * 16, 16), 16)

    def dispatch(k, carry):
        e = lax.rem(me + k, 128)
        eh, eq = e // 8, lax.rem(e, 8)
        off = lax.rem(eh - head + 16, 16)
        pltpu.make_async_remote_copy(
            src_ref=outbox.at[rows16(e)], dst_ref=inbox.at[rows16(off * 8 + qblk)],
            send_sem=send1, recv_sem=recv1.at[off // 4],
            device_id=(eh, eq), device_id_type=MESH,
        ).start()
        return carry

    lax.fori_loop(1, 128, dispatch, 0)
    pltpu.make_async_copy(outbox.at[rows16(me)], inbox.at[rows16(qblk)], recv1.at[0]).start()

    spread_t = jnp.where(iota((128, 2048), 1) // 16 == iota((128, 2048), 0), 1.0, 0.0).astype(BF16)
    at_t = dot(rank4.astype(BF16), spread_t)
    jt = iota((128, 2048), 1)
    take_t = (at_t == lax.rem(jt, 4).astype(F32)) & (lax.rem(jt // 4, 4) == iota((128, 2048), 0) // 32)
    high = weight.astype(BF16)
    low = (weight - high.astype(F32)).astype(BF16)
    for i, w in enumerate((high, low)):
        w4 = dot(jnp.concatenate([w] * 4, axis=0), spread_t)
        mix[i] = jnp.where(take_t, w4, 0.0).astype(BF16)

    r, col = iota((128, 128), 0), iota((128, 128), 1)
    source_row = (lax.rem(r, 32) // 4) * 16 + (r // 32) * 4 + lax.rem(r, 4)
    sort = jnp.where(col == source_row, 1.0, 0.0).astype(BF16)
    c_row = (lax.rem(r, 16) // 4) * 32 + (r // 16) * 4 + lax.rem(r, 4)
    unsort = jnp.where(col == c_row, 1.0, 0.0).astype(BF16)

    for c in w_copies:
        c.wait()

    def one_round(rnd, carry):
        block = pl.ds(pl.multiple_of(rnd * 512, 512), 512)
        wait_bytes(inbox.at[block], recv1.at[rnd])
        for i in range(4):
            x = dot(sort, inbox[pl.ds(pl.multiple_of(rnd * 512 + i * 128, 128), 128), :]).astype(BF16)
            for c in range(4):
                x_buf[i * 32:(i + 1) * 32, c * 512:(c + 1) * 512] = x[c * 32:(c + 1) * 32]
        gate = dot(x_buf[...], wg[...])
        up = dot(x_buf[...], wu[...])
        hidden = (gate / (1.0 + jnp.exp(-gate)) * up).astype(BF16)
        y_buf[...] = dot(hidden, wd[...]).astype(BF16)
        for i in range(4):
            y = jnp.concatenate(
                [y_buf[i * 32:(i + 1) * 32, c * 512:(c + 1) * 512] for c in range(4)], axis=0
            )
            ybox[pl.ds(pl.multiple_of(rnd * 512 + i * 128, 128), 128), :] = dot(unsort, y).astype(BF16)

        def send_back(k, carry):
            p = rnd * 32 + k
            sh, sq = lax.rem(head - p // 8 + 16, 16), lax.rem(p, 8)
            remote = sh * 8 + sq != me

            @pl.when(remote)
            def _():
                pltpu.make_async_remote_copy(
                    src_ref=ybox.at[rows16(p)], dst_ref=backbox.at[rows16(me)],
                    send_sem=send2, recv_sem=recv2,
                    device_id=(sh, sq), device_id_type=MESH,
                ).start()

            @pl.when(jnp.logical_not(remote))
            def _():
                pltpu.make_async_copy(ybox.at[rows16(p)], backbox.at[rows16(me)], recv2).start()

            return carry

        lax.fori_loop(0, 32, send_back, 0)
        return carry

    lax.fori_loop(0, 4, one_round, 0)

    wait_bytes(backbox, recv2)
    total = dot(mix[0], backbox[...]) + dot(mix[1], backbox[...])
    for c in range(4):
        f = slice(c * 512, (c + 1) * 512)
        out_ref[:, f] = (hid_ref[:, f] + total[c * 32:(c + 1) * 32]).astype(BF16)
    wait_bytes(outbox.at[pl.ds(0, 127 * 16)], send1)
    wait_bytes(ybox.at[pl.ds(0, 127 * 16)], send2)


def per_device(
    residual, queries, key_cache, value_cache, visible_len, out_weight, norm_gain,
    expert_ids, route_weights, w_gate, w_up, w_down,
):
    vmem, hbm = pl.BlockSpec(memory_space=pltpu.VMEM), pl.BlockSpec(memory_space=pl.ANY)
    dma, scratch = pltpu.SemaphoreType.DMA, pltpu.VMEM
    params = pltpu.CompilerParams(has_side_effects=True, vmem_limit_bytes=VMEM_LIMIT)
    hidden, normed = pl.pallas_call(
        attention_kernel,
        out_shape=(
            jax.ShapeDtypeStruct((32, D), F32),
            jax.ShapeDtypeStruct((32, D), BF16),
        ),
        in_specs=[vmem, hbm, hbm, vmem, vmem, vmem, hbm],
        out_specs=(vmem, vmem),
        scratch_shapes=[
            scratch((8, 2, 256, HD), BF16),
            scratch((256, D), BF16),
            scratch((HD, 512), BF16),
            scratch((1, 1024), F32),
            scratch((1, 1024), F32),
            scratch((HD, 1024), F32),
            scratch((512, 256), BF16),
            scratch((2, 4, 128, HALF), BF16),
            scratch((2, 4, 128, HALF), BF16),
            scratch((2, 4, 32, HALF), BF16),
            scratch((2, 4, 32, HALF), BF16),
            dma, dma, dma, dma((8,)), dma, dma((2, 4)), dma, dma((2, 4)),
        ],
        compiler_params=params,
        name="attention",
    )(
        queries, key_cache, value_cache, visible_len.reshape(1, -1), residual,
        norm_gain.reshape(1, -1), out_weight,
    )
    return pl.pallas_call(
        expert_kernel,
        out_shape=jax.ShapeDtypeStruct((32, D), BF16),
        in_specs=[vmem, vmem, vmem, vmem, hbm, hbm, hbm],
        out_specs=vmem,
        scratch_shapes=[
            scratch((D, FF), BF16),
            scratch((D, FF), BF16),
            scratch((FF, D), BF16),
            scratch((2048, 512), BF16),
            scratch((2048, 512), BF16),
            scratch((2048, 512), BF16),
            scratch((2048, 512), BF16),
            scratch((2, 128, 2048), BF16),
            scratch((128, D), BF16),
            scratch((128, D), BF16),
            dma((3,)), dma, dma((4,)), dma, dma,
        ],
        compiler_params=params,
        name="experts",
    )(expert_ids, route_weights, hidden, normed, w_gate, w_up, w_down)


def solution(mesh):
    in_specs = (
        P(("qblk", "head"), None),
        P("qblk", "head"),
        P(None, "qblk", None),
        P(None, "qblk", None),
        P("qblk"),
        P("head", None),
        P(),
        P(("qblk", "head"), None),
        P(("qblk", "head"), None),
        P(("head", "qblk"), None, None),
        P(("head", "qblk"), None, None),
        P(("head", "qblk"), None, None),
    )
    return jax.shard_map(
        per_device, mesh=mesh, in_specs=in_specs, out_specs=P(("qblk", "head"), None),
        check_vma=False,
    )
```

```python
import jax
import jax.numpy as jnp
from jax import lax
from jax.experimental import pallas as pl
from jax.experimental.pallas import tpu as pltpu
from jax.sharding import PartitionSpec as P

MESH = pl.DeviceIdType.MESH
F32, BF16 = jnp.float32, jnp.bfloat16
D = 2048
HD = 128
FF = 768
HALF = D // 2
NEG = -1e30
STRIDE = 37
QSCALE = HD ** (-0.5) * 1.4426950408889634
VMEM_LIMIT = 58 * 1024 * 1024


def dot(a, b):
    return jnp.dot(a, b, preferred_element_type=F32)


def dot_nt(a, b):
    return lax.dot_general(a, b, (((1,), (1,)), ((), ())), preferred_element_type=F32)


def dot_tn(a, b):
    return lax.dot_general(a, b, (((0,), (0,)), ((), ())), preferred_element_type=F32)


def wait_bytes(ref, sem):
    pltpu.make_async_copy(ref, ref, sem).wait()


def iota(shape, axis):
    return lax.broadcasted_iota(jnp.int32, shape, axis)


def rows16(i):
    return pl.ds(pl.multiple_of(i * 16, 16), 16)


def route(ids_ref, rw_ref, pick, mix):
    expert = iota((128, 32), 0)
    named = jnp.zeros((128, 32), F32)
    weight = jnp.zeros((128, 32), F32)
    for k in range(8):
        hit = ids_ref[k:k + 1, :] == expert
        named = jnp.where(hit, 1.0, named)
        weight = jnp.where(hit, rw_ref[k:k + 1, :], weight)
    later = jnp.where(iota((32, 32), 0) < iota((32, 32), 1), 1.0, 0.0).astype(BF16)
    rank = jnp.where(named > 0.0, dot(named.astype(BF16), later), -1.0)
    four = jnp.where(iota((32, 128), 0) == lax.rem(iota((32, 128), 1), 32), 1.0, 0.0).astype(BF16)
    rank4 = dot(rank.astype(BF16), four)
    high = weight.astype(BF16)
    low = (weight - high.astype(F32)).astype(BF16)

    spread = jnp.where(iota((2048, 128), 0) // 16 == iota((2048, 128), 1), 1.0, 0.0).astype(BF16)
    at = dot(spread, rank4.astype(BF16))
    j = iota((2048, 128), 0)
    take = (at == lax.rem(j, 4).astype(F32)) & (lax.rem(j // 4, 4) == iota((2048, 128), 1) // 32)
    pick[...] = jnp.where(take, 1.0, 0.0).astype(BF16)

    spread_t = jnp.where(iota((128, 2048), 1) // 16 == iota((128, 2048), 0), 1.0, 0.0).astype(BF16)
    at_t = dot(rank4.T.astype(BF16), spread_t)
    jt = iota((128, 2048), 1)
    take_t = (at_t == lax.rem(jt, 4).astype(F32)) & (lax.rem(jt // 4, 4) == iota((128, 2048), 0) // 32)
    for i, w in enumerate((high, low)):
        w4 = dot(dot(w, four).T.astype(BF16), spread_t)
        mix[i] = jnp.where(take_t, w4, 0.0).astype(BF16)


def layer_kernel(
    q_ref, key_ref, value_ref, vis_ref, res_ref, gain_ref, ids_ref, rw_ref, w_ref, wg_ref, wu_ref, wd_ref,
    out_ref,
    kv, w_buf, vt, top, den, acc, att, part, got, mid, got2,
    own_sem, w_sem, kv_send, kv_recv, send1, recv1, send2, recv2,
    wg, wu, wd, hid, x4, pick, outbox, inbox, ybox, backbox, mix, x_buf, y_buf,
    e_sem, send3, recv3, send4, recv4, plane_sem, all_sem,
):
    head, qblk = lax.axis_index("head"), lax.axis_index("qblk")
    yy, zz = head // 4, lax.rem(head, 4)
    xx, core = qblk // 2, lax.rem(qblk, 2)
    sibling = 2 * xx + 1 - core
    me = head * 8 + qblk

    def remote(src, dst, ssem, rsem, h, q):
        c = pltpu.make_async_remote_copy(
            src_ref=src, dst_ref=dst, send_sem=ssem, recv_sem=rsem,
            device_id=(h, q), device_id_type=MESH,
        )
        c.start()

    def signal(sem, h, q):
        pl.semaphore_signal(sem, inc=1, device_id=(h, q), device_id_type=MESH)

    y_line = [(lax.rem(yy + d, 4) * 4 + zz, qblk) for d in (1, 3, 2)]
    z_line = [(yy * 4 + lax.rem(zz + d, 4), qblk) for d in (1, 3, 2)]
    x_line = [(head, lax.rem(qblk + d, 8)) for d in range(1, 8)]

    barrier = pltpu.get_barrier_semaphore()
    for h, q in x_line + y_line + z_line:
        signal(barrier, h, q)
    pl.semaphore_wait(barrier, 13)

    for j, src in enumerate((key_ref, value_ref)):
        remote(src.at[yy], kv.at[qblk, j], kv_send, kv_recv.at[qblk], head, sibling)
        for dx in (1, 3, 2):
            peer = 2 * lax.rem(xx + dx, 4) + core
            remote(src.at[yy], kv.at[qblk, j], kv_send, kv_recv.at[qblk], head, peer)
    for j, src in enumerate((key_ref, value_ref)):
        pltpu.make_async_copy(src.at[yy], kv.at[qblk, j], own_sem).start()
    for h, q in y_line:
        signal(plane_sem, h, q)
    w_copy = pltpu.make_async_copy(w_ref, w_buf, w_sem)
    w_copy.start()
    w_copies = [
        pltpu.make_async_copy(src.at[0], dst, e_sem.at[i])
        for i, (src, dst) in enumerate(((wg_ref, wg), (wu_ref, wu), (wd_ref, wd)))
    ]
    for c in w_copies:
        c.start()
    route(ids_ref, rw_ref, pick, mix)
    pl.semaphore_wait(plane_sem, 3)
    for h, q in z_line:
        signal(all_sem, h, q)
    wait_bytes(kv.at[qblk], own_sem)

    top[...] = jnp.full(top.shape, NEG, F32)
    den[...] = jnp.zeros(den.shape, F32)
    acc[...] = jnp.zeros(acc.shape, F32)

    for dx in (0, 1, 3, 2):
        chip = lax.rem(xx + dx, 4)
        if dx:
            mine = 2 * chip + core
            wait_bytes(kv.at[mine], kv_recv.at[mine])
            remote(kv.at[mine], kv.at[mine], kv_send, kv_recv.at[mine], head, sibling)
        other = 2 * chip + 1 - core
        wait_bytes(kv.at[other], kv_recv.at[other])
        keys = kv[pl.ds(2 * chip, 2), 0].reshape(512, HD)
        vt[...] = kv[pl.ds(2 * chip, 2), 1].reshape(512, HD).astype(F32).T.astype(BF16)
        base = chip * 512

        def rows(i, carry, keys=keys, base=base):
            h, t0 = i // 2, pl.multiple_of(lax.rem(i, 2) * 256, 256)
            q = q_ref[pl.ds(t0, 256), pl.ds(pl.multiple_of(h * HD, HD), HD)]
            cols = pl.ds(pl.multiple_of(i * 256, 256), 256)
            s = dot_nt(keys, q)
            seen = vis_ref[:, pl.ds(t0, 256)] - base
            s = jnp.where(lax.broadcasted_iota(jnp.int32, s.shape, 0) < seen, s, NEG)
            old = top[:, cols]
            new = jnp.maximum(old, jnp.max(s, axis=0, keepdims=True))
            p = jnp.exp2((s - new) * QSCALE)
            scale = jnp.exp2((old - new) * QSCALE)
            top[:, cols] = new
            den[:, cols] = den[:, cols] * scale + jnp.sum(p, axis=0, keepdims=True)
            acc[:, cols] = acc[:, cols] * scale + dot(vt[...], p.astype(BF16))
            return carry

        lax.fori_loop(0, 4, rows, 0)

    for h in range(2):
        cols = slice(h * 512, (h + 1) * 512)
        att[:, h * HD:(h + 1) * HD] = (acc[:, cols] / den[:, cols]).T.astype(BF16)

    w_copy.wait()
    for d in (2, 1, 3, 0):
        z2, y2 = lax.rem(zz + d, 4), lax.rem(yy + d, 4)
        a0 = jnp.concatenate(
            [att[pl.ds(pl.multiple_of((i * 4 + z2) * 32, 32), 32), :] for i in range(4)], axis=0
        )
        part[0, z2] = dot(a0, w_buf[:, :HALF]).astype(BF16)
        if d:
            remote(part.at[0, z2], got.at[0, zz], send1, recv1.at[0, zz], yy * 4 + z2, qblk)
        a1 = att[pl.ds(pl.multiple_of(y2 * 128, 128), 128), :]
        part[1, y2] = dot(a1, w_buf[:, HALF:]).astype(BF16)
        if d:
            remote(part.at[1, y2], got.at[1, yy], send1, recv1.at[1, yy], y2 * 4 + zz, qblk)

    sum0 = part[0, zz].astype(F32)
    sum1 = part[1, yy].astype(F32)
    for d in (1, 3, 2):
        z2, y2 = lax.rem(zz + d, 4), lax.rem(yy + d, 4)
        wait_bytes(got.at[0, z2], recv1.at[0, z2])
        sum0 += got[0, z2].astype(F32)
        wait_bytes(got.at[1, y2], recv1.at[1, y2])
        sum1 += got[1, y2].astype(F32)
    mid[0] = sum0.reshape(4, 32, HALF).astype(BF16)
    mid[1] = sum1.reshape(4, 32, HALF).astype(BF16)
    for d in (2, 1, 3):
        z2, y2 = lax.rem(zz + d, 4), lax.rem(yy + d, 4)
        remote(mid.at[0, y2], got2.at[0, yy], send2, recv2.at[0, yy], y2 * 4 + zz, qblk)
        remote(mid.at[1, z2], got2.at[1, zz], send2, recv2.at[1, zz], yy * 4 + z2, qblk)
    h0 = res_ref[:, :HALF].astype(F32) + mid[0, yy].astype(F32)
    h1 = res_ref[:, HALF:].astype(F32) + mid[1, zz].astype(F32)
    for d in (1, 3, 2):
        z2, y2 = lax.rem(zz + d, 4), lax.rem(yy + d, 4)
        wait_bytes(got2.at[0, y2], recv2.at[0, y2])
        h0 += got2[0, y2].astype(F32)
        wait_bytes(got2.at[1, z2], recv2.at[1, z2])
        h1 += got2[1, z2].astype(F32)
    square = jnp.sum(h0 * h0, axis=1, keepdims=True) + jnp.sum(h1 * h1, axis=1, keepdims=True)
    rs = lax.rsqrt(square * (1.0 / D) + 1e-6)
    hid[:, :HALF] = h0
    hid[:, HALF:] = h1
    n0 = (h0 * rs * gain_ref[:, :HALF]).astype(BF16)
    n1 = (h1 * rs * gain_ref[:, HALF:]).astype(BF16)
    for c, n in enumerate((n0, n1)):
        for half in range(2):
            x4[(2 * c + half) * 32:(2 * c + half + 1) * 32, :] = n[:, half * 512:(half + 1) * 512]
    pl.semaphore_wait(all_sem, 3)

    outbox[...] = dot(pick[...], x4[...]).astype(BF16)


    def partner(k, sign):
        d = lax.rem(k * STRIDE, 128)
        py = lax.rem(head // 4 + sign * (d // 32) + 4, 4)
        pz = lax.rem(lax.rem(head, 4) + sign * lax.rem(d // 8, 4) + 4, 4)
        px = lax.rem(qblk // 2 + sign * lax.rem(d // 2, 4) + 4, 4)
        return py * 4 + pz, px * 2 + lax.rem(lax.rem(qblk, 2) + lax.rem(d, 2), 2)

    def dispatch(k, carry):
        eh, eq = partner(k, 1)
        pltpu.make_async_remote_copy(
            src_ref=outbox.at[rows16(eh * 8 + eq)], dst_ref=inbox.at[rows16(k)],
            send_sem=send3, recv_sem=recv3.at[k // 32],
            device_id=(eh, eq), device_id_type=MESH,
        ).start()
        return carry

    lax.fori_loop(1, 128, dispatch, 0)
    pltpu.make_async_copy(outbox.at[rows16(me)], inbox.at[rows16(0)], recv3.at[0]).start()

    r, col = iota((128, 128), 0), iota((128, 128), 1)
    source_row = (lax.rem(r, 32) // 4) * 16 + (r // 32) * 4 + lax.rem(r, 4)
    sort = jnp.where(col == source_row, 1.0, 0.0).astype(BF16)
    c_row = (lax.rem(r, 16) // 4) * 32 + (r // 16) * 4 + lax.rem(r, 4)
    unsort = jnp.where(col == c_row, 1.0, 0.0).astype(BF16)

    for c in w_copies:
        c.wait()

    def one_round(rnd, carry):
        block = pl.ds(pl.multiple_of(rnd * 512, 512), 512)
        wait_bytes(inbox.at[block], recv3.at[rnd])
        for i in range(4):
            x = dot(sort, inbox[pl.ds(pl.multiple_of(rnd * 512 + i * 128, 128), 128), :]).astype(BF16)
            for c in range(4):
                x_buf[i * 32:(i + 1) * 32, c * 512:(c + 1) * 512] = x[c * 32:(c + 1) * 32]
        gate = dot(x_buf[...], wg[...])
        up = dot(x_buf[...], wu[...])
        hidden = (gate / (1.0 + jnp.exp(-gate)) * up).astype(BF16)
        y_buf[...] = dot(hidden, wd[...]).astype(BF16)
        for i in range(4):
            y = jnp.concatenate(
                [y_buf[i * 32:(i + 1) * 32, c * 512:(c + 1) * 512] for c in range(4)], axis=0
            )
            ybox[pl.ds(pl.multiple_of(rnd * 512 + i * 128, 128), 128), :] = dot(unsort, y).astype(BF16)

        def send_back(k, carry):
            p = rnd * 32 + k
            sh, sq = partner(p, -1)
            remote = p != 0

            @pl.when(remote)
            def _():
                pltpu.make_async_remote_copy(
                    src_ref=ybox.at[rows16(p)], dst_ref=backbox.at[rows16(me)],
                    send_sem=send4, recv_sem=recv4,
                    device_id=(sh, sq), device_id_type=MESH,
                ).start()

            @pl.when(jnp.logical_not(remote))
            def _():
                pltpu.make_async_copy(ybox.at[rows16(p)], backbox.at[rows16(me)], recv4).start()

            return carry

        lax.fori_loop(0, 32, send_back, 0)
        return carry

    lax.fori_loop(0, 4, one_round, 0)

    wait_bytes(backbox, recv4)
    total = dot(mix[0], backbox[...]) + dot(mix[1], backbox[...])
    for c in range(4):
        f = slice(c * 512, (c + 1) * 512)
        out_ref[:, f] = (hid[:, f] + total[c * 32:(c + 1) * 32]).astype(BF16)
    wait_bytes(kv.at[pl.ds(0, 7)], kv_send)
    wait_bytes(part.at[:, pl.ds(0, 3)], send1)
    wait_bytes(mid.at[:, pl.ds(0, 3)], send2)
    wait_bytes(outbox.at[pl.ds(0, 127 * 16)], send3)
    wait_bytes(ybox.at[pl.ds(0, 127 * 16)], send4)


def per_device(
    residual, queries, key_cache, value_cache, visible_len, out_weight, norm_gain,
    expert_ids, route_weights, w_gate, w_up, w_down,
):
    vmem, hbm = pl.BlockSpec(memory_space=pltpu.VMEM), pl.BlockSpec(memory_space=pl.ANY)
    dma, scratch = pltpu.SemaphoreType.DMA, pltpu.VMEM
    return pl.pallas_call(
        layer_kernel,
        out_shape=jax.ShapeDtypeStruct((32, D), BF16),
        in_specs=[vmem, hbm, hbm, vmem, vmem, vmem, vmem, vmem, hbm, hbm, hbm, hbm],
        out_specs=vmem,
        scratch_shapes=[
            scratch((8, 2, 256, HD), BF16),
            scratch((256, D), BF16),
            scratch((HD, 512), BF16),
            scratch((1, 1024), F32),
            scratch((1, 1024), F32),
            scratch((HD, 1024), F32),
            scratch((512, 256), BF16),
            scratch((2, 4, 128, HALF), BF16),
            scratch((2, 4, 128, HALF), BF16),
            scratch((2, 4, 32, HALF), BF16),
            scratch((2, 4, 32, HALF), BF16),
            dma, dma, dma, dma((8,)), dma, dma((2, 4)), dma, dma((2, 4)),
            scratch((D, FF), BF16),
            scratch((D, FF), BF16),
            scratch((FF, D), BF16),
            scratch((32, D), F32),
            scratch((128, 512), BF16),
            scratch((2048, 128), BF16),
            scratch((2048, 512), BF16),
            scratch((2048, 512), BF16),
            scratch((2048, 512), BF16),
            scratch((2048, 512), BF16),
            scratch((2, 128, 2048), BF16),
            scratch((128, D), BF16),
            scratch((128, D), BF16),
            dma((3,)), dma, dma((4,)), dma, dma,
            pltpu.SemaphoreType.REGULAR, pltpu.SemaphoreType.REGULAR,
        ],
        compiler_params=pltpu.CompilerParams(
            collective_id=0, has_side_effects=True, vmem_limit_bytes=VMEM_LIMIT
        ),
        name="layer",
    )(
        queries, key_cache, value_cache, visible_len.reshape(1, -1), residual,
        norm_gain.reshape(1, -1), expert_ids.T, route_weights.T, out_weight, w_gate, w_up, w_down,
    )


def solution(mesh):
    in_specs = (
        P(("qblk", "head"), None),
        P("qblk", "head"),
        P(None, "qblk", None),
        P(None, "qblk", None),
        P("qblk"),
        P("head", None),
        P(),
        P(("qblk", "head"), None),
        P(("qblk", "head"), None),
        P(("head", "qblk"), None, None),
        P(("head", "qblk"), None, None),
        P(("head", "qblk"), None, None),
    )
    return jax.shard_map(
        per_device, mesh=mesh, in_specs=in_specs, out_specs=P(("qblk", "head"), None),
        check_vma=False,
    )
```

```python
import jax
import jax.numpy as jnp
from jax import lax
from jax.experimental import pallas as pl
from jax.experimental.pallas import tpu as pltpu
from jax.sharding import PartitionSpec as P

MESH = pl.DeviceIdType.MESH
F32, BF16 = jnp.float32, jnp.bfloat16
D = 2048
HD = 128
FF = 768
NEG = -1e30
STRIDE = 37
QSCALE = HD ** (-0.5) * 1.4426950408889634
VMEM_LIMIT = 58 * 1024 * 1024


def dot(a, b):
    return jnp.dot(a, b, preferred_element_type=F32)


def dot_nt(a, b):
    return lax.dot_general(a, b, (((1,), (1,)), ((), ())), preferred_element_type=F32)


def dot_tn(a, b):
    return lax.dot_general(a, b, (((0,), (0,)), ((), ())), preferred_element_type=F32)


def wait_bytes(ref, sem):
    pltpu.make_async_copy(ref, ref, sem).wait()


def iota(shape, axis):
    return lax.broadcasted_iota(jnp.int32, shape, axis)


def rows16(i):
    return pl.ds(pl.multiple_of(i * 16, 16), 16)


def route(ids_ref, rw_ref, pick, mix):
    expert = iota((128, 32), 0)
    named = jnp.zeros((128, 32), F32)
    weight = jnp.zeros((128, 32), F32)
    for k in range(8):
        hit = ids_ref[k:k + 1, :] == expert
        named = jnp.where(hit, 1.0, named)
        weight = jnp.where(hit, rw_ref[k:k + 1, :], weight)
    later = jnp.where(iota((32, 32), 0) < iota((32, 32), 1), 1.0, 0.0).astype(BF16)
    rank = jnp.where(named > 0.0, dot(named.astype(BF16), later), -1.0)
    four = jnp.where(iota((32, 128), 0) == lax.rem(iota((32, 128), 1), 32), 1.0, 0.0).astype(BF16)
    rank4 = dot(rank.astype(BF16), four)
    high = weight.astype(BF16)
    low = (weight - high.astype(F32)).astype(BF16)

    spread = jnp.where(iota((2048, 128), 0) // 16 == iota((2048, 128), 1), 1.0, 0.0).astype(BF16)
    at = dot(spread, rank4.astype(BF16))
    j = iota((2048, 128), 0)
    take = (at == lax.rem(j, 4).astype(F32)) & (lax.rem(j // 4, 4) == iota((2048, 128), 1) // 32)
    pick[...] = jnp.where(take, 1.0, 0.0).astype(BF16)

    spread_t = jnp.where(iota((128, 2048), 1) // 16 == iota((128, 2048), 0), 1.0, 0.0).astype(BF16)
    at_t = dot(rank4.T.astype(BF16), spread_t)
    jt = iota((128, 2048), 1)
    take_t = (at_t == lax.rem(jt, 4).astype(F32)) & (lax.rem(jt // 4, 4) == iota((128, 2048), 0) // 32)
    for i, w in enumerate((high, low)):
        w4 = dot(dot(w, four).T.astype(BF16), spread_t)
        mix[i] = jnp.where(take_t, w4, 0.0).astype(BF16)


def layer_kernel(
    q_ref, key_ref, value_ref, vis_ref, res_ref, gain_ref, ids_ref, rw_ref, w_ref, wg_ref, wu_ref, wd_ref,
    out_ref,
    kv, q_buf, w_buf, vt, top, den, acc, att, part, got,
    own_sem, w_sem, kv_send, kv_recv, q_send, q_recv, w_send, wz_recv, wx_recv, wf_recv, ws_recv, send1, recv1,
    wg, wu, wd, hid, x4, pick, outbox, inbox, ybox, backbox, mix, x_buf, y_buf,
    e_sem, send3, recv3, send4, recv4, plane_sem, all_sem,
):
    head, qblk = lax.axis_index("head"), lax.axis_index("qblk")
    yy, zz = head // 4, lax.rem(head, 4)
    xx, core = qblk // 2, lax.rem(qblk, 2)
    sibling = 2 * xx + 1 - core
    me = head * 8 + qblk

    def remote(src, dst, ssem, rsem, h, q):
        c = pltpu.make_async_remote_copy(
            src_ref=src, dst_ref=dst, send_sem=ssem, recv_sem=rsem,
            device_id=(h, q), device_id_type=MESH,
        )
        c.start()

    def signal(sem, h, q):
        pl.semaphore_signal(sem, inc=1, device_id=(h, q), device_id_type=MESH)

    y_line = [(lax.rem(yy + d, 4) * 4 + zz, qblk) for d in (1, 3, 2)]
    z_line = [(yy * 4 + lax.rem(zz + d, 4), qblk) for d in (1, 3, 2)]
    x_line = [(head, lax.rem(qblk + d, 8)) for d in range(1, 8)]

    barrier = pltpu.get_barrier_semaphore()
    for h, q in x_line + y_line + z_line:
        signal(barrier, h, q)
    pl.semaphore_wait(barrier, 13)

    for d in (1, 3, 2):
        z2 = lax.rem(zz + d, 4)
        remote(q_ref.at[:, z2], q_buf.at[zz], q_send, q_recv.at[zz], yy * 4 + z2, qblk)
    for j, src in enumerate((key_ref, value_ref)):
        remote(src.at[yy], kv.at[qblk, j], kv_send, kv_recv.at[qblk], head, sibling)
        for dx in (1, 3, 2):
            peer = 2 * lax.rem(xx + dx, 4) + core
            remote(src.at[yy], kv.at[qblk, j], kv_send, kv_recv.at[qblk], head, peer)
    def w_rows(z, first, count):
        return pl.ds(pl.multiple_of(z * 256 + first, 16), count)

    mine16 = 128 + core * 64 + xx * 16
    for d in (1, 3, 2):
        z2 = lax.rem(zz + d, 4)
        remote(w_ref.at[w_rows(0, mine16, 16)], w_buf.at[w_rows(zz, mine16, 16)],
               w_send, wx_recv.at[zz], yy * 4 + z2, qblk)
    for d in (1, 3, 2):
        z2 = lax.rem(zz + d, 4)
        remote(w_ref.at[w_rows(0, core * 64, 64)], w_buf.at[w_rows(zz, core * 64, 64)],
               w_send, wz_recv.at[zz], yy * 4 + z2, qblk)
    for j, src in enumerate((key_ref, value_ref)):
        pltpu.make_async_copy(src.at[yy], kv.at[qblk, j], own_sem).start()
    pltpu.make_async_copy(q_ref.at[:, zz], q_buf.at[zz], q_recv.at[zz]).start()
    for h, q in y_line:
        signal(plane_sem, h, q)
    w_copy = pltpu.make_async_copy(w_ref, w_buf.at[w_rows(zz, 0, 256)], w_sem)
    w_copy.start()
    w_copies = [
        pltpu.make_async_copy(src.at[0], dst, e_sem.at[i])
        for i, (src, dst) in enumerate(((wg_ref, wg), (wu_ref, wu), (wd_ref, wd)))
    ]
    for c in w_copies:
        c.start()
    route(ids_ref, rw_ref, pick, mix)
    pl.semaphore_wait(plane_sem, 3)
    for h, q in z_line:
        signal(all_sem, h, q)
    lane = iota((8, 128), 1)
    seen_all = jnp.zeros((8, 128), jnp.int32)
    for i in range(4):
        block = jnp.broadcast_to(vis_ref[:, i * 128:(i + 1) * 128], (8, 128))
        block = pltpu.roll(block, lax.rem((i - zz) * 32 + 128, 128), 1)
        seen_all = jnp.where(lane // 32 == i, block, seen_all)
    seen_all = jnp.concatenate([seen_all, seen_all], axis=1)[:1]

    wait_bytes(kv.at[qblk], own_sem)
    for d in range(4):
        z2 = lax.rem(zz + d, 4)
        wait_bytes(q_buf.at[z2], q_recv.at[z2])

    top[...] = jnp.full(top.shape, NEG, F32)
    den[...] = jnp.zeros(den.shape, F32)
    acc[...] = jnp.zeros(acc.shape, F32)

    for dx in (0, 1, 3, 2):
        chip = lax.rem(xx + dx, 4)
        if dx:
            mine = 2 * chip + core
            wait_bytes(kv.at[mine], kv_recv.at[mine])
            remote(kv.at[mine], kv.at[mine], kv_send, kv_recv.at[mine], head, sibling)
        other = 2 * chip + 1 - core
        wait_bytes(kv.at[other], kv_recv.at[other])
        keys = kv[pl.ds(2 * chip, 2), 0].reshape(512, HD)
        vt[...] = kv[pl.ds(2 * chip, 2), 1].reshape(512, HD).astype(F32).T.astype(BF16)
        base = chip * 512

        def rows(i, carry, keys=keys, base=base):
            q = q_buf[i].reshape(128, 2 * HD)
            q = jnp.concatenate([q[:, :HD], q[:, HD:]], axis=0)
            cols = pl.ds(pl.multiple_of(i * 256, 256), 256)
            s = dot_nt(keys, q)
            s = jnp.where(iota(s.shape, 0) < seen_all - base, s, NEG)
            old = top[:, cols]
            new = jnp.maximum(old, jnp.max(s, axis=0, keepdims=True))
            p = jnp.exp2((s - new) * QSCALE)
            scale = jnp.exp2((old - new) * QSCALE)
            top[:, cols] = new
            den[:, cols] = den[:, cols] * scale + jnp.sum(p, axis=0, keepdims=True)
            acc[:, cols] = acc[:, cols] * scale + dot(vt[...], p.astype(BF16))
            return carry

        lax.fori_loop(0, 4, rows, 0)

        if dx == 0:
            for d in (1, 3, 2):
                z2 = lax.rem(zz + d, 4)
                wait_bytes(w_buf.at[w_rows(z2, mine16, 16)], wx_recv.at[z2])
                for ex in (1, 3, 2):
                    peer = 2 * lax.rem(xx + ex, 4) + core
                    remote(w_buf.at[w_rows(z2, mine16, 16)], w_buf.at[w_rows(z2, mine16, 16)],
                           w_send, wf_recv.at[z2], head, peer)

    for n in range(8):
        cols = slice(n * HD, (n + 1) * HD)
        att[:, cols] = (acc[:, cols] / den[:, cols]).T.astype(BF16)

    for d in (1, 3, 2):
        z2 = lax.rem(zz + d, 4)
        wait_bytes(w_buf.at[w_rows(z2, 0, 48)], wf_recv.at[z2])
        here = w_rows(z2, 128 + core * 64, 64)
        remote(w_buf.at[here], w_buf.at[here], w_send, ws_recv.at[z2, 1], head, sibling)
    for d in (1, 3, 2):
        z2 = lax.rem(zz + d, 4)
        here = w_rows(z2, core * 64, 64)
        wait_bytes(w_buf.at[here], wz_recv.at[z2])
        remote(w_buf.at[here], w_buf.at[here], w_send, ws_recv.at[z2, 0], head, sibling)
    for d in (1, 3, 2):
        z2 = lax.rem(zz + d, 4)
        for i in range(2):
            wait_bytes(w_buf.at[w_rows(z2, i * 128 + (1 - core) * 64, 64)], ws_recv.at[z2, i])
    w_copy.wait()

    for n in range(4):
        part[n] = dot(att[...], w_buf[:, n * 512:(n + 1) * 512]).reshape(4, 32, 512).astype(BF16)
        for d in (2, 1, 3):
            y2 = lax.rem(yy + d, 4)
            remote(part.at[n, y2], got.at[n, yy], send1, recv1.at[yy], y2 * 4 + zz, qblk)

    h = [
        res_ref[:, n * 512:(n + 1) * 512].astype(F32) + part[n, yy].astype(F32) for n in range(4)
    ]
    for d in (1, 3, 2):
        y2 = lax.rem(yy + d, 4)
        wait_bytes(got.at[:, y2], recv1.at[y2])
        h = [h[n] + got[n, y2].astype(F32) for n in range(4)]
    square = sum(jnp.sum(v * v, axis=1, keepdims=True) for v in h)
    rs = lax.rsqrt(square * (1.0 / D) + 1e-6)
    for n in range(4):
        f = slice(n * 512, (n + 1) * 512)
        hid[:, f] = h[n]
        x4[n * 32:(n + 1) * 32, :] = (h[n] * rs * gain_ref[:, f]).astype(BF16)
    pl.semaphore_wait(all_sem, 3)

    outbox[...] = dot(pick[...], x4[...]).astype(BF16)


    def partner(k, sign):
        d = lax.rem(k * STRIDE, 128)
        py = lax.rem(head // 4 + sign * (d // 32) + 4, 4)
        pz = lax.rem(lax.rem(head, 4) + sign * lax.rem(d // 8, 4) + 4, 4)
        px = lax.rem(qblk // 2 + sign * lax.rem(d // 2, 4) + 4, 4)
        return py * 4 + pz, px * 2 + lax.rem(lax.rem(qblk, 2) + lax.rem(d, 2), 2)

    def dispatch(k, carry):
        eh, eq = partner(k, 1)
        pltpu.make_async_remote_copy(
            src_ref=outbox.at[rows16(eh * 8 + eq)], dst_ref=inbox.at[rows16(k)],
            send_sem=send3, recv_sem=recv3.at[k // 32],
            device_id=(eh, eq), device_id_type=MESH,
        ).start()
        return carry

    lax.fori_loop(1, 128, dispatch, 0)
    pltpu.make_async_copy(outbox.at[rows16(me)], inbox.at[rows16(0)], recv3.at[0]).start()

    r, col = iota((128, 128), 0), iota((128, 128), 1)
    source_row = (lax.rem(r, 32) // 4) * 16 + (r // 32) * 4 + lax.rem(r, 4)
    sort = jnp.where(col == source_row, 1.0, 0.0).astype(BF16)
    c_row = (lax.rem(r, 16) // 4) * 32 + (r // 16) * 4 + lax.rem(r, 4)
    unsort = jnp.where(col == c_row, 1.0, 0.0).astype(BF16)

    for c in w_copies:
        c.wait()

    def one_round(rnd, carry):
        block = pl.ds(pl.multiple_of(rnd * 512, 512), 512)
        wait_bytes(inbox.at[block], recv3.at[rnd])
        for i in range(4):
            x = dot(sort, inbox[pl.ds(pl.multiple_of(rnd * 512 + i * 128, 128), 128), :]).astype(BF16)
            for c in range(4):
                x_buf[i * 32:(i + 1) * 32, c * 512:(c + 1) * 512] = x[c * 32:(c + 1) * 32]
        gate = dot(x_buf[...], wg[...])
        up = dot(x_buf[...], wu[...])
        hidden = (gate / (1.0 + jnp.exp(-gate)) * up).astype(BF16)
        y_buf[...] = dot(hidden, wd[...]).astype(BF16)
        for i in range(4):
            y = jnp.concatenate(
                [y_buf[i * 32:(i + 1) * 32, c * 512:(c + 1) * 512] for c in range(4)], axis=0
            )
            ybox[pl.ds(pl.multiple_of(rnd * 512 + i * 128, 128), 128), :] = dot(unsort, y).astype(BF16)

        def send_back(k, carry):
            p = rnd * 32 + k
            sh, sq = partner(p, -1)
            remote = p != 0

            @pl.when(remote)
            def _():
                pltpu.make_async_remote_copy(
                    src_ref=ybox.at[rows16(p)], dst_ref=backbox.at[rows16(me)],
                    send_sem=send4, recv_sem=recv4,
                    device_id=(sh, sq), device_id_type=MESH,
                ).start()

            @pl.when(jnp.logical_not(remote))
            def _():
                pltpu.make_async_copy(ybox.at[rows16(p)], backbox.at[rows16(me)], recv4).start()

            return carry

        lax.fori_loop(0, 32, send_back, 0)
        return carry

    lax.fori_loop(0, 4, one_round, 0)

    wait_bytes(backbox, recv4)
    total = dot(mix[0], backbox[...]) + dot(mix[1], backbox[...])
    for c in range(4):
        f = slice(c * 512, (c + 1) * 512)
        out_ref[:, f] = (hid[:, f] + total[c * 32:(c + 1) * 32]).astype(BF16)
    wait_bytes(kv.at[pl.ds(0, 7)], kv_send)
    wait_bytes(q_buf.at[pl.ds(0, 3)], q_send)
    wait_bytes(w_buf.at[pl.ds(0, 768)], w_send)
    wait_bytes(part.at[:, pl.ds(0, 3)], send1)
    wait_bytes(outbox.at[pl.ds(0, 127 * 16)], send3)
    wait_bytes(ybox.at[pl.ds(0, 127 * 16)], send4)


def per_device(
    residual, queries, key_cache, value_cache, visible_len, out_weight, norm_gain,
    expert_ids, route_weights, w_gate, w_up, w_down,
):
    vmem, hbm = pl.BlockSpec(memory_space=pltpu.VMEM), pl.BlockSpec(memory_space=pl.ANY)
    dma, scratch = pltpu.SemaphoreType.DMA, pltpu.VMEM
    return pl.pallas_call(
        layer_kernel,
        out_shape=jax.ShapeDtypeStruct((32, D), BF16),
        in_specs=[hbm, hbm, hbm, vmem, vmem, vmem, vmem, vmem, hbm, hbm, hbm, hbm],
        out_specs=vmem,
        scratch_shapes=[
            scratch((8, 2, 256, HD), BF16),
            scratch((4, 4, 32, 2 * HD), BF16),
            scratch((1024, D), BF16),
            scratch((HD, 512), BF16),
            scratch((1, 1024), F32),
            scratch((1, 1024), F32),
            scratch((HD, 1024), F32),
            scratch((128, 1024), BF16),
            scratch((4, 4, 32, 512), BF16),
            scratch((4, 4, 32, 512), BF16),
            dma, dma, dma, dma((8,)), dma, dma((4,)), dma, dma((4,)), dma((4,)), dma((4,)), dma((4, 2)), dma, dma((4,)),
            scratch((D, FF), BF16),
            scratch((D, FF), BF16),
            scratch((FF, D), BF16),
            scratch((32, D), F32),
            scratch((128, 512), BF16),
            scratch((2048, 128), BF16),
            scratch((2048, 512), BF16),
            scratch((2048, 512), BF16),
            scratch((2048, 512), BF16),
            scratch((2048, 512), BF16),
            scratch((2, 128, 2048), BF16),
            scratch((128, D), BF16),
            scratch((128, D), BF16),
            dma((3,)), dma, dma((4,)), dma, dma,
            pltpu.SemaphoreType.REGULAR, pltpu.SemaphoreType.REGULAR,
        ],
        compiler_params=pltpu.CompilerParams(
            collective_id=0, has_side_effects=True, vmem_limit_bytes=VMEM_LIMIT
        ),
        name="layer",
    )(
        queries.reshape(4, 4, 32, 2 * HD), key_cache, value_cache, visible_len.reshape(1, -1), residual,
        norm_gain.reshape(1, -1), expert_ids.T, route_weights.T, out_weight, w_gate, w_up, w_down,
    )


def solution(mesh):
    in_specs = (
        P(("qblk", "head"), None),
        P("qblk", "head"),
        P(None, "qblk", None),
        P(None, "qblk", None),
        P("qblk"),
        P("head", None),
        P(),
        P(("qblk", "head"), None),
        P(("qblk", "head"), None),
        P(("head", "qblk"), None, None),
        P(("head", "qblk"), None, None),
        P(("head", "qblk"), None, None),
    )
    return jax.shard_map(
        per_device, mesh=mesh, in_specs=in_specs, out_specs=P(("qblk", "head"), None),
        check_vma=False,
    )
```

```python
import jax
import jax.numpy as jnp
from jax import lax
from jax.experimental import pallas as pl
from jax.experimental.pallas import tpu as pltpu
from jax.sharding import PartitionSpec as P

MESH = pl.DeviceIdType.MESH
F32, BF16 = jnp.float32, jnp.bfloat16
D = 2048
HD = 128
FF = 768
NEG = -1e30
WIDTH = (640, 640, 768)
FEATURES = (slice(0, 640), slice(640, 1280), slice(1280, 2048))
QSCALE = HD ** (-0.5) * 1.4426950408889634
VMEM_LIMIT = 58 * 1024 * 1024


def dot(a, b):
    return jnp.dot(a, b, preferred_element_type=F32)


def dot_nt(a, b):
    return lax.dot_general(a, b, (((1,), (1,)), ((), ())), preferred_element_type=F32)


def dot_tn(a, b):
    return lax.dot_general(a, b, (((0,), (0,)), ((), ())), preferred_element_type=F32)


def wait_bytes(ref, sem):
    pltpu.make_async_copy(ref, ref, sem).wait()


def iota(shape, axis):
    return lax.broadcasted_iota(jnp.int32, shape, axis)


def rows16(i):
    return pl.ds(pl.multiple_of(i * 16, 16), 16)


def offsets(m):
    e = ((m & 15) * 5) & 15
    return e >> 2, e & 3


def partner(axis, head, qblk, m, sign):
    p, q = offsets(m)
    x, y, z = qblk >> 1, head >> 2, head & 3
    if axis == 0:
        y, z = (y + sign * p) & 3, (z + sign * q) & 3
    elif axis == 1:
        x, z = (x + sign * p) & 3, (z + sign * q) & 3
    else:
        x, y = (x + sign * p) & 3, (y + sign * q) & 3
    return y * 4 + z, x * 2 + ((qblk + (m >> 4)) & 1)


def source(axis, head, qblk, row):
    p, q = offsets(row >> 4)
    i = (row >> 2) & 3
    x, y, z = qblk >> 1, head >> 2, head & 3
    if axis == 0:
        x, y, z = i, (y - p) & 3, (z - q) & 3
    elif axis == 1:
        x, y, z = (x - p) & 3, i, (z - q) & 3
    else:
        x, y, z = (x - p) & 3, (y - q) & 3, i
    return x * 64 + y * 16 + z * 4 + (row & 3)


def one_hot(hit):
    return jnp.where(hit, 1.0, 0.0).astype(BF16)


def route(axis, head, qblk, info, pick, mix):
    line = info[axis, 0]
    for i in range(1, 4):
        line += pltpu.roll(info[axis, i], 32 * i, 1)
    expert = iota((128, 128), 0).astype(F32)
    token = iota((128, 128), 1)
    named = jnp.zeros((128, 128), F32)
    weight = jnp.zeros((128, 128), F32)
    for k in range(8):
        hit = line[k:k + 1] == expert
        named = jnp.where(hit, 1.0, named)
        weight = jnp.where(hit, line[8 + k:9 + k], weight)
    before = iota((128, 128), 0)
    later = one_hot((before < token) & (before >> 5 == token >> 5))
    rank = jnp.where(named > 0.0, dot(named.astype(BF16), later), -1.0)
    high = weight.astype(BF16)
    low = (weight - high.astype(F32)).astype(BF16)
    m_head, m_qblk = partner(axis, head, qblk, iota((32, 128), 0), 1)
    order = one_hot(m_head * 8 + m_qblk == iota((32, 128), 1))
    rank = dot(order, rank.astype(BF16))

    j = iota((512, 128), 0)
    at = dot(one_hot(iota((512, 32), 0) >> 4 == iota((512, 32), 1)), rank.astype(BF16))
    take = (at == (j & 3).astype(F32)) & ((j >> 2) & 3 == iota((512, 128), 1) >> 5)
    pick[axis] = one_hot(take)
    spread = one_hot(iota((32, 512), 1) >> 4 == iota((32, 512), 0))
    j = iota((128, 512), 1)
    at = dot(rank.T.astype(BF16), spread)
    take = (at == (j & 3).astype(F32)) & ((j >> 2) & 3 == iota((128, 512), 0) >> 5)
    for i, w in enumerate((high, low)):
        w = dot(dot(order, w).T.astype(BF16), spread)
        mix[axis, i] = jnp.where(take, w, 0.0).astype(BF16)


def layer_kernel(
    q_ref, key_ref, value_ref, vis_ref, res_ref, gain_ref, ids_ref, rw_ref, w_ref, wg_ref, wu_ref, wd_ref,
    out_ref,
    kv, q_buf, w_buf, vt, top, den, acc, att, total, part, got,
    own_sem, w_sem, kv_send, kv_recv, q_send, q_recv, w_send, wz_recv, wx_recv, wf_recv, ws_recv, send1, recv1,
    wg, wu, wd, hid, own_info, info, pick, mix, sort, unsort, x_buf, y_buf,
    lines_x, lines_y, lines_z, out_x, out_y, out_z, in_x, in_y, in_z, ret_x, ret_y, ret_z, back_x, back_y, back_z,
    sum_x, sum_y, sum_z, got_x, got_y, got_z,
    e_sem, info_send, info_recv, line_send, line_recv, send3, recv3, send4, recv4, sum_send, sum_recv, plane_sem, all_sem,
):
    head, qblk = lax.axis_index("head"), lax.axis_index("qblk")
    yy, zz = head // 4, lax.rem(head, 4)
    xx, core = qblk // 2, lax.rem(qblk, 2)
    sibling = 2 * xx + 1 - core

    def remote(src, dst, ssem, rsem, h, q):
        c = pltpu.make_async_remote_copy(
            src_ref=src, dst_ref=dst, send_sem=ssem, recv_sem=rsem,
            device_id=(h, q), device_id_type=MESH,
        )
        c.start()

    def signal(sem, h, q):
        pl.semaphore_signal(sem, inc=1, device_id=(h, q), device_id_type=MESH)

    y_line = [(lax.rem(yy + d, 4) * 4 + zz, qblk) for d in (1, 3, 2)]
    z_line = [(yy * 4 + lax.rem(zz + d, 4), qblk) for d in (1, 3, 2)]
    x_line = [(head, lax.rem(qblk + d, 8)) for d in range(1, 8)]

    place = (xx, yy, zz)
    peers = (
        [(head, 2 * lax.rem(xx + d, 4) + core) for d in (1, 3, 2)], y_line, z_line,
    )
    lines, outbox, inbox = (lines_x, lines_y, lines_z), (out_x, out_y, out_z), (in_x, in_y, in_z)
    ybox, backbox = (ret_x, ret_y, ret_z), (back_x, back_y, back_z)
    sums, others = (sum_x, sum_y, sum_z), (got_x, got_y, got_z)

    def rows32(i):
        return pl.ds(pl.multiple_of(i * 32, 32), 32)

    barrier = pltpu.get_barrier_semaphore()
    for h, q in x_line + y_line + z_line:
        signal(barrier, h, q)
    pl.semaphore_wait(barrier, 13)

    for d in (1, 3, 2):
        z2 = lax.rem(zz + d, 4)
        remote(q_ref.at[:, z2], q_buf.at[zz], q_send, q_recv.at[zz], yy * 4 + z2, qblk)
    for j, src in enumerate((key_ref, value_ref)):
        remote(src.at[yy], kv.at[qblk, j], kv_send, kv_recv.at[qblk], head, sibling)
        for dx in (1, 3, 2):
            peer = 2 * lax.rem(xx + dx, 4) + core
            remote(src.at[yy], kv.at[qblk, j], kv_send, kv_recv.at[qblk], head, peer)
    own = jnp.concatenate([ids_ref[...].astype(F32), rw_ref[...]], axis=0)
    own_info[...] = jnp.concatenate([own, jnp.zeros((16, 96), F32)], axis=1)
    for a in range(3):
        info[a, place[a]] = own_info[...]
        for h, q in peers[a]:
            remote(own_info, info.at[a, place[a]], info_send, info_recv.at[a], h, q)
    def w_rows(z, first, count):
        return pl.ds(pl.multiple_of(z * 256 + first, 16), count)

    mine16 = 128 + core * 64 + xx * 16
    for d in (1, 3, 2):
        z2 = lax.rem(zz + d, 4)
        remote(w_ref.at[w_rows(0, mine16, 16)], w_buf.at[w_rows(zz, mine16, 16)],
               w_send, wx_recv.at[zz], yy * 4 + z2, qblk)
    for d in (1, 3, 2):
        z2 = lax.rem(zz + d, 4)
        remote(w_ref.at[w_rows(0, core * 64, 64)], w_buf.at[w_rows(zz, core * 64, 64)],
               w_send, wz_recv.at[zz], yy * 4 + z2, qblk)
    for j, src in enumerate((key_ref, value_ref)):
        pltpu.make_async_copy(src.at[yy], kv.at[qblk, j], own_sem).start()
    pltpu.make_async_copy(q_ref.at[:, zz], q_buf.at[zz], q_recv.at[zz]).start()
    for h, q in y_line:
        signal(plane_sem, h, q)
    w_copy = pltpu.make_async_copy(w_ref, w_buf.at[w_rows(zz, 0, 256)], w_sem)
    w_copy.start()
    w_copies = [
        pltpu.make_async_copy(src.at[0], dst, e_sem.at[i])
        for i, (src, dst) in enumerate(((wg_ref, wg), (wu_ref, wu), (wd_ref, wd)))
    ]
    for c in w_copies:
        c.start()
    for a in range(3):
        wait_bytes(info.at[a, pl.ds(0, 3)], info_recv.at[a])
        route(a, head, qblk, info, pick, mix)
        sort[a] = one_hot(source(a, head, qblk, iota((256, 256), 1)) == iota((256, 256), 0))
        unsort[a] = one_hot(source(a, head, qblk, iota((256, 256), 0)) == iota((256, 256), 1))
    pl.semaphore_wait(plane_sem, 3)
    for h, q in z_line:
        signal(all_sem, h, q)
    lane = iota((8, 128), 1)
    seen_all = jnp.zeros((8, 128), jnp.int32)
    for i in range(4):
        block = jnp.broadcast_to(vis_ref[:, i * 128:(i + 1) * 128], (8, 128))
        block = pltpu.roll(block, lax.rem((i - zz) * 32 + 128, 128), 1)
        seen_all = jnp.where(lane // 32 == i, block, seen_all)
    seen_all = jnp.concatenate([seen_all, seen_all], axis=1)[:1]

    wait_bytes(kv.at[qblk], own_sem)
    for d in range(4):
        z2 = lax.rem(zz + d, 4)
        wait_bytes(q_buf.at[z2], q_recv.at[z2])

    top[...] = jnp.full(top.shape, NEG, F32)
    den[...] = jnp.zeros(den.shape, F32)
    acc[...] = jnp.zeros(acc.shape, F32)

    for dx in (0, 1, 3, 2):
        chip = lax.rem(xx + dx, 4)
        if dx:
            mine = 2 * chip + core
            wait_bytes(kv.at[mine], kv_recv.at[mine])
            remote(kv.at[mine], kv.at[mine], kv_send, kv_recv.at[mine], head, sibling)
        other = 2 * chip + 1 - core
        wait_bytes(kv.at[other], kv_recv.at[other])
        keys = kv[pl.ds(2 * chip, 2), 0].reshape(512, HD)
        vt[...] = kv[pl.ds(2 * chip, 2), 1].reshape(512, HD).astype(F32).T.astype(BF16)
        base = chip * 512

        def rows(i, carry, keys=keys, base=base):
            q = q_buf[i].reshape(128, 2 * HD)
            q = jnp.concatenate([q[:, :HD], q[:, HD:]], axis=0)
            cols = pl.ds(pl.multiple_of(i * 256, 256), 256)
            s = dot_nt(keys, q)
            s = jnp.where(iota(s.shape, 0) < seen_all - base, s, NEG)
            old = top[:, cols]
            new = jnp.maximum(old, jnp.max(s, axis=0, keepdims=True))
            p = jnp.exp2((s - new) * QSCALE)
            scale = jnp.exp2((old - new) * QSCALE)
            top[:, cols] = new
            den[:, cols] = den[:, cols] * scale + jnp.sum(p, axis=0, keepdims=True)
            acc[:, cols] = acc[:, cols] * scale + dot(vt[...], p.astype(BF16))
            return carry

        lax.fori_loop(0, 4, rows, 0, unroll=True)

        if dx == 0:
            for d in (1, 3, 2):
                z2 = lax.rem(zz + d, 4)
                wait_bytes(w_buf.at[w_rows(z2, mine16, 16)], wx_recv.at[z2])
                for ex in (1, 3, 2):
                    peer = 2 * lax.rem(xx + ex, 4) + core
                    remote(w_buf.at[w_rows(z2, mine16, 16)], w_buf.at[w_rows(z2, mine16, 16)],
                           w_send, wf_recv.at[z2], head, peer)

    for n in range(8):
        cols = slice(n * HD, (n + 1) * HD)
        att[n // 2, :, (n % 2) * HD:(n % 2 + 1) * HD] = (acc[:, cols] / den[:, cols]).T.astype(BF16)

    for d in (1, 3):
        z2 = lax.rem(zz + d, 4)
        here = w_rows(z2, core * 64, 64)
        wait_bytes(w_buf.at[here], wz_recv.at[z2])
        remote(w_buf.at[here], w_buf.at[here], w_send, ws_recv.at[z2, 0], head, sibling)
    for d in (1, 3, 2):
        z2 = lax.rem(zz + d, 4)
        wait_bytes(w_buf.at[w_rows(z2, 0, 48)], wf_recv.at[z2])
        here = w_rows(z2, 128 + core * 64, 64)
        remote(w_buf.at[here], w_buf.at[here], w_send, ws_recv.at[z2, 1], head, sibling)
    z2 = lax.rem(zz + 2, 4)
    here = w_rows(z2, core * 64, 64)
    wait_bytes(w_buf.at[here], wz_recv.at[z2])
    remote(w_buf.at[here], w_buf.at[here], w_send, ws_recv.at[z2, 0], head, sibling)

    w_copy.wait()
    total[...] = dot(att[zz], w_buf[w_rows(zz, 0, 256), :])
    for d in (1, 3, 2):
        z2 = lax.rem(zz + d, 4)
        for i in range(2):
            wait_bytes(w_buf.at[w_rows(z2, i * 128 + (1 - core) * 64, 64)], ws_recv.at[z2, i])
        if d != 2:
            total[...] += dot(att[z2], w_buf[w_rows(z2, 0, 256), :])
    for n in range(4):
        f = slice(n * 512, (n + 1) * 512)
        last = total[:, f] + dot(att[z2], w_buf[w_rows(z2, 0, 256), f])
        part[n] = last.reshape(4, 32, 512).astype(BF16)
        for d in (2, 1, 3):
            y2 = lax.rem(yy + d, 4)
            remote(part.at[n, y2], got.at[n, yy], send1, recv1.at[yy], y2 * 4 + zz, qblk)

    h = [
        res_ref[:, n * 512:(n + 1) * 512].astype(F32) + part[n, yy].astype(F32) for n in range(4)
    ]
    for d in (1, 3, 2):
        y2 = lax.rem(yy + d, 4)
        wait_bytes(got.at[:, y2], recv1.at[y2])
        h = [h[n] + got[n, y2].astype(F32) for n in range(4)]
    square = sum(jnp.sum(v * v, axis=1, keepdims=True) for v in h)
    rs = lax.rsqrt(square * (1.0 / D) + 1e-6)
    for n in range(4):
        hid[:, n * 512:(n + 1) * 512] = h[n]
    for a, f in enumerate(FEATURES):
        here = lines[a].at[rows32(place[a])]
        here[...] = (hid[:, f] * rs * gain_ref[:, f]).astype(BF16)
        for h, q in peers[a]:
            remote(here, here, line_send.at[a], line_recv.at[a], h, q)
    pl.semaphore_wait(all_sem, 3)
    for a in range(3):
        wait_bytes(lines[a].at[pl.ds(0, 96)], line_recv.at[a])

    def dispatch(m, carry):
        for a in range(3):
            h, q = partner(a, head, qblk, m, 1)
            remote(outbox[a].at[rows16(m)], inbox[a].at[rows16(m)], send3.at[a], recv3.at[a, m // 16], h, q)
        return carry

    for r in range(2):
        block = pl.ds(r * 256, 256)
        for a in range(3):
            outbox[a][block] = dot(pick[a, block], lines[a][...]).astype(BF16)
            if r == 0:
                pltpu.make_async_copy(outbox[a].at[rows16(0)], inbox[a].at[rows16(0)], recv3.at[a, 0]).start()
        lax.fori_loop(max(r * 16, 1), r * 16 + 16, dispatch, 0)

    for c in w_copies:
        c.wait()

    def one_round(r, carry):
        block = pl.ds(pl.multiple_of(r * 256, 256), 256)
        for a, f in enumerate(FEATURES):
            wait_bytes(inbox[a].at[block], recv3.at[a, r])
            x_buf[:, f] = dot(sort[a], inbox[a][block]).astype(BF16)
        gate = dot(x_buf[...], wg[...])
        up = dot(x_buf[...], wu[...])
        hidden = (gate / (1.0 + jnp.exp(-gate)) * up).astype(BF16)
        y_buf[...] = dot(hidden, wd[...]).astype(BF16)
        for a, f in enumerate(FEATURES):
            ybox[a][block] = dot(unsort[a], y_buf[:, f]).astype(BF16)

        def send_back(m, carry):
            for a in range(3):
                h, q = partner(a, head, qblk, m, -1)
                remote(ybox[a].at[rows16(m)], backbox[a].at[rows16(m)], send4.at[a], recv4.at[a, r], h, q)
            return carry

        @pl.when(r == 0)
        def _():
            for a in range(3):
                pltpu.make_async_copy(ybox[a].at[rows16(0)], backbox[a].at[rows16(0)], recv4.at[a, 0]).start()

        lax.fori_loop(jnp.maximum(r * 16, 1), r * 16 + 16, send_back, 0)
        return carry

    lax.fori_loop(0, 2, one_round, 0)

    for a in range(3):
        mixed = jnp.zeros((128, WIDTH[a]), F32)
        for r in range(2):
            block = slice(r * 256, (r + 1) * 256)
            wait_bytes(backbox[a].at[block], recv4.at[a, r])
            mixed += dot(mix[a, 0, :, block], backbox[a][block]) + dot(mix[a, 1, :, block], backbox[a][block])
        sums[a][...] = mixed.astype(BF16)
        for d, (h, q) in zip((1, 3, 2), peers[a]):
            remote(sums[a].at[rows32(lax.rem(place[a] + d, 4))], others[a].at[rows32(place[a])],
                   sum_send.at[a], sum_recv.at[a], h, q)
    for a, f in enumerate(FEATURES):
        v = hid[:, f] + sums[a][rows32(place[a])].astype(F32)
        wait_bytes(others[a].at[pl.ds(0, 96)], sum_recv.at[a])
        for d in (1, 3, 2):
            v += others[a][rows32(lax.rem(place[a] + d, 4))].astype(F32)
        out_ref[:, f] = v.astype(BF16)
    wait_bytes(kv.at[pl.ds(0, 7)], kv_send)
    wait_bytes(q_buf.at[pl.ds(0, 3)], q_send)
    wait_bytes(w_buf.at[pl.ds(0, 768)], w_send)
    wait_bytes(part.at[:, pl.ds(0, 3)], send1)
    wait_bytes(info.at[:, pl.ds(0, 3)], info_send)
    for a in range(3):
        wait_bytes(lines[a].at[pl.ds(0, 96)], line_send.at[a])
        wait_bytes(outbox[a].at[pl.ds(0, 31 * 16)], send3.at[a])
        wait_bytes(ybox[a].at[pl.ds(0, 31 * 16)], send4.at[a])
        wait_bytes(sums[a].at[pl.ds(0, 96)], sum_send.at[a])


def per_device(
    residual, queries, key_cache, value_cache, visible_len, out_weight, norm_gain,
    expert_ids, route_weights, w_gate, w_up, w_down,
):
    vmem, hbm = pl.BlockSpec(memory_space=pltpu.VMEM), pl.BlockSpec(memory_space=pl.ANY)
    dma, scratch = pltpu.SemaphoreType.DMA, pltpu.VMEM
    return pl.pallas_call(
        layer_kernel,
        out_shape=jax.ShapeDtypeStruct((32, D), BF16),
        in_specs=[hbm, hbm, hbm, vmem, vmem, vmem, vmem, vmem, hbm, hbm, hbm, hbm],
        out_specs=vmem,
        scratch_shapes=[
            scratch((8, 2, 256, HD), BF16),
            scratch((4, 4, 32, 2 * HD), BF16),
            scratch((1024, D), BF16),
            scratch((HD, 512), BF16),
            scratch((1, 1024), F32),
            scratch((1, 1024), F32),
            scratch((HD, 1024), F32),
            scratch((4, 128, 2 * HD), BF16),
            scratch((128, D), F32),
            scratch((4, 4, 32, 512), BF16),
            scratch((4, 4, 32, 512), BF16),
            dma, dma, dma, dma((8,)), dma, dma((4,)), dma, dma((4,)), dma((4,)), dma((4,)), dma((4, 2)), dma, dma((4,)),
            scratch((D, FF), BF16),
            scratch((D, FF), BF16),
            scratch((FF, D), BF16),
            scratch((32, D), F32),
            scratch((16, 128), F32),
            scratch((3, 4, 16, 128), F32),
            scratch((3, 512, 128), BF16),
            scratch((3, 2, 128, 512), BF16),
            scratch((3, 256, 256), BF16),
            scratch((3, 256, 256), BF16),
            scratch((256, D), BF16),
            scratch((256, D), BF16),
            *[scratch((rows, w), BF16) for rows in (128, 512, 512, 512, 512, 128, 128) for w in WIDTH],
            dma((3,)), dma, dma((3,)), dma((3,)), dma((3,)), dma((3,)), dma((3, 2)), dma((3,)), dma((3, 2)), dma((3,)), dma((3,)),
            pltpu.SemaphoreType.REGULAR, pltpu.SemaphoreType.REGULAR,
        ],
        compiler_params=pltpu.CompilerParams(
            collective_id=0, has_side_effects=True, vmem_limit_bytes=VMEM_LIMIT
        ),
        name="layer",
    )(
        queries.reshape(4, 4, 32, 2 * HD), key_cache, value_cache, visible_len.reshape(1, -1), residual,
        norm_gain.reshape(1, -1), expert_ids.T, route_weights.T, out_weight, w_gate, w_up, w_down,
    )


def solution(mesh):
    in_specs = (
        P(("qblk", "head"), None),
        P("qblk", "head"),
        P(None, "qblk", None),
        P(None, "qblk", None),
        P("qblk"),
        P("head", None),
        P(),
        P(("qblk", "head"), None),
        P(("qblk", "head"), None),
        P(("head", "qblk"), None, None),
        P(("head", "qblk"), None, None),
        P(("head", "qblk"), None, None),
    )
    return jax.shard_map(
        per_device, mesh=mesh, in_specs=in_specs, out_specs=P(("qblk", "head"), None),
        check_vma=False,
    )
```

```python
import jax
import jax.numpy as jnp
from jax import lax
from jax.experimental import pallas as pl
from jax.experimental.pallas import tpu as pltpu
from jax.sharding import PartitionSpec as P

MESH = pl.DeviceIdType.MESH
F32, BF16 = jnp.float32, jnp.bfloat16
D = 2048
HD = 128
FF = 768
NEG = -1e30
WIDTH = (640, 640, 768)
FEATURES = (slice(0, 640), slice(640, 1280), slice(1280, 2048))
QSCALE = HD ** (-0.5) * 1.4426950408889634
VMEM_LIMIT = 58 * 1024 * 1024


def dot(a, b):
    return jnp.dot(a, b, preferred_element_type=F32)


def dot_nt(a, b):
    return lax.dot_general(a, b, (((1,), (1,)), ((), ())), preferred_element_type=F32)


def dot_tn(a, b):
    return lax.dot_general(a, b, (((0,), (0,)), ((), ())), preferred_element_type=F32)


def wait_bytes(ref, sem):
    pltpu.make_async_copy(ref, ref, sem).wait()


def iota(shape, axis):
    return lax.broadcasted_iota(jnp.int32, shape, axis)


def rows16(i):
    return pl.ds(pl.multiple_of(i * 16, 16), 16)


def offsets(m):
    e = ((m & 15) * 5) & 15
    return e >> 2, e & 3


def partner(axis, head, qblk, m, sign):
    p, q = offsets(m)
    x, y, z = qblk >> 1, head >> 2, head & 3
    if axis == 0:
        y, z = (y + sign * p) & 3, (z + sign * q) & 3
    elif axis == 1:
        x, z = (x + sign * p) & 3, (z + sign * q) & 3
    else:
        x, y = (x + sign * p) & 3, (y + sign * q) & 3
    return y * 4 + z, x * 2 + ((qblk + (m >> 4)) & 1)


def source(axis, head, qblk, row):
    p, q = offsets(row >> 4)
    i = (row >> 2) & 3
    x, y, z = qblk >> 1, head >> 2, head & 3
    if axis == 0:
        x, y, z = i, (y - p) & 3, (z - q) & 3
    elif axis == 1:
        x, y, z = (x - p) & 3, i, (z - q) & 3
    else:
        x, y, z = (x - p) & 3, (y - q) & 3, i
    return x * 64 + y * 16 + z * 4 + (row & 3)


def one_hot(hit):
    return jnp.where(hit, 1.0, 0.0).astype(BF16)


def route(axis, head, qblk, info, pick, tab):
    line = info[axis, 0]
    for i in range(1, 4):
        line += pltpu.roll(info[axis, i], 32 * i, 1)
    expert = iota((128, 128), 0).astype(F32)
    token = iota((128, 128), 1)
    named = jnp.zeros((128, 128), F32)
    weight = jnp.zeros((128, 128), F32)
    for k in range(8):
        hit = line[k:k + 1] == expert
        named = jnp.where(hit, 1.0, named)
        weight = jnp.where(hit, line[8 + k:9 + k], weight)
    before = iota((128, 128), 0)
    later = one_hot((before < token) & (before >> 5 == token >> 5))
    rank = jnp.where(named > 0.0, dot(named.astype(BF16), later), -1.0)
    high = weight.astype(BF16)
    low = (weight - high.astype(F32)).astype(BF16)
    m_head, m_qblk = partner(axis, head, qblk, iota((32, 128), 0), 1)
    order = one_hot(m_head * 8 + m_qblk == iota((32, 128), 1))
    rank = dot(order, rank.astype(BF16))

    j = iota((512, 128), 0)
    at = dot(one_hot(iota((512, 32), 0) >> 4 == iota((512, 32), 1)), rank.astype(BF16))
    take = (at == (j & 3).astype(F32)) & ((j >> 2) & 3 == iota((512, 128), 1) >> 5)
    pick[axis] = one_hot(take)
    tab[axis, 0] = rank
    for i, w in enumerate((high, low)):
        tab[axis, 1 + i] = dot(order, w)


def route_back(axis, tab, mix):
    spread = one_hot(iota((32, 512), 1) >> 4 == iota((32, 512), 0))
    j = iota((128, 512), 1)
    at = dot(tab[axis, 0].T.astype(BF16), spread)
    take = (at == (j & 3).astype(F32)) & ((j >> 2) & 3 == iota((128, 512), 0) >> 5)
    for i in range(2):
        w = dot(tab[axis, 1 + i].T.astype(BF16), spread)
        mix[axis, i] = jnp.where(take, w, 0.0).astype(BF16)


def layer_kernel(
    q_ref, key_ref, value_ref, vis_ref, res_ref, gain_ref, ids_ref, rw_ref, w_ref, wg_ref, wu_ref, wd_ref,
    out_ref,
    kv, q_buf, w_buf, vt, top, den, acc, att, total, part, got,
    own_sem, w_sem, kv_send, kv_recv, q_send, q_recv, w_send, wz_recv, wx_recv, wf_recv, ws_recv, send1, recv1,
    wg, wu, wd, hid, own_info, info, pick, tab, mix, sort, unsort, x_buf, y_buf,
    lines_x, lines_y, lines_z, out_x, out_y, out_z, in_x, in_y, in_z, ret_x, ret_y, ret_z, back_x, back_y, back_z,
    sum_x, sum_y, sum_z, got_x, got_y, got_z,
    e_sem, info_send, info_recv, line_send, line_recv, send3, recv3, send4, recv4, sum_send, sum_recv, plane_sem, all_sem,
):
    head, qblk = lax.axis_index("head"), lax.axis_index("qblk")
    yy, zz = head // 4, lax.rem(head, 4)
    xx, core = qblk // 2, lax.rem(qblk, 2)
    sibling = 2 * xx + 1 - core

    def remote(src, dst, ssem, rsem, h, q):
        c = pltpu.make_async_remote_copy(
            src_ref=src, dst_ref=dst, send_sem=ssem, recv_sem=rsem,
            device_id=(h, q), device_id_type=MESH,
        )
        c.start()

    def signal(sem, h, q):
        pl.semaphore_signal(sem, inc=1, device_id=(h, q), device_id_type=MESH)

    y_line = [(lax.rem(yy + d, 4) * 4 + zz, qblk) for d in (1, 3, 2)]
    z_line = [(yy * 4 + lax.rem(zz + d, 4), qblk) for d in (1, 3, 2)]
    x_line = [(head, lax.rem(qblk + d, 8)) for d in range(1, 8)]

    place = (xx, yy, zz)
    peers = (
        [(head, 2 * lax.rem(xx + d, 4) + core) for d in (1, 3, 2)], y_line, z_line,
    )
    lines, outbox, inbox = (lines_x, lines_y, lines_z), (out_x, out_y, out_z), (in_x, in_y, in_z)
    ybox, backbox = (ret_x, ret_y, ret_z), (back_x, back_y, back_z)
    sums, others = (sum_x, sum_y, sum_z), (got_x, got_y, got_z)

    def rows32(i):
        return pl.ds(pl.multiple_of(i * 32, 32), 32)

    barrier = pltpu.get_barrier_semaphore()
    for h, q in x_line + y_line + z_line:
        signal(barrier, h, q)
    pl.semaphore_wait(barrier, 13)

    for d in (1, 3, 2):
        z2 = lax.rem(zz + d, 4)
        remote(q_ref.at[:, z2], q_buf.at[zz], q_send, q_recv.at[zz], yy * 4 + z2, qblk)
    for j, src in enumerate((key_ref, value_ref)):
        remote(src.at[yy], kv.at[qblk, j], kv_send, kv_recv.at[qblk], head, sibling)
        for dx in (1, 3, 2):
            peer = 2 * lax.rem(xx + dx, 4) + core
            remote(src.at[yy], kv.at[qblk, j], kv_send, kv_recv.at[qblk], head, peer)
    own = jnp.concatenate([ids_ref[...].astype(F32), rw_ref[...]], axis=0)
    own_info[...] = jnp.concatenate([own, jnp.zeros((16, 96), F32)], axis=1)
    for a in range(3):
        info[a, place[a]] = own_info[...]
        for h, q in peers[a]:
            remote(own_info, info.at[a, place[a]], info_send, info_recv.at[a], h, q)
    def w_rows(z, first, count):
        return pl.ds(pl.multiple_of(z * 256 + first, 16), count)

    mine16 = 128 + core * 64 + xx * 16
    for d in (1, 3, 2):
        z2 = lax.rem(zz + d, 4)
        remote(w_ref.at[w_rows(0, mine16, 16)], w_buf.at[w_rows(zz, mine16, 16)],
               w_send, wx_recv.at[zz], yy * 4 + z2, qblk)
    for d in (1, 3, 2):
        z2 = lax.rem(zz + d, 4)
        remote(w_ref.at[w_rows(0, core * 64, 64)], w_buf.at[w_rows(zz, core * 64, 64)],
               w_send, wz_recv.at[zz], yy * 4 + z2, qblk)
    for j, src in enumerate((key_ref, value_ref)):
        pltpu.make_async_copy(src.at[yy], kv.at[qblk, j], own_sem).start()
    pltpu.make_async_copy(q_ref.at[:, zz], q_buf.at[zz], q_recv.at[zz]).start()
    for h, q in y_line:
        signal(plane_sem, h, q)
    w_copy = pltpu.make_async_copy(w_ref, w_buf.at[w_rows(zz, 0, 256)], w_sem)
    w_copy.start()
    w_copies = [
        pltpu.make_async_copy(src.at[0], dst, e_sem.at[i])
        for i, (src, dst) in enumerate(((wg_ref, wg), (wu_ref, wu), (wd_ref, wd)))
    ]
    for c in w_copies:
        c.start()
    pl.semaphore_wait(plane_sem, 3)
    for h, q in z_line:
        signal(all_sem, h, q)
    lane = iota((8, 128), 1)
    seen_all = jnp.zeros((8, 128), jnp.int32)
    for i in range(4):
        block = jnp.broadcast_to(vis_ref[:, i * 128:(i + 1) * 128], (8, 128))
        block = pltpu.roll(block, lax.rem((i - zz) * 32 + 128, 128), 1)
        seen_all = jnp.where(lane // 32 == i, block, seen_all)
    seen_all = jnp.concatenate([seen_all, seen_all], axis=1)[:1]

    wait_bytes(kv.at[qblk], own_sem)
    for d in range(4):
        z2 = lax.rem(zz + d, 4)
        wait_bytes(q_buf.at[z2], q_recv.at[z2])

    top[...] = jnp.full(top.shape, NEG, F32)
    den[...] = jnp.zeros(den.shape, F32)
    acc[...] = jnp.zeros(acc.shape, F32)

    for dx in (0, 1, 3, 2):
        chip = lax.rem(xx + dx, 4)
        if dx:
            mine = 2 * chip + core
            wait_bytes(kv.at[mine], kv_recv.at[mine])
            remote(kv.at[mine], kv.at[mine], kv_send, kv_recv.at[mine], head, sibling)
        other = 2 * chip + 1 - core
        wait_bytes(kv.at[other], kv_recv.at[other])
        keys = kv[pl.ds(2 * chip, 2), 0].reshape(512, HD)
        vt[...] = kv[pl.ds(2 * chip, 2), 1].reshape(512, HD).astype(F32).T.astype(BF16)
        base = chip * 512

        def rows(i, carry, keys=keys, base=base):
            q = q_buf[i].reshape(128, 2 * HD)
            q = jnp.concatenate([q[:, :HD], q[:, HD:]], axis=0)
            cols = pl.ds(pl.multiple_of(i * 256, 256), 256)
            s = dot_nt(keys, q)
            s = jnp.where(iota(s.shape, 0) < seen_all - base, s, NEG)
            old = top[:, cols]
            new = jnp.maximum(old, jnp.max(s, axis=0, keepdims=True))
            p = jnp.exp2((s - new) * QSCALE)
            scale = jnp.exp2((old - new) * QSCALE)
            top[:, cols] = new
            den[:, cols] = den[:, cols] * scale + jnp.sum(p, axis=0, keepdims=True)
            acc[:, cols] = acc[:, cols] * scale + dot(vt[...], p.astype(BF16))
            return carry

        lax.fori_loop(0, 4, rows, 0, unroll=True)

        if dx == 0:
            for d in (1, 3, 2):
                z2 = lax.rem(zz + d, 4)
                wait_bytes(w_buf.at[w_rows(z2, mine16, 16)], wx_recv.at[z2])
                for ex in (1, 3, 2):
                    peer = 2 * lax.rem(xx + ex, 4) + core
                    remote(w_buf.at[w_rows(z2, mine16, 16)], w_buf.at[w_rows(z2, mine16, 16)],
                           w_send, wf_recv.at[z2], head, peer)

    for n in range(8):
        cols = slice(n * HD, (n + 1) * HD)
        att[n // 2, :, (n % 2) * HD:(n % 2 + 1) * HD] = (acc[:, cols] / den[:, cols]).T.astype(BF16)

    for d in (1, 3):
        z2 = lax.rem(zz + d, 4)
        here = w_rows(z2, core * 64, 64)
        wait_bytes(w_buf.at[here], wz_recv.at[z2])
        remote(w_buf.at[here], w_buf.at[here], w_send, ws_recv.at[z2, 0], head, sibling)
    for d in (1, 3, 2):
        z2 = lax.rem(zz + d, 4)
        wait_bytes(w_buf.at[w_rows(z2, 0, 48)], wf_recv.at[z2])
        here = w_rows(z2, 128 + core * 64, 64)
        remote(w_buf.at[here], w_buf.at[here], w_send, ws_recv.at[z2, 1], head, sibling)
    z2 = lax.rem(zz + 2, 4)
    here = w_rows(z2, core * 64, 64)
    wait_bytes(w_buf.at[here], wz_recv.at[z2])
    remote(w_buf.at[here], w_buf.at[here], w_send, ws_recv.at[z2, 0], head, sibling)

    w_copy.wait()
    total[...] = dot(att[zz], w_buf[w_rows(zz, 0, 256), :])
    for d in (1, 3, 2):
        z2 = lax.rem(zz + d, 4)
        for i in range(2):
            wait_bytes(w_buf.at[w_rows(z2, i * 128 + (1 - core) * 64, 64)], ws_recv.at[z2, i])
        if d != 2:
            total[...] += dot(att[z2], w_buf[w_rows(z2, 0, 256), :])
    for n in range(4):
        f = slice(n * 512, (n + 1) * 512)
        last = total[:, f] + dot(att[z2], w_buf[w_rows(z2, 0, 256), f])
        part[n] = last.reshape(4, 32, 512).astype(BF16)
        for d in (2, 1, 3):
            y2 = lax.rem(yy + d, 4)
            remote(part.at[n, y2], got.at[n, yy], send1, recv1.at[yy], y2 * 4 + zz, qblk)

    for a in range(3):
        wait_bytes(info.at[a, pl.ds(0, 3)], info_recv.at[a])
        route(a, head, qblk, info, pick, tab)

    h = [
        res_ref[:, n * 512:(n + 1) * 512].astype(F32) + part[n, yy].astype(F32) for n in range(4)
    ]
    for d in (1, 3, 2):
        y2 = lax.rem(yy + d, 4)
        wait_bytes(got.at[:, y2], recv1.at[y2])
        h = [h[n] + got[n, y2].astype(F32) for n in range(4)]
    square = sum(jnp.sum(v * v, axis=1, keepdims=True) for v in h)
    rs = lax.rsqrt(square * (1.0 / D) + 1e-6)
    for n in range(4):
        hid[:, n * 512:(n + 1) * 512] = h[n]
    for a, f in enumerate(FEATURES):
        here = lines[a].at[rows32(place[a])]
        here[...] = (hid[:, f] * rs * gain_ref[:, f]).astype(BF16)
        for h, q in peers[a]:
            remote(here, here, line_send.at[a], line_recv.at[a], h, q)
    pl.semaphore_wait(all_sem, 3)
    for a in range(3):
        wait_bytes(lines[a].at[pl.ds(0, 96)], line_recv.at[a])

    def dispatch(m, carry):
        for a in range(3):
            h, q = partner(a, head, qblk, m, 1)
            remote(outbox[a].at[rows16(m)], inbox[a].at[rows16(m)], send3.at[a], recv3.at[a, m // 16], h, q)
        return carry

    for r in range(2):
        block = pl.ds(r * 256, 256)
        for a in range(3):
            outbox[a][block] = dot(pick[a, block], lines[a][...]).astype(BF16)
            if r == 0:
                pltpu.make_async_copy(outbox[a].at[rows16(0)], inbox[a].at[rows16(0)], recv3.at[a, 0]).start()
        lax.fori_loop(max(r * 16, 1), r * 16 + 16, dispatch, 0)

    for a in range(3):
        sort[a] = one_hot(source(a, head, qblk, iota((256, 256), 1)) == iota((256, 256), 0))
        unsort[a] = one_hot(source(a, head, qblk, iota((256, 256), 0)) == iota((256, 256), 1))
        route_back(a, tab, mix)
    for c in w_copies:
        c.wait()

    def one_round(r, carry):
        block = pl.ds(pl.multiple_of(r * 256, 256), 256)
        for a, f in enumerate(FEATURES):
            wait_bytes(inbox[a].at[block], recv3.at[a, r])
            x_buf[:, f] = dot(sort[a], inbox[a][block]).astype(BF16)
        gate = dot(x_buf[...], wg[...])
        up = dot(x_buf[...], wu[...])
        hidden = (gate / (1.0 + jnp.exp(-gate)) * up).astype(BF16)
        y_buf[...] = dot(hidden, wd[...]).astype(BF16)
        for a, f in enumerate(FEATURES):
            ybox[a][block] = dot(unsort[a], y_buf[:, f]).astype(BF16)

        def send_back(m, carry):
            for a in range(3):
                h, q = partner(a, head, qblk, m, -1)
                remote(ybox[a].at[rows16(m)], backbox[a].at[rows16(m)], send4.at[a], recv4.at[a, r], h, q)
            return carry

        @pl.when(r == 0)
        def _():
            for a in range(3):
                pltpu.make_async_copy(ybox[a].at[rows16(0)], backbox[a].at[rows16(0)], recv4.at[a, 0]).start()

        lax.fori_loop(jnp.maximum(r * 16, 1), r * 16 + 16, send_back, 0)
        return carry

    lax.fori_loop(0, 2, one_round, 0)

    for a in range(3):
        mixed = jnp.zeros((128, WIDTH[a]), F32)
        for r in range(2):
            block = slice(r * 256, (r + 1) * 256)
            wait_bytes(backbox[a].at[block], recv4.at[a, r])
            mixed += dot(mix[a, 0, :, block], backbox[a][block]) + dot(mix[a, 1, :, block], backbox[a][block])
        sums[a][...] = mixed.astype(BF16)
        for d, (h, q) in zip((1, 3, 2), peers[a]):
            remote(sums[a].at[rows32(lax.rem(place[a] + d, 4))], others[a].at[rows32(place[a])],
                   sum_send.at[a], sum_recv.at[a], h, q)
    for a, f in enumerate(FEATURES):
        v = hid[:, f] + sums[a][rows32(place[a])].astype(F32)
        wait_bytes(others[a].at[pl.ds(0, 96)], sum_recv.at[a])
        for d in (1, 3, 2):
            v += others[a][rows32(lax.rem(place[a] + d, 4))].astype(F32)
        out_ref[:, f] = v.astype(BF16)
    wait_bytes(kv.at[pl.ds(0, 7)], kv_send)
    wait_bytes(q_buf.at[pl.ds(0, 3)], q_send)
    wait_bytes(w_buf.at[pl.ds(0, 768)], w_send)
    wait_bytes(part.at[:, pl.ds(0, 3)], send1)
    wait_bytes(info.at[:, pl.ds(0, 3)], info_send)
    for a in range(3):
        wait_bytes(lines[a].at[pl.ds(0, 96)], line_send.at[a])
        wait_bytes(outbox[a].at[pl.ds(0, 31 * 16)], send3.at[a])
        wait_bytes(ybox[a].at[pl.ds(0, 31 * 16)], send4.at[a])
        wait_bytes(sums[a].at[pl.ds(0, 96)], sum_send.at[a])


def per_device(
    residual, queries, key_cache, value_cache, visible_len, out_weight, norm_gain,
    expert_ids, route_weights, w_gate, w_up, w_down,
):
    vmem, hbm = pl.BlockSpec(memory_space=pltpu.VMEM), pl.BlockSpec(memory_space=pl.ANY)
    dma, scratch = pltpu.SemaphoreType.DMA, pltpu.VMEM
    return pl.pallas_call(
        layer_kernel,
        out_shape=jax.ShapeDtypeStruct((32, D), BF16),
        in_specs=[hbm, hbm, hbm, vmem, vmem, vmem, vmem, vmem, hbm, hbm, hbm, hbm],
        out_specs=vmem,
        scratch_shapes=[
            scratch((8, 2, 256, HD), BF16),
            scratch((4, 4, 32, 2 * HD), BF16),
            scratch((1024, D), BF16),
            scratch((HD, 512), BF16),
            scratch((1, 1024), F32),
            scratch((1, 1024), F32),
            scratch((HD, 1024), F32),
            scratch((4, 128, 2 * HD), BF16),
            scratch((128, D), F32),
            scratch((4, 4, 32, 512), BF16),
            scratch((4, 4, 32, 512), BF16),
            dma, dma, dma, dma((8,)), dma, dma((4,)), dma, dma((4,)), dma((4,)), dma((4,)), dma((4, 2)), dma, dma((4,)),
            scratch((D, FF), BF16),
            scratch((D, FF), BF16),
            scratch((FF, D), BF16),
            scratch((32, D), F32),
            scratch((16, 128), F32),
            scratch((3, 4, 16, 128), F32),
            scratch((3, 512, 128), BF16),
            scratch((3, 3, 32, 128), F32),
            scratch((3, 2, 128, 512), BF16),
            scratch((3, 256, 256), BF16),
            scratch((3, 256, 256), BF16),
            scratch((256, D), BF16),
            scratch((256, D), BF16),
            *[scratch((rows, w), BF16) for rows in (128, 512, 512, 512, 512, 128, 128) for w in WIDTH],
            dma((3,)), dma, dma((3,)), dma((3,)), dma((3,)), dma((3,)), dma((3, 2)), dma((3,)), dma((3, 2)), dma((3,)), dma((3,)),
            pltpu.SemaphoreType.REGULAR, pltpu.SemaphoreType.REGULAR,
        ],
        compiler_params=pltpu.CompilerParams(
            collective_id=0, has_side_effects=True, vmem_limit_bytes=VMEM_LIMIT
        ),
        name="layer",
    )(
        queries.reshape(4, 4, 32, 2 * HD), key_cache, value_cache, visible_len.reshape(1, -1), residual,
        norm_gain.reshape(1, -1), expert_ids.T, route_weights.T, out_weight, w_gate, w_up, w_down,
    )


def solution(mesh):
    in_specs = (
        P(("qblk", "head"), None),
        P("qblk", "head"),
        P(None, "qblk", None),
        P(None, "qblk", None),
        P("qblk"),
        P("head", None),
        P(),
        P(("qblk", "head"), None),
        P(("qblk", "head"), None),
        P(("head", "qblk"), None, None),
        P(("head", "qblk"), None, None),
        P(("head", "qblk"), None, None),
    )
    return jax.shard_map(
        per_device, mesh=mesh, in_specs=in_specs, out_specs=P(("qblk", "head"), None),
        check_vma=False,
    )
```

```python
import jax
import jax.numpy as jnp
from jax import lax
from jax.experimental import pallas as pl
from jax.experimental.pallas import tpu as pltpu
from jax.sharding import PartitionSpec as P

MESH = pl.DeviceIdType.MESH
F32, BF16 = jnp.float32, jnp.bfloat16
D = 2048
HD = 128
FF = 768
NEG = -1e30
WIDTH = (640, 640, 768)
FORWARD = (0, 3)
FEATURES = (slice(0, 640), slice(640, 1280), slice(1280, 2048))
QSCALE = HD ** (-0.5) * 1.4426950408889634
VMEM_LIMIT = 58 * 1024 * 1024


def dot(a, b):
    return jnp.dot(a, b, preferred_element_type=F32)


def dot_nt(a, b):
    return lax.dot_general(a, b, (((1,), (1,)), ((), ())), preferred_element_type=F32)


def dot_tn(a, b):
    return lax.dot_general(a, b, (((0,), (0,)), ((), ())), preferred_element_type=F32)


def wait_bytes(ref, sem):
    pltpu.make_async_copy(ref, ref, sem).wait()


def iota(shape, axis):
    return lax.broadcasted_iota(jnp.int32, shape, axis)


def rows16(i):
    return pl.ds(pl.multiple_of(i * 16, 16), 16)


def offsets(m):
    e = ((m & 15) * 5) & 15
    return e >> 2, e & 3


def partner(axis, head, qblk, m, sign):
    p, q = offsets(m)
    x, y, z = qblk >> 1, head >> 2, head & 3
    if axis == 0:
        y, z = (y + sign * p) & 3, (z + sign * q) & 3
    elif axis == 1:
        x, z = (x + sign * p) & 3, (z + sign * q) & 3
    else:
        x, y = (x + sign * p) & 3, (y + sign * q) & 3
    return y * 4 + z, x * 2 + ((qblk + (m >> 4)) & 1)


def source(axis, head, qblk, row):
    p, q = offsets(row >> 4)
    i = (row >> 2) & 3
    x, y, z = qblk >> 1, head >> 2, head & 3
    if axis == 0:
        x, y, z = i, (y - p) & 3, (z - q) & 3
    elif axis == 1:
        x, y, z = (x - p) & 3, i, (z - q) & 3
    else:
        x, y, z = (x - p) & 3, (y - q) & 3, i
    return x * 64 + y * 16 + z * 4 + (row & 3)


def one_hot(hit):
    return jnp.where(hit, 1.0, 0.0).astype(BF16)


def route(axis, head, qblk, info, pick, tab):
    line = info[axis, 0]
    for i in range(1, 4):
        line += pltpu.roll(info[axis, i], 32 * i, 1)
    expert = iota((128, 128), 0).astype(F32)
    token = iota((128, 128), 1)
    named = jnp.zeros((128, 128), F32)
    weight = jnp.zeros((128, 128), F32)
    for k in range(8):
        hit = line[k:k + 1] == expert
        named = jnp.where(hit, 1.0, named)
        weight = jnp.where(hit, line[8 + k:9 + k], weight)
    before = iota((128, 128), 0)
    later = one_hot((before < token) & (before >> 5 == token >> 5))
    rank = jnp.where(named > 0.0, dot(named.astype(BF16), later), -1.0)
    high = weight.astype(BF16)
    low = (weight - high.astype(F32)).astype(BF16)
    m_head, m_qblk = partner(axis, head, qblk, iota((32, 128), 0), 1)
    order = one_hot(m_head * 8 + m_qblk == iota((32, 128), 1))
    rank = dot(order, rank.astype(BF16))

    j = iota((512, 128), 0)
    at = dot(one_hot(iota((512, 32), 0) >> 4 == iota((512, 32), 1)), rank.astype(BF16))
    take = (at == (j & 3).astype(F32)) & ((j >> 2) & 3 == iota((512, 128), 1) >> 5)
    pick[axis] = one_hot(take)
    tab[axis, 0] = rank
    for i, w in enumerate((high, low)):
        tab[axis, 1 + i] = dot(order, w)


def route_back(axis, tab, mix):
    spread = one_hot(iota((32, 512), 1) >> 4 == iota((32, 512), 0))
    j = iota((128, 512), 1)
    at = dot(tab[axis, 0].T.astype(BF16), spread)
    take = (at == (j & 3).astype(F32)) & ((j >> 2) & 3 == iota((128, 512), 0) >> 5)
    for i in range(2):
        w = dot(tab[axis, 1 + i].T.astype(BF16), spread)
        mix[axis, i] = jnp.where(take, w, 0.0).astype(BF16)


def layer_kernel(
    q_ref, key_ref, value_ref, vis_in, res_in, gain_in, ids_in, rw_in, w_ref, wg_ref, wu_ref, wd_ref,
    out_ref,
    vis_ref, res_ref, gain_ref, ids_ref, rw_ref, small_sem,
    kv, q_buf, q_t, w_buf, vt, top, den, acc, att, total, part, got,
    own_sem, w_sem, kv_send, kv_recv, q_send, q_recv, w_send, wz_recv, wx_recv, wf_recv, ws_recv, send1, recv1,
    wg, wu, wd, hid, own_info, info, pick, tab, mix, sort, unsort, x_buf, y_buf,
    lines_x, lines_y, lines_z, out_x, out_y, out_z, in_x, in_y, in_z, ret_x, ret_y, ret_z, back_x, back_y, back_z,
    sum_x, sum_y, sum_z, got_x, got_y, got_z,
    e_sem, info_send, info_recv, line_send, line_recv, send3, recv3, send4, recv4, sum_send, sum_recv, plane_sem, all_sem,
):
    head, qblk = lax.axis_index("head"), lax.axis_index("qblk")
    yy, zz = head // 4, lax.rem(head, 4)
    xx, core = qblk // 2, lax.rem(qblk, 2)
    sibling = 2 * xx + 1 - core

    def remote(src, dst, ssem, rsem, h, q):
        c = pltpu.make_async_remote_copy(
            src_ref=src, dst_ref=dst, send_sem=ssem, recv_sem=rsem,
            device_id=(h, q), device_id_type=MESH,
        )
        c.start()

    def signal(sem, h, q):
        pl.semaphore_signal(sem, inc=1, device_id=(h, q), device_id_type=MESH)

    y_line = [(lax.rem(yy + d, 4) * 4 + zz, qblk) for d in (1, 3, 2)]
    z_line = [(yy * 4 + lax.rem(zz + d, 4), qblk) for d in (1, 3, 2)]
    x_line = [(head, lax.rem(qblk + d, 8)) for d in range(1, 8)]

    place = (xx, yy, zz)
    peers = (
        [(head, 2 * lax.rem(xx + d, 4) + core) for d in (1, 3, 2)], y_line, z_line,
    )
    lines, outbox, inbox = (lines_x, lines_y, lines_z), (out_x, out_y, out_z), (in_x, in_y, in_z)
    ybox, backbox = (ret_x, ret_y, ret_z), (back_x, back_y, back_z)
    sums, others = (sum_x, sum_y, sum_z), (got_x, got_y, got_z)

    def rows32(i):
        return pl.ds(pl.multiple_of(i * 32, 32), 32)

    barrier = pltpu.get_barrier_semaphore()
    for h, q in x_line + y_line + z_line:
        signal(barrier, h, q)
    smalls = [
        pltpu.make_async_copy(src, dst, small_sem.at[i]) for i, (src, dst) in enumerate((
            (ids_in, ids_ref), (rw_in, rw_ref), (vis_in, vis_ref), (res_in, res_ref), (gain_in, gain_ref)))
    ]
    for c in smalls:
        c.start()
    pl.semaphore_wait(barrier, 13)

    for d in (1, 3, 2):
        z2 = lax.rem(zz + d, 4)
        remote(q_ref.at[:, z2], q_buf.at[zz], q_send, q_recv.at[zz], yy * 4 + z2, qblk)
    for j, src in enumerate((key_ref, value_ref)):
        remote(src.at[yy], kv.at[qblk, j], kv_send, kv_recv.at[qblk], head, sibling)
        for dx in (1, 3, 2):
            peer = 2 * lax.rem(xx + dx, 4) + core
            remote(src.at[yy], kv.at[qblk, j], kv_send, kv_recv.at[qblk], head, peer)
    for c in smalls:
        c.wait()
    own = jnp.concatenate([ids_ref[...].astype(F32), rw_ref[...]], axis=0)
    own_info[...] = jnp.concatenate([own, jnp.zeros((16, 96), F32)], axis=1)
    for a in range(3):
        info[a, place[a]] = own_info[...]
        for h, q in peers[a]:
            remote(own_info, info.at[a, place[a]], info_send, info_recv.at[a], h, q)
    def w_rows(z, first, count):
        return pl.ds(pl.multiple_of(z * 256 + first, 16), count)

    mine16 = 128 + core * 64 + xx * 16
    half = (slice(0, 1024), slice(1024, 2048))
    for c in range(2):
        for first, count, sems in ((mine16, 16, wx_recv), (core * 64, 64, wz_recv)):
            for d in (1, 3, 2):
                z2 = lax.rem(zz + d, 4)
                remote(w_ref.at[w_rows(0, first, count), half[c]], w_buf.at[c, w_rows(zz, first, count)],
                       w_send, sems.at[c, zz], yy * 4 + z2, qblk)
    for j, src in enumerate((key_ref, value_ref)):
        pltpu.make_async_copy(src.at[yy], kv.at[qblk, j], own_sem).start()
    pltpu.make_async_copy(q_ref.at[:, zz], q_buf.at[zz], q_recv.at[zz]).start()
    for h, q in y_line:
        signal(plane_sem, h, q)
    for c in range(2):
        pltpu.make_async_copy(w_ref.at[:, half[c]], w_buf.at[c, w_rows(zz, 0, 256)], w_sem).start()
    w_copies = [
        pltpu.make_async_copy(src.at[0], dst, e_sem.at[i])
        for i, (src, dst) in enumerate(((wg_ref, wg), (wu_ref, wu), (wd_ref, wd)))
    ]
    for c in w_copies:
        c.start()
    pl.semaphore_wait(plane_sem, 3)
    for h, q in z_line:
        signal(all_sem, h, q)
    lane = iota((8, 128), 1)
    seen_all = jnp.zeros((8, 128), jnp.int32)
    for i in range(4):
        block = jnp.broadcast_to(vis_ref[:, i * 128:(i + 1) * 128], (8, 128))
        block = pltpu.roll(block, lax.rem((i - zz) * 32 + 128, 128), 1)
        seen_all = jnp.where(lane // 32 == i, block, seen_all)
    seen_all = jnp.concatenate([seen_all, seen_all], axis=1)[:1]

    wait_bytes(kv.at[qblk], own_sem)
    for d in range(4):
        z2 = lax.rem(zz + d, 4)
        wait_bytes(q_buf.at[z2], q_recv.at[z2])
        q = q_buf[z2].reshape(128, 2 * HD).astype(F32)
        q_t[z2, :, :128] = q[:, :HD].T.astype(BF16)
        q_t[z2, :, 128:] = q[:, HD:].T.astype(BF16)

    top[...] = jnp.full(top.shape, NEG, F32)
    den[...] = jnp.zeros(den.shape, F32)
    acc[...] = jnp.zeros(acc.shape, F32)

    for dx in (0, 1, 3, 2):
        chip = lax.rem(xx + dx, 4)
        if dx:
            mine = 2 * chip + core
            wait_bytes(kv.at[mine], kv_recv.at[mine])
            remote(kv.at[mine], kv.at[mine], kv_send, kv_recv.at[mine], head, sibling)
        other = 2 * chip + 1 - core
        wait_bytes(kv.at[other], kv_recv.at[other])
        keys = kv[pl.ds(2 * chip, 2), 0].reshape(512, HD)
        vt[...] = kv[pl.ds(2 * chip, 2), 1].reshape(512, HD).astype(F32).T.astype(BF16)
        base = chip * 512

        def rows(i, carry, keys=keys, base=base):
            cols = pl.ds(pl.multiple_of(i * 256, 256), 256)
            s = dot(keys, q_t[i])
            s = jnp.where(iota(s.shape, 0) < seen_all - base, s, NEG)
            old = top[:, cols]
            new = jnp.maximum(old, jnp.max(s, axis=0, keepdims=True))
            p = jnp.exp2((s - new) * QSCALE)
            scale = jnp.exp2((old - new) * QSCALE)
            top[:, cols] = new
            den[:, cols] = den[:, cols] * scale + jnp.sum(p, axis=0, keepdims=True)
            acc[:, cols] = acc[:, cols] * scale + dot(vt[...], p.astype(BF16))
            return carry

        lax.fori_loop(0, 4, rows, 0, unroll=True)

        if dx in FORWARD:
            c = FORWARD.index(dx)
            for d in (1, 3, 2):
                z2 = lax.rem(zz + d, 4)
                here = w_buf.at[c, w_rows(z2, mine16, 16)]
                wait_bytes(here, wx_recv.at[c, z2])
                for ex in (1, 3, 2):
                    peer = 2 * lax.rem(xx + ex, 4) + core
                    remote(here, here, w_send, wf_recv.at[c, z2], head, peer)

    for n in range(8):
        cols = slice(n * HD, (n + 1) * HD)
        att[n // 2, :, (n % 2) * HD:(n % 2 + 1) * HD] = (acc[:, cols] / den[:, cols]).T.astype(BF16)

    wait_bytes(w_buf.at[:, w_rows(zz, 0, 256)], w_sem)
    for c in range(2):
        for d in (1, 3, 2):
            z2 = lax.rem(zz + d, 4)
            here = w_buf.at[c, w_rows(z2, 128 + core * 64, 64)]
            wait_bytes(w_buf.at[c, w_rows(z2, 0, 48)], wf_recv.at[c, z2])
            remote(here, here, w_send, ws_recv.at[c, z2, 1], head, sibling)
            here = w_buf.at[c, w_rows(z2, core * 64, 64)]
            wait_bytes(here, wz_recv.at[c, z2])
            remote(here, here, w_send, ws_recv.at[c, z2, 0], head, sibling)
        total[...] = dot(att[zz], w_buf[c, w_rows(zz, 0, 256), :])
        for d in (1, 3, 2):
            z2 = lax.rem(zz + d, 4)
            for i in range(2):
                wait_bytes(w_buf.at[c, w_rows(z2, i * 128 + (1 - core) * 64, 64)], ws_recv.at[c, z2, i])
            if d != 2:
                total[...] += dot(att[z2], w_buf[c, w_rows(z2, 0, 256), :])
        for n in (2 * c, 2 * c + 1):
            f = slice((n % 2) * 512, (n % 2 + 1) * 512)
            last = total[:, f] + dot(att[z2], w_buf[c, w_rows(z2, 0, 256), f])
            part[n] = last.reshape(4, 32, 512).astype(BF16)
            for d in (2, 1, 3):
                y2 = lax.rem(yy + d, 4)
                remote(part.at[n, y2], got.at[n, yy], send1, recv1.at[yy], y2 * 4 + zz, qblk)

    for a in range(3):
        wait_bytes(info.at[a, pl.ds(0, 3)], info_recv.at[a])
        route(a, head, qblk, info, pick, tab)

    h = [
        res_ref[:, n * 512:(n + 1) * 512].astype(F32) + part[n, yy].astype(F32) for n in range(4)
    ]
    for d in (1, 3, 2):
        y2 = lax.rem(yy + d, 4)
        wait_bytes(got.at[:, y2], recv1.at[y2])
        h = [h[n] + got[n, y2].astype(F32) for n in range(4)]
    square = sum(jnp.sum(v * v, axis=1, keepdims=True) for v in h)
    rs = lax.rsqrt(square * (1.0 / D) + 1e-6)
    for n in range(4):
        hid[:, n * 512:(n + 1) * 512] = h[n]
    for a, f in enumerate(FEATURES):
        here = lines[a].at[rows32(place[a])]
        here[...] = (hid[:, f] * rs * gain_ref[:, f]).astype(BF16)
        for h, q in peers[a]:
            remote(here, here, line_send.at[a], line_recv.at[a], h, q)
    pl.semaphore_wait(all_sem, 3)
    for a in range(3):
        wait_bytes(lines[a].at[pl.ds(0, 96)], line_recv.at[a])

    def dispatch(m, carry):
        for a in range(3):
            h, q = partner(a, head, qblk, m, 1)
            remote(outbox[a].at[rows16(m)], inbox[a].at[rows16(m)], send3.at[a], recv3.at[a, m // 16], h, q)
        return carry

    for r in range(2):
        block = pl.ds(r * 256, 256)
        for a in range(3):
            outbox[a][block] = dot(pick[a, block], lines[a][...]).astype(BF16)
            if r == 0:
                pltpu.make_async_copy(outbox[a].at[rows16(0)], inbox[a].at[rows16(0)], recv3.at[a, 0]).start()
        lax.fori_loop(max(r * 16, 1), r * 16 + 16, dispatch, 0)

    for a in range(3):
        sort[a] = one_hot(source(a, head, qblk, iota((256, 256), 1)) == iota((256, 256), 0))
        unsort[a] = one_hot(source(a, head, qblk, iota((256, 256), 0)) == iota((256, 256), 1))
        route_back(a, tab, mix)
    for c in w_copies:
        c.wait()

    def one_round(r, carry):
        block = pl.ds(pl.multiple_of(r * 256, 256), 256)
        for a, f in enumerate(FEATURES):
            wait_bytes(inbox[a].at[block], recv3.at[a, r])
            x_buf[:, f] = dot(sort[a], inbox[a][block]).astype(BF16)
        gate = dot(x_buf[...], wg[...])
        up = dot(x_buf[...], wu[...])
        hidden = (gate / (1.0 + jnp.exp(-gate)) * up).astype(BF16)
        y_buf[...] = dot(hidden, wd[...]).astype(BF16)
        for a, f in enumerate(FEATURES):
            ybox[a][block] = dot(unsort[a], y_buf[:, f]).astype(BF16)

        def send_back(m, carry):
            for a in range(3):
                h, q = partner(a, head, qblk, m, -1)
                remote(ybox[a].at[rows16(m)], backbox[a].at[rows16(m)], send4.at[a], recv4.at[a, r], h, q)
            return carry

        @pl.when(r == 0)
        def _():
            for a in range(3):
                pltpu.make_async_copy(ybox[a].at[rows16(0)], backbox[a].at[rows16(0)], recv4.at[a, 0]).start()

        lax.fori_loop(jnp.maximum(r * 16, 1), r * 16 + 16, send_back, 0)
        return carry

    lax.fori_loop(0, 2, one_round, 0)

    for a in range(3):
        mixed = jnp.zeros((128, WIDTH[a]), F32)
        for r in range(2):
            block = slice(r * 256, (r + 1) * 256)
            wait_bytes(backbox[a].at[block], recv4.at[a, r])
            mixed += dot(mix[a, 0, :, block], backbox[a][block]) + dot(mix[a, 1, :, block], backbox[a][block])
        sums[a][...] = mixed.astype(BF16)
        for d, (h, q) in zip((1, 3, 2), peers[a]):
            remote(sums[a].at[rows32(lax.rem(place[a] + d, 4))], others[a].at[rows32(place[a])],
                   sum_send.at[a], sum_recv.at[a], h, q)
    for a, f in enumerate(FEATURES):
        v = hid[:, f] + sums[a][rows32(place[a])].astype(F32)
        wait_bytes(others[a].at[pl.ds(0, 96)], sum_recv.at[a])
        for d in (1, 3, 2):
            v += others[a][rows32(lax.rem(place[a] + d, 4))].astype(F32)
        out_ref[:, f] = v.astype(BF16)
    wait_bytes(kv.at[pl.ds(0, 7)], kv_send)
    wait_bytes(q_buf.at[pl.ds(0, 3)], q_send)
    wait_bytes(w_buf.at[:, pl.ds(0, 768)], w_send)
    wait_bytes(part.at[:, pl.ds(0, 3)], send1)
    wait_bytes(info.at[:, pl.ds(0, 3)], info_send)
    for a in range(3):
        wait_bytes(lines[a].at[pl.ds(0, 96)], line_send.at[a])
        wait_bytes(outbox[a].at[pl.ds(0, 31 * 16)], send3.at[a])
        wait_bytes(ybox[a].at[pl.ds(0, 31 * 16)], send4.at[a])
        wait_bytes(sums[a].at[pl.ds(0, 96)], sum_send.at[a])


def per_device(
    residual, queries, key_cache, value_cache, visible_len, out_weight, norm_gain,
    expert_ids, route_weights, w_gate, w_up, w_down,
):
    vmem, hbm = pl.BlockSpec(memory_space=pltpu.VMEM), pl.BlockSpec(memory_space=pl.ANY)
    dma, scratch = pltpu.SemaphoreType.DMA, pltpu.VMEM
    return pl.pallas_call(
        layer_kernel,
        out_shape=jax.ShapeDtypeStruct((32, D), BF16),
        in_specs=[hbm, hbm, hbm, hbm, hbm, hbm, hbm, hbm, hbm, hbm, hbm, hbm],
        out_specs=vmem,
        scratch_shapes=[
            scratch((1, 512), jnp.int32),
            scratch((32, D), BF16),
            scratch((1, D), F32),
            scratch((8, 32), jnp.int32),
            scratch((8, 32), F32),
            dma((5,)),
            scratch((8, 2, 256, HD), BF16),
            scratch((4, 4, 32, 2 * HD), BF16),
            scratch((4, HD, 256), BF16),
            scratch((2, 1024, 1024), BF16),
            scratch((HD, 512), BF16),
            scratch((1, 1024), F32),
            scratch((1, 1024), F32),
            scratch((HD, 1024), F32),
            scratch((4, 128, 2 * HD), BF16),
            scratch((128, 1024), F32),
            scratch((4, 4, 32, 512), BF16),
            scratch((4, 4, 32, 512), BF16),
            dma, dma, dma, dma((8,)), dma, dma((4,)), dma, dma((2, 4)), dma((2, 4)), dma((2, 4)), dma((2, 4, 2)), dma, dma((4,)),
            scratch((D, FF), BF16),
            scratch((D, FF), BF16),
            scratch((FF, D), BF16),
            scratch((32, D), F32),
            scratch((16, 128), F32),
            scratch((3, 4, 16, 128), F32),
            scratch((3, 512, 128), BF16),
            scratch((3, 3, 32, 128), F32),
            scratch((3, 2, 128, 512), BF16),
            scratch((3, 256, 256), BF16),
            scratch((3, 256, 256), BF16),
            scratch((256, D), BF16),
            scratch((256, D), BF16),
            *[scratch((rows, w), BF16) for rows in (128, 512, 512, 512, 512, 128, 128) for w in WIDTH],
            dma((3,)), dma, dma((3,)), dma((3,)), dma((3,)), dma((3,)), dma((3, 2)), dma((3,)), dma((3, 2)), dma((3,)), dma((3,)),
            pltpu.SemaphoreType.REGULAR, pltpu.SemaphoreType.REGULAR,
        ],
        compiler_params=pltpu.CompilerParams(
            collective_id=0, has_side_effects=True, vmem_limit_bytes=VMEM_LIMIT
        ),
        name="layer",
    )(
        queries.reshape(4, 4, 32, 2 * HD), key_cache, value_cache, visible_len.reshape(1, -1), residual,
        norm_gain.reshape(1, -1), expert_ids.T, route_weights.T, out_weight, w_gate, w_up, w_down,
    )


def solution(mesh):
    in_specs = (
        P(("qblk", "head"), None),
        P("qblk", "head"),
        P(None, "qblk", None),
        P(None, "qblk", None),
        P("qblk"),
        P("head", None),
        P(),
        P(("qblk", "head"), None),
        P(("qblk", "head"), None),
        P(("head", "qblk"), None, None),
        P(("head", "qblk"), None, None),
        P(("head", "qblk"), None, None),
    )
    return jax.shard_map(
        per_device, mesh=mesh, in_specs=in_specs, out_specs=P(("qblk", "head"), None),
        check_vma=False,
    )
```

```python
import jax
import jax.numpy as jnp
from jax import lax
from jax.experimental import pallas as pl
from jax.experimental.pallas import tpu as pltpu
from jax.sharding import PartitionSpec as P

MESH = pl.DeviceIdType.MESH
F32, BF16 = jnp.float32, jnp.bfloat16
D = 2048
HD = 128
FF = 768
NEG = -1e30
WIDTH = (640, 640, 768)
FORWARD = {0: (0,), 1: (1,), 3: (2,), 2: (3,)}
FEATURES = (slice(0, 640), slice(640, 1280), slice(1280, 2048))
QSCALE = HD ** (-0.5) * 1.4426950408889634
VMEM_LIMIT = 58 * 1024 * 1024


def dot(a, b):
    return jnp.dot(a, b, preferred_element_type=F32)


def dot_nt(a, b):
    return lax.dot_general(a, b, (((1,), (1,)), ((), ())), preferred_element_type=F32)


def dot_tn(a, b):
    return lax.dot_general(a, b, (((0,), (0,)), ((), ())), preferred_element_type=F32)


def wait_bytes(ref, sem):
    pltpu.make_async_copy(ref, ref, sem).wait()


def iota(shape, axis):
    return lax.broadcasted_iota(jnp.int32, shape, axis)


def rows16(i):
    return pl.ds(pl.multiple_of(i * 16, 16), 16)


def offsets(m):
    e = ((m & 15) * 5) & 15
    return e >> 2, e & 3


def partner(axis, head, qblk, m, sign):
    p, q = offsets(m)
    x, y, z = qblk >> 1, head >> 2, head & 3
    if axis == 0:
        y, z = (y + sign * p) & 3, (z + sign * q) & 3
    elif axis == 1:
        x, z = (x + sign * p) & 3, (z + sign * q) & 3
    else:
        x, y = (x + sign * p) & 3, (y + sign * q) & 3
    return y * 4 + z, x * 2 + ((qblk + (m >> 4)) & 1)


def source(axis, head, qblk, row):
    p, q = offsets(row >> 4)
    i = (row >> 2) & 3
    x, y, z = qblk >> 1, head >> 2, head & 3
    if axis == 0:
        x, y, z = i, (y - p) & 3, (z - q) & 3
    elif axis == 1:
        x, y, z = (x - p) & 3, i, (z - q) & 3
    else:
        x, y, z = (x - p) & 3, (y - q) & 3, i
    return x * 64 + y * 16 + z * 4 + (row & 3)


def one_hot(hit):
    return jnp.where(hit, 1.0, 0.0).astype(BF16)


def route(axis, head, qblk, info, pick, tab):
    line = info[axis, 0]
    for i in range(1, 4):
        line += pltpu.roll(info[axis, i], 32 * i, 1)
    expert = iota((128, 128), 0).astype(F32)
    token = iota((128, 128), 1)
    named = jnp.zeros((128, 128), F32)
    weight = jnp.zeros((128, 128), F32)
    for k in range(8):
        hit = line[k:k + 1] == expert
        named = jnp.where(hit, 1.0, named)
        weight = jnp.where(hit, line[8 + k:9 + k], weight)
    before = iota((128, 128), 0)
    later = one_hot((before < token) & (before >> 5 == token >> 5))
    rank = jnp.where(named > 0.0, dot(named.astype(BF16), later), -1.0)
    high = weight.astype(BF16)
    low = (weight - high.astype(F32)).astype(BF16)
    m_head, m_qblk = partner(axis, head, qblk, iota((32, 128), 0), 1)
    order = one_hot(m_head * 8 + m_qblk == iota((32, 128), 1))
    rank = dot(order, rank.astype(BF16))

    j = iota((512, 128), 0)
    at = dot(one_hot(iota((512, 32), 0) >> 4 == iota((512, 32), 1)), rank.astype(BF16))
    take = (at == (j & 3).astype(F32)) & ((j >> 2) & 3 == iota((512, 128), 1) >> 5)
    pick[axis] = one_hot(take)
    tab[axis, 0] = rank
    for i, w in enumerate((high, low)):
        tab[axis, 1 + i] = dot(order, w)


def route_back(axis, tab, mix):
    spread = one_hot(iota((32, 512), 1) >> 4 == iota((32, 512), 0))
    j = iota((128, 512), 1)
    at = dot(tab[axis, 0].T.astype(BF16), spread)
    take = (at == (j & 3).astype(F32)) & ((j >> 2) & 3 == iota((128, 512), 0) >> 5)
    for i in range(2):
        w = dot(tab[axis, 1 + i].T.astype(BF16), spread)
        mix[axis, i] = jnp.where(take, w, 0.0).astype(BF16)


def layer_kernel(
    q_ref, key_ref, value_ref, vis_in, res_in, gain_in, ids_in, rw_in, w_ref, wg_ref, wu_ref, wd_ref,
    out_ref,
    vis_ref, res_ref, gain_ref, ids_ref, rw_ref, small_sem,
    kv, q_buf, q_t, w_buf, vt, top, den, acc, att, total, part, got,
    own_sem, w_sem, kv_send, kv_recv, q_send, q_recv, w_send, wz_recv, wx_recv, wf_recv, ws_recv, send1, recv1,
    wg, wu, wd, hid, own_info, info, pick, tab, mix, sort, unsort, x_buf, y_buf,
    lines_x, lines_y, lines_z, out_x, out_y, out_z, in_x, in_y, in_z, ret_x, ret_y, ret_z, back_x, back_y, back_z,
    sum_x, sum_y, sum_z, got_x, got_y, got_z,
    e_sem, info_send, info_recv, line_send, line_recv, send3, recv3, send4, recv4, sum_send, sum_recv, plane_sem, all_sem,
):
    head, qblk = lax.axis_index("head"), lax.axis_index("qblk")
    yy, zz = head // 4, lax.rem(head, 4)
    xx, core = qblk // 2, lax.rem(qblk, 2)
    sibling = 2 * xx + 1 - core

    def remote(src, dst, ssem, rsem, h, q):
        c = pltpu.make_async_remote_copy(
            src_ref=src, dst_ref=dst, send_sem=ssem, recv_sem=rsem,
            device_id=(h, q), device_id_type=MESH,
        )
        c.start()

    def signal(sem, h, q):
        pl.semaphore_signal(sem, inc=1, device_id=(h, q), device_id_type=MESH)

    y_line = [(lax.rem(yy + d, 4) * 4 + zz, qblk) for d in (1, 3, 2)]
    z_line = [(yy * 4 + lax.rem(zz + d, 4), qblk) for d in (1, 3, 2)]
    x_line = [(head, lax.rem(qblk + d, 8)) for d in range(1, 8)]

    place = (xx, yy, zz)
    peers = (
        [(head, 2 * lax.rem(xx + d, 4) + core) for d in (1, 3, 2)], y_line, z_line,
    )
    lines, outbox, inbox = (lines_x, lines_y, lines_z), (out_x, out_y, out_z), (in_x, in_y, in_z)
    ybox, backbox = (ret_x, ret_y, ret_z), (back_x, back_y, back_z)
    sums, others = (sum_x, sum_y, sum_z), (got_x, got_y, got_z)

    def rows32(i):
        return pl.ds(pl.multiple_of(i * 32, 32), 32)

    barrier = pltpu.get_barrier_semaphore()
    for h, q in x_line + y_line + z_line:
        signal(barrier, h, q)
    smalls = [
        pltpu.make_async_copy(src, dst, small_sem.at[i]) for i, (src, dst) in enumerate((
            (ids_in, ids_ref), (rw_in, rw_ref), (vis_in, vis_ref), (res_in, res_ref), (gain_in, gain_ref)))
    ]
    for c in smalls:
        c.start()
    pl.semaphore_wait(barrier, 13)

    for d in (1, 3, 2):
        z2 = lax.rem(zz + d, 4)
        remote(q_ref.at[:, z2], q_buf.at[zz], q_send, q_recv.at[zz], yy * 4 + z2, qblk)
    for j, src in enumerate((key_ref, value_ref)):
        remote(src.at[yy], kv.at[qblk, j], kv_send, kv_recv.at[qblk], head, sibling)
        for dx in (1, 3, 2):
            peer = 2 * lax.rem(xx + dx, 4) + core
            remote(src.at[yy], kv.at[qblk, j], kv_send, kv_recv.at[qblk], head, peer)
    for c in smalls:
        c.wait()
    own = jnp.concatenate([ids_ref[...].astype(F32), rw_ref[...]], axis=0)
    own_info[...] = jnp.concatenate([own, jnp.zeros((16, 96), F32)], axis=1)
    for a in range(3):
        info[a, place[a]] = own_info[...]
        for h, q in peers[a]:
            remote(own_info, info.at[a, place[a]], info_send, info_recv.at[a], h, q)
    def w_rows(z, first, count):
        return pl.ds(pl.multiple_of(z * 256 + first, 16), count)

    mine16 = 128 + core * 64 + xx * 16
    quarter = [slice(c * 512, (c + 1) * 512) for c in range(4)]
    for c in range(4):
        for first, count, sems in ((mine16, 16, wx_recv), (core * 64, 64, wz_recv)):
            for d in (1, 3, 2):
                z2 = lax.rem(zz + d, 4)
                remote(w_ref.at[w_rows(0, first, count), quarter[c]], w_buf.at[c, w_rows(zz, first, count)],
                       w_send, sems.at[c, zz], yy * 4 + z2, qblk)
    for j, src in enumerate((key_ref, value_ref)):
        pltpu.make_async_copy(src.at[yy], kv.at[qblk, j], own_sem).start()
    pltpu.make_async_copy(q_ref.at[:, zz], q_buf.at[zz], q_recv.at[zz]).start()
    for h, q in y_line:
        signal(plane_sem, h, q)
    for c in range(4):
        pltpu.make_async_copy(w_ref.at[:, quarter[c]], w_buf.at[c, w_rows(zz, 0, 256)], w_sem).start()
    w_copies = [
        pltpu.make_async_copy(src.at[0], dst, e_sem.at[i])
        for i, (src, dst) in enumerate(((wg_ref, wg), (wu_ref, wu), (wd_ref, wd)))
    ]
    for c in w_copies:
        c.start()
    pl.semaphore_wait(plane_sem, 3)
    for h, q in z_line:
        signal(all_sem, h, q)
    lane = iota((8, 128), 1)
    seen_all = jnp.zeros((8, 128), jnp.int32)
    for i in range(4):
        block = jnp.broadcast_to(vis_ref[:, i * 128:(i + 1) * 128], (8, 128))
        block = pltpu.roll(block, lax.rem((i - zz) * 32 + 128, 128), 1)
        seen_all = jnp.where(lane // 32 == i, block, seen_all)
    seen_all = jnp.concatenate([seen_all, seen_all], axis=1)[:1]

    wait_bytes(kv.at[qblk], own_sem)
    for d in range(4):
        z2 = lax.rem(zz + d, 4)
        wait_bytes(q_buf.at[z2], q_recv.at[z2])
        q = q_buf[z2].reshape(128, 2 * HD).astype(F32)
        q_t[z2, :, :128] = q[:, :HD].T.astype(BF16)
        q_t[z2, :, 128:] = q[:, HD:].T.astype(BF16)

    top[...] = jnp.full(top.shape, NEG, F32)
    den[...] = jnp.zeros(den.shape, F32)
    acc[...] = jnp.zeros(acc.shape, F32)

    for dx in (0, 1, 3, 2):
        chip = lax.rem(xx + dx, 4)
        if dx:
            mine = 2 * chip + core
            wait_bytes(kv.at[mine], kv_recv.at[mine])
            remote(kv.at[mine], kv.at[mine], kv_send, kv_recv.at[mine], head, sibling)
        other = 2 * chip + 1 - core
        wait_bytes(kv.at[other], kv_recv.at[other])
        keys = kv[pl.ds(2 * chip, 2), 0].reshape(512, HD)
        vt[...] = kv[pl.ds(2 * chip, 2), 1].reshape(512, HD).astype(F32).T.astype(BF16)
        base = chip * 512

        def rows(i, carry, keys=keys, base=base):
            cols = pl.ds(pl.multiple_of(i * 256, 256), 256)
            s = dot(keys, q_t[i])
            s = jnp.where(iota(s.shape, 0) < seen_all - base, s, NEG)
            old = top[:, cols]
            new = jnp.maximum(old, jnp.max(s, axis=0, keepdims=True))
            p = jnp.exp2((s - new) * QSCALE)
            scale = jnp.exp2((old - new) * QSCALE)
            top[:, cols] = new
            den[:, cols] = den[:, cols] * scale + jnp.sum(p, axis=0, keepdims=True)
            acc[:, cols] = acc[:, cols] * scale + dot(vt[...], p.astype(BF16))
            return carry

        lax.fori_loop(0, 4, rows, 0, unroll=True)

        for c in FORWARD[dx]:
            for d in (1, 3, 2):
                z2 = lax.rem(zz + d, 4)
                here = w_buf.at[c, w_rows(z2, mine16, 16)]
                wait_bytes(here, wx_recv.at[c, z2])
                for ex in (1, 3, 2):
                    peer = 2 * lax.rem(xx + ex, 4) + core
                    remote(here, here, w_send, wf_recv.at[c, z2], head, peer)

    for n in range(8):
        cols = slice(n * HD, (n + 1) * HD)
        att[n // 2, :, (n % 2) * HD:(n % 2 + 1) * HD] = (acc[:, cols] / den[:, cols]).T.astype(BF16)

    wait_bytes(w_buf.at[:, w_rows(zz, 0, 256)], w_sem)
    for c in range(4):
        for d in (1, 3, 2):
            z2 = lax.rem(zz + d, 4)
            here = w_buf.at[c, w_rows(z2, 128 + core * 64, 64)]
            wait_bytes(w_buf.at[c, w_rows(z2, 0, 48)], wf_recv.at[c, z2])
            remote(here, here, w_send, ws_recv.at[c, z2, 1], head, sibling)
            here = w_buf.at[c, w_rows(z2, core * 64, 64)]
            wait_bytes(here, wz_recv.at[c, z2])
            remote(here, here, w_send, ws_recv.at[c, z2, 0], head, sibling)
        total[...] = dot(att[zz], w_buf[c, w_rows(zz, 0, 256), :])
        for d in (1, 3, 2):
            z2 = lax.rem(zz + d, 4)
            for i in range(2):
                wait_bytes(w_buf.at[c, w_rows(z2, i * 128 + (1 - core) * 64, 64)], ws_recv.at[c, z2, i])
            if d != 2:
                total[...] += dot(att[z2], w_buf[c, w_rows(z2, 0, 256), :])
        last = total[...] + dot(att[z2], w_buf[c, w_rows(z2, 0, 256), :])
        part[c] = last.reshape(4, 32, 512).astype(BF16)
        for d in (2, 1, 3):
            y2 = lax.rem(yy + d, 4)
            remote(part.at[c, y2], got.at[c, yy], send1, recv1.at[yy], y2 * 4 + zz, qblk)

    for a in range(3):
        wait_bytes(info.at[a, pl.ds(0, 3)], info_recv.at[a])
        route(a, head, qblk, info, pick, tab)

    h = [
        res_ref[:, n * 512:(n + 1) * 512].astype(F32) + part[n, yy].astype(F32) for n in range(4)
    ]
    for d in (1, 3, 2):
        y2 = lax.rem(yy + d, 4)
        wait_bytes(got.at[:, y2], recv1.at[y2])
        h = [h[n] + got[n, y2].astype(F32) for n in range(4)]
    square = sum(jnp.sum(v * v, axis=1, keepdims=True) for v in h)
    rs = lax.rsqrt(square * (1.0 / D) + 1e-6)
    for n in range(4):
        hid[:, n * 512:(n + 1) * 512] = h[n]
    for a, f in enumerate(FEATURES):
        here = lines[a].at[rows32(place[a])]
        here[...] = (hid[:, f] * rs * gain_ref[:, f]).astype(BF16)
        for h, q in peers[a]:
            remote(here, here, line_send.at[a], line_recv.at[a], h, q)
    pl.semaphore_wait(all_sem, 3)
    for a in range(3):
        wait_bytes(lines[a].at[pl.ds(0, 96)], line_recv.at[a])

    def dispatch(m, carry):
        for a in range(3):
            h, q = partner(a, head, qblk, m, 1)
            remote(outbox[a].at[rows16(m)], inbox[a].at[rows16(m)], send3.at[a], recv3.at[a, m // 16], h, q)
        return carry

    for r in range(2):
        block = pl.ds(r * 256, 256)
        for a in range(3):
            outbox[a][block] = dot(pick[a, block], lines[a][...]).astype(BF16)
            if r == 0:
                pltpu.make_async_copy(outbox[a].at[rows16(0)], inbox[a].at[rows16(0)], recv3.at[a, 0]).start()
        lax.fori_loop(max(r * 16, 1), r * 16 + 16, dispatch, 0)

    for a in range(3):
        sort[a] = one_hot(source(a, head, qblk, iota((256, 256), 1)) == iota((256, 256), 0))
        unsort[a] = one_hot(source(a, head, qblk, iota((256, 256), 0)) == iota((256, 256), 1))
        route_back(a, tab, mix)
    for c in w_copies:
        c.wait()

    def one_round(r, carry):
        block = pl.ds(pl.multiple_of(r * 256, 256), 256)
        for a, f in enumerate(FEATURES):
            wait_bytes(inbox[a].at[block], recv3.at[a, r])
            x_buf[:, f] = dot(sort[a], inbox[a][block]).astype(BF16)
        gate = dot(x_buf[...], wg[...])
        up = dot(x_buf[...], wu[...])
        hidden = (gate / (1.0 + jnp.exp(-gate)) * up).astype(BF16)
        y_buf[...] = dot(hidden, wd[...]).astype(BF16)
        for a, f in enumerate(FEATURES):
            ybox[a][block] = dot(unsort[a], y_buf[:, f]).astype(BF16)

        def send_back(m, carry):
            for a in range(3):
                h, q = partner(a, head, qblk, m, -1)
                remote(ybox[a].at[rows16(m)], backbox[a].at[rows16(m)], send4.at[a], recv4.at[a, r], h, q)
            return carry

        @pl.when(r == 0)
        def _():
            for a in range(3):
                pltpu.make_async_copy(ybox[a].at[rows16(0)], backbox[a].at[rows16(0)], recv4.at[a, 0]).start()

        lax.fori_loop(jnp.maximum(r * 16, 1), r * 16 + 16, send_back, 0)
        return carry

    lax.fori_loop(0, 2, one_round, 0)

    def mixed(a, r):
        block = slice(r * 256, (r + 1) * 256)
        wait_bytes(backbox[a].at[block], recv4.at[a, r])
        return dot(mix[a, 0, :, block], backbox[a][block]) + dot(mix[a, 1, :, block], backbox[a][block])

    first = [mixed(a, 0) for a in range(3)]
    for a in range(3):
        sums[a][...] = (first[a] + mixed(a, 1)).astype(BF16)
        for d, (h, q) in zip((1, 3, 2), peers[a]):
            remote(sums[a].at[rows32(lax.rem(place[a] + d, 4))], others[a].at[rows32(place[a])],
                   sum_send.at[a], sum_recv.at[a], h, q)
    for a, f in enumerate(FEATURES):
        v = hid[:, f] + sums[a][rows32(place[a])].astype(F32)
        wait_bytes(others[a].at[pl.ds(0, 96)], sum_recv.at[a])
        for d in (1, 3, 2):
            v += others[a][rows32(lax.rem(place[a] + d, 4))].astype(F32)
        out_ref[:, f] = v.astype(BF16)
    wait_bytes(kv.at[pl.ds(0, 7)], kv_send)
    wait_bytes(q_buf.at[pl.ds(0, 3)], q_send)
    wait_bytes(w_buf.at[:, pl.ds(0, 768)], w_send)
    wait_bytes(part.at[:, pl.ds(0, 3)], send1)
    wait_bytes(info.at[:, pl.ds(0, 3)], info_send)
    for a in range(3):
        wait_bytes(lines[a].at[pl.ds(0, 96)], line_send.at[a])
        wait_bytes(outbox[a].at[pl.ds(0, 31 * 16)], send3.at[a])
        wait_bytes(ybox[a].at[pl.ds(0, 31 * 16)], send4.at[a])
        wait_bytes(sums[a].at[pl.ds(0, 96)], sum_send.at[a])


def per_device(
    residual, queries, key_cache, value_cache, visible_len, out_weight, norm_gain,
    expert_ids, route_weights, w_gate, w_up, w_down,
):
    vmem, hbm = pl.BlockSpec(memory_space=pltpu.VMEM), pl.BlockSpec(memory_space=pl.ANY)
    dma, scratch = pltpu.SemaphoreType.DMA, pltpu.VMEM
    return pl.pallas_call(
        layer_kernel,
        out_shape=jax.ShapeDtypeStruct((32, D), BF16),
        in_specs=[hbm, hbm, hbm, hbm, hbm, hbm, hbm, hbm, hbm, hbm, hbm, hbm],
        out_specs=vmem,
        scratch_shapes=[
            scratch((1, 512), jnp.int32),
            scratch((32, D), BF16),
            scratch((1, D), F32),
            scratch((8, 32), jnp.int32),
            scratch((8, 32), F32),
            dma((5,)),
            scratch((8, 2, 256, HD), BF16),
            scratch((4, 4, 32, 2 * HD), BF16),
            scratch((4, HD, 256), BF16),
            scratch((4, 1024, 512), BF16),
            scratch((HD, 512), BF16),
            scratch((1, 1024), F32),
            scratch((1, 1024), F32),
            scratch((HD, 1024), F32),
            scratch((4, 128, 2 * HD), BF16),
            scratch((128, 512), F32),
            scratch((4, 4, 32, 512), BF16),
            scratch((4, 4, 32, 512), BF16),
            dma, dma, dma, dma((8,)), dma, dma((4,)), dma, dma((4, 4)), dma((4, 4)), dma((4, 4)), dma((4, 4, 2)), dma, dma((4,)),
            scratch((D, FF), BF16),
            scratch((D, FF), BF16),
            scratch((FF, D), BF16),
            scratch((32, D), F32),
            scratch((16, 128), F32),
            scratch((3, 4, 16, 128), F32),
            scratch((3, 512, 128), BF16),
            scratch((3, 3, 32, 128), F32),
            scratch((3, 2, 128, 512), BF16),
            scratch((3, 256, 256), BF16),
            scratch((3, 256, 256), BF16),
            scratch((256, D), BF16),
            scratch((256, D), BF16),
            *[scratch((rows, w), BF16) for rows in (128, 512, 512, 512, 512, 128, 128) for w in WIDTH],
            dma((3,)), dma, dma((3,)), dma((3,)), dma((3,)), dma((3,)), dma((3, 2)), dma((3,)), dma((3, 2)), dma((3,)), dma((3,)),
            pltpu.SemaphoreType.REGULAR, pltpu.SemaphoreType.REGULAR,
        ],
        compiler_params=pltpu.CompilerParams(
            collective_id=0, has_side_effects=True, vmem_limit_bytes=VMEM_LIMIT
        ),
        name="layer",
    )(
        queries.reshape(4, 4, 32, 2 * HD), key_cache, value_cache, visible_len.reshape(1, -1), residual,
        norm_gain.reshape(1, -1), expert_ids.T, route_weights.T, out_weight, w_gate, w_up, w_down,
    )


def solution(mesh):
    in_specs = (
        P(("qblk", "head"), None),
        P("qblk", "head"),
        P(None, "qblk", None),
        P(None, "qblk", None),
        P("qblk"),
        P("head", None),
        P(),
        P(("qblk", "head"), None),
        P(("qblk", "head"), None),
        P(("head", "qblk"), None, None),
        P(("head", "qblk"), None, None),
        P(("head", "qblk"), None, None),
    )
    return jax.shard_map(
        per_device, mesh=mesh, in_specs=in_specs, out_specs=P(("qblk", "head"), None),
        check_vma=False,
    )
```

```python
import jax
import jax.numpy as jnp
from jax import lax
from jax.experimental import pallas as pl
from jax.experimental.pallas import tpu as pltpu
from jax.sharding import PartitionSpec as P

MESH = pl.DeviceIdType.MESH
F32, BF16 = jnp.float32, jnp.bfloat16
D = 2048
HD = 128
FF = 768
NEG = -1e30
WIDTH = (640, 640, 768)
FORWARD = {0: (0,), 1: (1,), 3: (2,), 2: (3,)}
FEATURES = (slice(0, 640), slice(640, 1280), slice(1280, 2048))
QSCALE = HD ** (-0.5) * 1.4426950408889634
VMEM_LIMIT = 58 * 1024 * 1024


def dot(a, b):
    return jnp.dot(a, b, preferred_element_type=F32)


def dot_nt(a, b):
    return lax.dot_general(a, b, (((1,), (1,)), ((), ())), preferred_element_type=F32)


def dot_tn(a, b):
    return lax.dot_general(a, b, (((0,), (0,)), ((), ())), preferred_element_type=F32)


def wait_bytes(ref, sem):
    pltpu.make_async_copy(ref, ref, sem).wait()


def iota(shape, axis):
    return lax.broadcasted_iota(jnp.int32, shape, axis)


def rows16(i):
    return pl.ds(pl.multiple_of(i * 16, 16), 16)


def offsets(m):
    e = ((m & 15) * 5) & 15
    return e >> 2, e & 3


def partner(axis, head, qblk, m, sign):
    p, q = offsets(m)
    x, y, z = qblk >> 1, head >> 2, head & 3
    if axis == 0:
        y, z = (y + sign * p) & 3, (z + sign * q) & 3
    elif axis == 1:
        x, z = (x + sign * p) & 3, (z + sign * q) & 3
    else:
        x, y = (x + sign * p) & 3, (y + sign * q) & 3
    return y * 4 + z, x * 2 + ((qblk + (m >> 4)) & 1)


def source(axis, head, qblk, row):
    p, q = offsets(row >> 4)
    i = (row >> 2) & 3
    x, y, z = qblk >> 1, head >> 2, head & 3
    if axis == 0:
        x, y, z = i, (y - p) & 3, (z - q) & 3
    elif axis == 1:
        x, y, z = (x - p) & 3, i, (z - q) & 3
    else:
        x, y, z = (x - p) & 3, (y - q) & 3, i
    return x * 64 + y * 16 + z * 4 + (row & 3)


def one_hot(hit):
    return jnp.where(hit, 1.0, 0.0).astype(BF16)


def route(axis, head, qblk, info, pick, tab):
    line = info[axis, 0]
    for i in range(1, 4):
        line += pltpu.roll(info[axis, i], 32 * i, 1)
    expert = iota((128, 128), 0).astype(F32)
    token = iota((128, 128), 1)
    named = jnp.zeros((128, 128), F32)
    weight = jnp.zeros((128, 128), F32)
    for k in range(8):
        hit = line[k:k + 1] == expert
        named = jnp.where(hit, 1.0, named)
        weight = jnp.where(hit, line[8 + k:9 + k], weight)
    before = iota((128, 128), 0)
    later = one_hot((before < token) & (before >> 5 == token >> 5))
    rank = jnp.where(named > 0.0, dot(named.astype(BF16), later), -1.0)
    high = weight.astype(BF16)
    low = (weight - high.astype(F32)).astype(BF16)
    m_head, m_qblk = partner(axis, head, qblk, iota((32, 128), 0), 1)
    order = one_hot(m_head * 8 + m_qblk == iota((32, 128), 1))
    rank = dot(order, rank.astype(BF16))

    j = iota((512, 128), 0)
    at = dot(one_hot(iota((512, 32), 0) >> 4 == iota((512, 32), 1)), rank.astype(BF16))
    take = (at == (j & 3).astype(F32)) & ((j >> 2) & 3 == iota((512, 128), 1) >> 5)
    pick[axis] = one_hot(take)
    tab[axis, 0] = rank
    for i, w in enumerate((high, low)):
        tab[axis, 1 + i] = dot(order, w)


def route_back(axis, tab, mix):
    spread = one_hot(iota((32, 512), 1) >> 4 == iota((32, 512), 0))
    j = iota((128, 512), 1)
    at = dot(tab[axis, 0].T.astype(BF16), spread)
    take = (at == (j & 3).astype(F32)) & ((j >> 2) & 3 == iota((128, 512), 0) >> 5)
    for i in range(2):
        w = dot(tab[axis, 1 + i].T.astype(BF16), spread)
        mix[axis, i] = jnp.where(take, w, 0.0).astype(BF16)


def layer_kernel(
    q_ref, key_ref, value_ref, vis_in, res_in, gain_in, ids_in, rw_in, w_ref, wg_ref, wu_ref, wd_ref,
    out_ref,
    vis_ref, res_ref, gain_ref, ids_ref, rw_ref, small_sem,
    kv, q_buf, q_t, w_buf, vt, top, den, acc, att, total, part, got,
    own_sem, w_sem, kv_send, kv_recv, q_send, q_recv, w_send, wz_recv, wx_recv, wf_recv, ws_recv, send1, recv1,
    wg, wu, wd, hid, own_info, info, pick, tab, mix, sort, unsort, x_buf, y_buf,
    lines_x, lines_y, lines_z, out_x, out_y, out_z, in_x, in_y, in_z, ret_x, ret_y, ret_z, back_x, back_y, back_z,
    sum_x, sum_y, sum_z, got_x, got_y, got_z,
    e_sem, info_send, info_recv, line_send, line_recv, send3, recv3, send4, recv4, sum_send, sum_recv, plane_sem, all_sem,
):
    head, qblk = lax.axis_index("head"), lax.axis_index("qblk")
    yy, zz = head // 4, lax.rem(head, 4)
    xx, core = qblk // 2, lax.rem(qblk, 2)
    sibling = 2 * xx + 1 - core

    def remote(src, dst, ssem, rsem, h, q):
        c = pltpu.make_async_remote_copy(
            src_ref=src, dst_ref=dst, send_sem=ssem, recv_sem=rsem,
            device_id=(h, q), device_id_type=MESH,
        )
        c.start()

    def signal(sem, h, q):
        pl.semaphore_signal(sem, inc=1, device_id=(h, q), device_id_type=MESH)

    y_line = [(lax.rem(yy + d, 4) * 4 + zz, qblk) for d in (1, 3, 2)]
    z_line = [(yy * 4 + lax.rem(zz + d, 4), qblk) for d in (1, 3, 2)]
    x_line = [(head, lax.rem(qblk + d, 8)) for d in range(1, 8)]

    place = (xx, yy, zz)
    peers = (
        [(head, 2 * lax.rem(xx + d, 4) + core) for d in (1, 3, 2)], y_line, z_line,
    )
    lines, outbox, inbox = (lines_x, lines_y, lines_z), (out_x, out_y, out_z), (in_x, in_y, in_z)
    ybox, backbox = (ret_x, ret_y, ret_z), (back_x, back_y, back_z)
    sums, others = (sum_x, sum_y, sum_z), (got_x, got_y, got_z)

    def rows32(i):
        return pl.ds(pl.multiple_of(i * 32, 32), 32)

    barrier = pltpu.get_barrier_semaphore()
    for h, q in x_line + y_line + z_line:
        signal(barrier, h, q)
    smalls = [
        pltpu.make_async_copy(src, dst, small_sem.at[i]) for i, (src, dst) in enumerate((
            (ids_in, ids_ref), (rw_in, rw_ref), (vis_in, vis_ref), (res_in, res_ref), (gain_in, gain_ref)))
    ]
    for c in smalls:
        c.start()
    pl.semaphore_wait(barrier, 13)

    for d in (1, 3, 2):
        z2 = lax.rem(zz + d, 4)
        remote(q_ref.at[:, z2], q_buf.at[zz], q_send, q_recv.at[zz], yy * 4 + z2, qblk)
    for j, src in enumerate((key_ref, value_ref)):
        remote(src.at[yy], kv.at[qblk, j], kv_send, kv_recv.at[qblk], head, sibling)
        for dx in (1, 3, 2):
            peer = 2 * lax.rem(xx + dx, 4) + core
            remote(src.at[yy], kv.at[qblk, j], kv_send, kv_recv.at[qblk], head, peer)
    for c in smalls:
        c.wait()
    own = jnp.concatenate([ids_ref[...].astype(F32), rw_ref[...]], axis=0)
    own_info[...] = jnp.concatenate([own, jnp.zeros((16, 96), F32)], axis=1)
    for a in range(3):
        info[a, place[a]] = own_info[...]
        for h, q in peers[a]:
            remote(own_info, info.at[a, place[a]], info_send, info_recv.at[a], h, q)
    def w_rows(z, first, count):
        return pl.ds(pl.multiple_of(z * 256 + first, 16), count)

    mine16 = 128 + core * 64 + xx * 16
    quarter = [slice(c * 512, (c + 1) * 512) for c in range(4)]
    for c in range(4):
        for first, count, sems in ((mine16, 16, wx_recv), (core * 64, 64, wz_recv)):
            for d in (1, 3, 2):
                z2 = lax.rem(zz + d, 4)
                remote(w_ref.at[w_rows(0, first, count), quarter[c]], w_buf.at[c, w_rows(zz, first, count)],
                       w_send, sems.at[c, zz], yy * 4 + z2, qblk)
    for j, src in enumerate((key_ref, value_ref)):
        pltpu.make_async_copy(src.at[yy], kv.at[qblk, j], own_sem).start()
    pltpu.make_async_copy(q_ref.at[:, zz], q_buf.at[zz], q_recv.at[zz]).start()
    for h, q in y_line:
        signal(plane_sem, h, q)
    for c in range(4):
        pltpu.make_async_copy(w_ref.at[:, quarter[c]], w_buf.at[c, w_rows(zz, 0, 256)], w_sem).start()
    w_copies = [
        pltpu.make_async_copy(src.at[0], dst, e_sem.at[i])
        for i, (src, dst) in enumerate(((wg_ref, wg), (wu_ref, wu), (wd_ref, wd)))
    ]
    for c in w_copies:
        c.start()
    pl.semaphore_wait(plane_sem, 3)
    for h, q in z_line:
        signal(all_sem, h, q)
    lane = iota((8, 128), 1)
    seen_all = jnp.zeros((8, 128), jnp.int32)
    for i in range(4):
        block = jnp.broadcast_to(vis_ref[:, i * 128:(i + 1) * 128], (8, 128))
        block = pltpu.roll(block, lax.rem((i - zz) * 32 + 128, 128), 1)
        seen_all = jnp.where(lane // 32 == i, block, seen_all)
    seen_all = jnp.concatenate([seen_all, seen_all], axis=1)[:1]

    wait_bytes(kv.at[qblk], own_sem)
    for d in range(4):
        z2 = lax.rem(zz + d, 4)
        wait_bytes(q_buf.at[z2], q_recv.at[z2])
        q = q_buf[z2].reshape(128, 2 * HD).astype(F32)
        q_t[z2, :, :128] = q[:, :HD].T.astype(BF16)
        q_t[z2, :, 128:] = q[:, HD:].T.astype(BF16)

    top[...] = jnp.full(top.shape, NEG, F32)
    den[...] = jnp.zeros(den.shape, F32)
    acc[...] = jnp.zeros(acc.shape, F32)

    for dx in (0, 1, 3, 2):
        chip = lax.rem(xx + dx, 4)
        if dx:
            mine = 2 * chip + core
            wait_bytes(kv.at[mine], kv_recv.at[mine])
            remote(kv.at[mine], kv.at[mine], kv_send, kv_recv.at[mine], head, sibling)
        other = 2 * chip + 1 - core
        wait_bytes(kv.at[other], kv_recv.at[other])
        keys = kv[pl.ds(2 * chip, 2), 0].reshape(512, HD)
        vt[...] = kv[pl.ds(2 * chip, 2), 1].reshape(512, HD).astype(F32).T.astype(BF16)
        base = chip * 512

        def rows(i, carry, keys=keys, base=base):
            cols = pl.ds(pl.multiple_of(i * 256, 256), 256)
            s = dot(keys, q_t[i])
            s = jnp.where(iota(s.shape, 0) < seen_all - base, s, NEG)
            old = top[:, cols]
            new = jnp.maximum(old, jnp.max(s, axis=0, keepdims=True))
            p = jnp.exp2((s - new) * QSCALE)
            scale = jnp.exp2((old - new) * QSCALE)
            top[:, cols] = new
            den[:, cols] = den[:, cols] * scale + jnp.sum(p, axis=0, keepdims=True)
            acc[:, cols] = acc[:, cols] * scale + dot(vt[...], p.astype(BF16))
            return carry

        lax.fori_loop(0, 4, rows, 0, unroll=True)

        for c in FORWARD[dx]:
            for d in (1, 3, 2):
                z2 = lax.rem(zz + d, 4)
                here = w_buf.at[c, w_rows(z2, mine16, 16)]
                wait_bytes(here, wx_recv.at[c, z2])
                for ex in (1, 3, 2):
                    peer = 2 * lax.rem(xx + ex, 4) + core
                    remote(here, here, w_send, wf_recv.at[c, z2], head, peer)

    for n in range(8):
        cols = slice(n * HD, (n + 1) * HD)
        att[n // 2, :, (n % 2) * HD:(n % 2 + 1) * HD] = (acc[:, cols] / den[:, cols]).T.astype(BF16)

    wait_bytes(w_buf.at[:, w_rows(zz, 0, 256)], w_sem)
    for c in range(4):
        for d in (1, 3, 2):
            z2 = lax.rem(zz + d, 4)
            here = w_buf.at[c, w_rows(z2, 128 + core * 64, 64)]
            wait_bytes(w_buf.at[c, w_rows(z2, 0, 48)], wf_recv.at[c, z2])
            remote(here, here, w_send, ws_recv.at[c, z2, 1], head, sibling)
            here = w_buf.at[c, w_rows(z2, core * 64, 64)]
            wait_bytes(here, wz_recv.at[c, z2])
            remote(here, here, w_send, ws_recv.at[c, z2, 0], head, sibling)
        total[...] = dot(att[zz], w_buf[c, w_rows(zz, 0, 256), :])
        for d in (1, 3, 2):
            z2 = lax.rem(zz + d, 4)
            for i in range(2):
                wait_bytes(w_buf.at[c, w_rows(z2, i * 128 + (1 - core) * 64, 64)], ws_recv.at[c, z2, i])
            if d != 2:
                total[...] += dot(att[z2], w_buf[c, w_rows(z2, 0, 256), :])
        last = total[...] + dot(att[z2], w_buf[c, w_rows(z2, 0, 256), :])
        part[c] = last.reshape(4, 32, 512).astype(BF16)
        for d in (2, 1, 3):
            y2 = lax.rem(yy + d, 4)
            remote(part.at[c, y2], got.at[c, yy], send1, recv1.at[yy], y2 * 4 + zz, qblk)

    for a in range(3):
        wait_bytes(info.at[a, pl.ds(0, 3)], info_recv.at[a])
        route(a, head, qblk, info, pick, tab)

    h = [
        res_ref[:, n * 512:(n + 1) * 512].astype(F32) + part[n, yy].astype(F32) for n in range(4)
    ]
    for d in (1, 3, 2):
        y2 = lax.rem(yy + d, 4)
        wait_bytes(got.at[:, y2], recv1.at[y2])
        h = [h[n] + got[n, y2].astype(F32) for n in range(4)]
    square = sum(jnp.sum(v * v, axis=1, keepdims=True) for v in h)
    rs = lax.rsqrt(square * (1.0 / D) + 1e-6)
    for n in range(4):
        hid[:, n * 512:(n + 1) * 512] = h[n]
    for a, f in enumerate(FEATURES):
        here = lines[a].at[rows32(place[a])]
        here[...] = (hid[:, f] * rs * gain_ref[:, f]).astype(BF16)
        for h, q in peers[a]:
            remote(here, here, line_send.at[a], line_recv.at[a], h, q)
    pl.semaphore_wait(all_sem, 3)
    for r in range(2):
        block = pl.ds(r * 256, 256)
        for a in range(3):
            if r == 0:
                wait_bytes(lines[a].at[pl.ds(0, 96)], line_recv.at[a])
            outbox[a][block] = dot(pick[a, block], lines[a][...]).astype(BF16)
            if r == 0:
                pltpu.make_async_copy(outbox[a].at[rows16(0)], inbox[a].at[rows16(0)], recv3.at[a, 0]).start()

            def dispatch(m, carry, a=a, r=r):
                h, q = partner(a, head, qblk, m, 1)
                remote(outbox[a].at[rows16(m)], inbox[a].at[rows16(m)], send3.at[a], recv3.at[a, r], h, q)
                return carry

            lax.fori_loop(max(r * 16, 1), r * 16 + 16, dispatch, 0, unroll=True)

    for a in range(3):
        sort[a] = one_hot(source(a, head, qblk, iota((256, 256), 1)) == iota((256, 256), 0))
        unsort[a] = one_hot(source(a, head, qblk, iota((256, 256), 0)) == iota((256, 256), 1))
        route_back(a, tab, mix)
    for c in w_copies:
        c.wait()

    def one_round(r, carry):
        block = pl.ds(pl.multiple_of(r * 256, 256), 256)
        for a, f in enumerate(FEATURES):
            wait_bytes(inbox[a].at[block], recv3.at[a, r])
            x_buf[:, f] = dot(sort[a], inbox[a][block]).astype(BF16)
        gate = dot(x_buf[...], wg[...])
        up = dot(x_buf[...], wu[...])
        hidden = (gate / (1.0 + jnp.exp(-gate)) * up).astype(BF16)
        y_buf[...] = dot(hidden, wd[...]).astype(BF16)
        for a, f in enumerate(FEATURES):
            ybox[a][block] = dot(unsort[a], y_buf[:, f]).astype(BF16)

        def send_back(m, carry):
            for a in range(3):
                h, q = partner(a, head, qblk, m, -1)
                remote(ybox[a].at[rows16(m)], backbox[a].at[rows16(m)], send4.at[a], recv4.at[a, r], h, q)
            return carry

        @pl.when(r == 0)
        def _():
            for a in range(3):
                pltpu.make_async_copy(ybox[a].at[rows16(0)], backbox[a].at[rows16(0)], recv4.at[a, 0]).start()

        lax.fori_loop(jnp.maximum(r * 16, 1), r * 16 + 16, send_back, 0)
        return carry

    lax.fori_loop(0, 2, one_round, 0)

    def mixed(a, r):
        block = slice(r * 256, (r + 1) * 256)
        wait_bytes(backbox[a].at[block], recv4.at[a, r])
        return dot(mix[a, 0, :, block], backbox[a][block]) + dot(mix[a, 1, :, block], backbox[a][block])

    first = [mixed(a, 0) for a in range(3)]
    for a in range(3):
        sums[a][...] = (first[a] + mixed(a, 1)).astype(BF16)
        for d, (h, q) in zip((1, 3, 2), peers[a]):
            remote(sums[a].at[rows32(lax.rem(place[a] + d, 4))], others[a].at[rows32(place[a])],
                   sum_send.at[a], sum_recv.at[a], h, q)
    for a, f in enumerate(FEATURES):
        v = hid[:, f] + sums[a][rows32(place[a])].astype(F32)
        wait_bytes(others[a].at[pl.ds(0, 96)], sum_recv.at[a])
        for d in (1, 3, 2):
            v += others[a][rows32(lax.rem(place[a] + d, 4))].astype(F32)
        out_ref[:, f] = v.astype(BF16)
    wait_bytes(kv.at[pl.ds(0, 7)], kv_send)
    wait_bytes(q_buf.at[pl.ds(0, 3)], q_send)
    wait_bytes(w_buf.at[:, pl.ds(0, 768)], w_send)
    wait_bytes(part.at[:, pl.ds(0, 3)], send1)
    wait_bytes(info.at[:, pl.ds(0, 3)], info_send)
    for a in range(3):
        wait_bytes(lines[a].at[pl.ds(0, 96)], line_send.at[a])
        wait_bytes(outbox[a].at[pl.ds(0, 31 * 16)], send3.at[a])
        wait_bytes(ybox[a].at[pl.ds(0, 31 * 16)], send4.at[a])
        wait_bytes(sums[a].at[pl.ds(0, 96)], sum_send.at[a])


def per_device(
    residual, queries, key_cache, value_cache, visible_len, out_weight, norm_gain,
    expert_ids, route_weights, w_gate, w_up, w_down,
):
    vmem, hbm = pl.BlockSpec(memory_space=pltpu.VMEM), pl.BlockSpec(memory_space=pl.ANY)
    dma, scratch = pltpu.SemaphoreType.DMA, pltpu.VMEM
    return pl.pallas_call(
        layer_kernel,
        out_shape=jax.ShapeDtypeStruct((32, D), BF16),
        in_specs=[hbm, hbm, hbm, hbm, hbm, hbm, hbm, hbm, hbm, hbm, hbm, hbm],
        out_specs=vmem,
        scratch_shapes=[
            scratch((1, 512), jnp.int32),
            scratch((32, D), BF16),
            scratch((1, D), F32),
            scratch((8, 32), jnp.int32),
            scratch((8, 32), F32),
            dma((5,)),
            scratch((8, 2, 256, HD), BF16),
            scratch((4, 4, 32, 2 * HD), BF16),
            scratch((4, HD, 256), BF16),
            scratch((4, 1024, 512), BF16),
            scratch((HD, 512), BF16),
            scratch((1, 1024), F32),
            scratch((1, 1024), F32),
            scratch((HD, 1024), F32),
            scratch((4, 128, 2 * HD), BF16),
            scratch((128, 512), F32),
            scratch((4, 4, 32, 512), BF16),
            scratch((4, 4, 32, 512), BF16),
            dma, dma, dma, dma((8,)), dma, dma((4,)), dma, dma((4, 4)), dma((4, 4)), dma((4, 4)), dma((4, 4, 2)), dma, dma((4,)),
            scratch((D, FF), BF16),
            scratch((D, FF), BF16),
            scratch((FF, D), BF16),
            scratch((32, D), F32),
            scratch((16, 128), F32),
            scratch((3, 4, 16, 128), F32),
            scratch((3, 512, 128), BF16),
            scratch((3, 3, 32, 128), F32),
            scratch((3, 2, 128, 512), BF16),
            scratch((3, 256, 256), BF16),
            scratch((3, 256, 256), BF16),
            scratch((256, D), BF16),
            scratch((256, D), BF16),
            *[scratch((rows, w), BF16) for rows in (128, 512, 512, 512, 512, 128, 128) for w in WIDTH],
            dma((3,)), dma, dma((3,)), dma((3,)), dma((3,)), dma((3,)), dma((3, 2)), dma((3,)), dma((3, 2)), dma((3,)), dma((3,)),
            pltpu.SemaphoreType.REGULAR, pltpu.SemaphoreType.REGULAR,
        ],
        compiler_params=pltpu.CompilerParams(
            collective_id=0, has_side_effects=True, vmem_limit_bytes=VMEM_LIMIT
        ),
        name="layer",
    )(
        queries.reshape(4, 4, 32, 2 * HD), key_cache, value_cache, visible_len.reshape(1, -1), residual,
        norm_gain.reshape(1, -1), expert_ids.T, route_weights.T, out_weight, w_gate, w_up, w_down,
    )


def solution(mesh):
    in_specs = (
        P(("qblk", "head"), None),
        P("qblk", "head"),
        P(None, "qblk", None),
        P(None, "qblk", None),
        P("qblk"),
        P("head", None),
        P(),
        P(("qblk", "head"), None),
        P(("qblk", "head"), None),
        P(("head", "qblk"), None, None),
        P(("head", "qblk"), None, None),
        P(("head", "qblk"), None, None),
    )
    return jax.shard_map(
        per_device, mesh=mesh, in_specs=in_specs, out_specs=P(("qblk", "head"), None),
        check_vma=False,
    )
```

```python
import jax
import jax.numpy as jnp
from jax import lax
from jax.experimental import pallas as pl
from jax.experimental.pallas import tpu as pltpu
from jax.sharding import PartitionSpec as P

MESH = pl.DeviceIdType.MESH
F32, BF16 = jnp.float32, jnp.bfloat16
D = 2048
HD = 128
FF = 768
NEG = -1e30
WIDTH = (640, 640, 768)
FORWARD = {0: (0,), 1: (1,), 3: (2,), 2: (3,)}
FEATURES = (slice(0, 640), slice(640, 1280), slice(1280, 2048))
QSCALE = HD ** (-0.5) * 1.4426950408889634
VMEM_LIMIT = 58 * 1024 * 1024


def dot(a, b):
    return jnp.dot(a, b, preferred_element_type=F32)


def dot_nt(a, b):
    return lax.dot_general(a, b, (((1,), (1,)), ((), ())), preferred_element_type=F32)


def dot_tn(a, b):
    return lax.dot_general(a, b, (((0,), (0,)), ((), ())), preferred_element_type=F32)


def wait_bytes(ref, sem):
    pltpu.make_async_copy(ref, ref, sem).wait()


def iota(shape, axis):
    return lax.broadcasted_iota(jnp.int32, shape, axis)


def rows16(i):
    return pl.ds(pl.multiple_of(i * 16, 16), 16)


def offsets(m):
    e = ((m & 15) * 5) & 15
    return e >> 2, e & 3


def partner(axis, head, qblk, m, sign):
    p, q = offsets(m)
    x, y, z = qblk >> 1, head >> 2, head & 3
    if axis == 0:
        y, z = (y + sign * p) & 3, (z + sign * q) & 3
    elif axis == 1:
        x, z = (x + sign * p) & 3, (z + sign * q) & 3
    else:
        x, y = (x + sign * p) & 3, (y + sign * q) & 3
    return y * 4 + z, x * 2 + ((qblk + (m >> 4)) & 1)


def source(axis, head, qblk, row):
    p, q = offsets(row >> 4)
    i = (row >> 2) & 3
    x, y, z = qblk >> 1, head >> 2, head & 3
    if axis == 0:
        x, y, z = i, (y - p) & 3, (z - q) & 3
    elif axis == 1:
        x, y, z = (x - p) & 3, i, (z - q) & 3
    else:
        x, y, z = (x - p) & 3, (y - q) & 3, i
    return x * 64 + y * 16 + z * 4 + (row & 3)


def one_hot(hit):
    return jnp.where(hit, 1.0, 0.0).astype(BF16)


def route(axis, head, qblk, info, pick, tab):
    line = info[axis, 0]
    for i in range(1, 4):
        line += pltpu.roll(info[axis, i], 32 * i, 1)
    expert = iota((128, 128), 0).astype(F32)
    token = iota((128, 128), 1)
    named = jnp.zeros((128, 128), F32)
    weight = jnp.zeros((128, 128), F32)
    for k in range(8):
        hit = line[k:k + 1] == expert
        named = jnp.where(hit, 1.0, named)
        weight = jnp.where(hit, line[8 + k:9 + k], weight)
    before = iota((128, 128), 0)
    later = one_hot((before < token) & (before >> 5 == token >> 5))
    rank = jnp.where(named > 0.0, dot(named.astype(BF16), later), -1.0)
    high = weight.astype(BF16)
    low = (weight - high.astype(F32)).astype(BF16)
    m_head, m_qblk = partner(axis, head, qblk, iota((32, 128), 0), 1)
    order = one_hot(m_head * 8 + m_qblk == iota((32, 128), 1))
    rank = dot(order, rank.astype(BF16))

    j = iota((512, 128), 0)
    at = dot(one_hot(iota((512, 32), 0) >> 4 == iota((512, 32), 1)), rank.astype(BF16))
    take = (at == (j & 3).astype(F32)) & ((j >> 2) & 3 == iota((512, 128), 1) >> 5)
    pick[axis] = one_hot(take)
    tab[axis, 0] = rank
    for i, w in enumerate((high, low)):
        tab[axis, 1 + i] = dot(order, w)


def route_back(axis, tab, mix):
    spread = one_hot(iota((32, 512), 1) >> 4 == iota((32, 512), 0))
    j = iota((128, 512), 1)
    at = dot(tab[axis, 0].T.astype(BF16), spread)
    take = (at == (j & 3).astype(F32)) & ((j >> 2) & 3 == iota((128, 512), 0) >> 5)
    for i in range(2):
        w = dot(tab[axis, 1 + i].T.astype(BF16), spread)
        mix[axis, i] = jnp.where(take, w, 0.0).astype(BF16)


def layer_kernel(
    q_ref, key_ref, value_ref, vis_in, res_in, gain_in, ids_in, rw_in, w_ref, wg_ref, wu_ref, wd_ref,
    out_ref,
    vis_ref, res_ref, gain_ref, ids_ref, rw_ref, small_sem,
    kv, q_buf, q_t, w_buf, vt, top, den, acc, att, total, part, got,
    own_sem, w_sem, kv_send, kv_recv, q_send, q_recv, w_send, wz_recv, wx_recv, wf_recv, ws_recv, send1, recv1,
    wg, wu, wd, hid, own_info, info, pick, tab, mix, sort, unsort, x_buf, y_buf,
    lines_x, lines_y, lines_z, out_x, out_y, out_z, in_x, in_y, in_z, ret_x, ret_y, ret_z, back_x, back_y, back_z,
    sum_x, sum_y, sum_z, got_x, got_y, got_z,
    e_sem, info_send, info_recv, line_send, line_recv, send3, recv3, send4, recv4, sum_send, sum_recv, plane_sem, all_sem,
):
    head, qblk = lax.axis_index("head"), lax.axis_index("qblk")
    yy, zz = head // 4, lax.rem(head, 4)
    xx, core = qblk // 2, lax.rem(qblk, 2)
    sibling = 2 * xx + 1 - core

    def remote(src, dst, ssem, rsem, h, q):
        c = pltpu.make_async_remote_copy(
            src_ref=src, dst_ref=dst, send_sem=ssem, recv_sem=rsem,
            device_id=(h, q), device_id_type=MESH,
        )
        c.start()

    def signal(sem, h, q):
        pl.semaphore_signal(sem, inc=1, device_id=(h, q), device_id_type=MESH)

    y_line = [(lax.rem(yy + d, 4) * 4 + zz, qblk) for d in (1, 3, 2)]
    z_line = [(yy * 4 + lax.rem(zz + d, 4), qblk) for d in (1, 3, 2)]
    x_line = [(head, lax.rem(qblk + d, 8)) for d in range(1, 8)]

    place = (xx, yy, zz)
    peers = (
        [(head, 2 * lax.rem(xx + d, 4) + core) for d in (1, 3, 2)], y_line, z_line,
    )
    lines, outbox, inbox = (lines_x, lines_y, lines_z), (out_x, out_y, out_z), (in_x, in_y, in_z)
    ybox, backbox = (ret_x, ret_y, ret_z), (back_x, back_y, back_z)
    sums, others = (sum_x, sum_y, sum_z), (got_x, got_y, got_z)

    def rows32(i):
        return pl.ds(pl.multiple_of(i * 32, 32), 32)

    barrier = pltpu.get_barrier_semaphore()
    for h, q in x_line + y_line + z_line:
        signal(barrier, h, q)
    smalls = [
        pltpu.make_async_copy(src, dst, small_sem.at[i]) for i, (src, dst) in enumerate((
            (ids_in, ids_ref), (rw_in, rw_ref), (vis_in, vis_ref), (res_in, res_ref), (gain_in, gain_ref)))
    ]
    for c in smalls:
        c.start()
    pl.semaphore_wait(barrier, 13)

    for d in (1, 3, 2):
        z2 = lax.rem(zz + d, 4)
        remote(q_ref.at[:, z2], q_buf.at[zz], q_send, q_recv.at[zz], yy * 4 + z2, qblk)
    for j, src in enumerate((key_ref, value_ref)):
        remote(src.at[yy], kv.at[qblk, j], kv_send, kv_recv.at[qblk], head, sibling)
        for dx in (1, 3, 2):
            peer = 2 * lax.rem(xx + dx, 4) + core
            remote(src.at[yy], kv.at[qblk, j], kv_send, kv_recv.at[qblk], head, peer)
    for c in smalls:
        c.wait()
    own = jnp.concatenate([ids_ref[...].astype(F32), rw_ref[...]], axis=0)
    own_info[...] = jnp.concatenate([own, jnp.zeros((16, 96), F32)], axis=1)
    for a in range(3):
        info[a, place[a]] = own_info[...]
        for h, q in peers[a]:
            remote(own_info, info.at[a, place[a]], info_send, info_recv.at[a], h, q)
    def w_rows(z, first, count):
        return pl.ds(pl.multiple_of(z * 256 + first, 16), count)

    mine16 = 128 + core * 64 + xx * 16
    quarter = [slice(c * 512, (c + 1) * 512) for c in range(4)]
    for c in range(4):
        for first, count, sems in ((mine16, 16, wx_recv), (core * 64, 64, wz_recv)):
            for d in (1, 3, 2):
                z2 = lax.rem(zz + d, 4)
                remote(w_ref.at[w_rows(0, first, count), quarter[c]], w_buf.at[c, w_rows(zz, first, count)],
                       w_send, sems.at[c, zz], yy * 4 + z2, qblk)
    for j, src in enumerate((key_ref, value_ref)):
        pltpu.make_async_copy(src.at[yy], kv.at[qblk, j], own_sem).start()
    pltpu.make_async_copy(q_ref.at[:, zz], q_buf.at[zz], q_recv.at[zz]).start()
    for h, q in y_line:
        signal(plane_sem, h, q)
    for c in range(4):
        pltpu.make_async_copy(w_ref.at[:, quarter[c]], w_buf.at[c, w_rows(zz, 0, 256)], w_sem).start()
    w_copies = [
        pltpu.make_async_copy(src.at[0], dst, e_sem.at[i])
        for i, (src, dst) in enumerate(((wg_ref, wg), (wu_ref, wu), (wd_ref, wd)))
    ]
    for c in w_copies:
        c.start()
    pl.semaphore_wait(plane_sem, 3)
    for h, q in z_line:
        signal(all_sem, h, q)
    lane = iota((8, 128), 1)
    seen_all = jnp.zeros((8, 128), jnp.int32)
    for i in range(4):
        block = jnp.broadcast_to(vis_ref[:, i * 128:(i + 1) * 128], (8, 128))
        block = pltpu.roll(block, lax.rem((i - zz) * 32 + 128, 128), 1)
        seen_all = jnp.where(lane // 32 == i, block, seen_all)
    seen_all = jnp.concatenate([seen_all, seen_all], axis=1)[:1]

    wait_bytes(kv.at[qblk], own_sem)
    for d in range(4):
        z2 = lax.rem(zz + d, 4)
        wait_bytes(q_buf.at[z2], q_recv.at[z2])
        q = q_buf[z2].reshape(128, 2 * HD).astype(F32)
        q_t[z2, :, :128] = q[:, :HD].T.astype(BF16)
        q_t[z2, :, 128:] = q[:, HD:].T.astype(BF16)

    top[...] = jnp.full(top.shape, NEG, F32)
    den[...] = jnp.zeros(den.shape, F32)
    acc[...] = jnp.zeros(acc.shape, F32)

    for dx in (0, 1, 3, 2):
        chip = lax.rem(xx + dx, 4)
        if dx:
            mine = 2 * chip + core
            wait_bytes(kv.at[mine], kv_recv.at[mine])
            remote(kv.at[mine], kv.at[mine], kv_send, kv_recv.at[mine], head, sibling)
        other = 2 * chip + 1 - core
        wait_bytes(kv.at[other], kv_recv.at[other])
        keys = kv[pl.ds(2 * chip, 2), 0].reshape(512, HD)
        vt[...] = kv[pl.ds(2 * chip, 2), 1].reshape(512, HD).astype(F32).T.astype(BF16)
        base = chip * 512

        def rows(i, carry, keys=keys, base=base):
            cols = pl.ds(pl.multiple_of(i * 256, 256), 256)
            s = dot(keys, q_t[i])
            s = jnp.where(iota(s.shape, 0) < seen_all - base, s, NEG)
            old = top[:, cols]
            new = jnp.maximum(old, jnp.max(s, axis=0, keepdims=True))
            p = jnp.exp2((s - new) * QSCALE)
            scale = jnp.exp2((old - new) * QSCALE)
            top[:, cols] = new
            den[:, cols] = den[:, cols] * scale + jnp.sum(p, axis=0, keepdims=True)
            acc[:, cols] = acc[:, cols] * scale + dot(vt[...], p.astype(BF16))
            return carry

        lax.fori_loop(0, 4, rows, 0, unroll=True)

        for c in FORWARD[dx]:
            for d in (1, 3, 2):
                z2 = lax.rem(zz + d, 4)
                here = w_buf.at[c, w_rows(z2, mine16, 16)]
                wait_bytes(here, wx_recv.at[c, z2])
                for ex in (1, 3, 2):
                    peer = 2 * lax.rem(xx + ex, 4) + core
                    remote(here, here, w_send, wf_recv.at[c, z2], head, peer)

    for n in range(8):
        cols = slice(n * HD, (n + 1) * HD)
        att[n // 2, :, (n % 2) * HD:(n % 2 + 1) * HD] = (acc[:, cols] / den[:, cols]).T.astype(BF16)

    wait_bytes(w_buf.at[:, w_rows(zz, 0, 256)], w_sem)
    for c in range(4):
        for d in (1, 3, 2):
            z2 = lax.rem(zz + d, 4)
            here = w_buf.at[c, w_rows(z2, 128 + core * 64, 64)]
            wait_bytes(w_buf.at[c, w_rows(z2, 0, 48)], wf_recv.at[c, z2])
            remote(here, here, w_send, ws_recv.at[c, z2, 1], head, sibling)
            here = w_buf.at[c, w_rows(z2, core * 64, 64)]
            wait_bytes(here, wz_recv.at[c, z2])
            remote(here, here, w_send, ws_recv.at[c, z2, 0], head, sibling)
        total[...] = dot(att[zz], w_buf[c, w_rows(zz, 0, 256), :])
        for d in (1, 3, 2):
            z2 = lax.rem(zz + d, 4)
            for i in range(2):
                wait_bytes(w_buf.at[c, w_rows(z2, i * 128 + (1 - core) * 64, 64)], ws_recv.at[c, z2, i])
            if d != 2:
                total[...] += dot(att[z2], w_buf[c, w_rows(z2, 0, 256), :])
        last = total[...] + dot(att[z2], w_buf[c, w_rows(z2, 0, 256), :])
        part[c] = last.reshape(4, 32, 512).astype(BF16)
        for d in (2, 1, 3):
            y2 = lax.rem(yy + d, 4)
            remote(part.at[c, y2], got.at[c, yy], send1, recv1.at[yy], y2 * 4 + zz, qblk)

    for a in range(3):
        wait_bytes(info.at[a, pl.ds(0, 3)], info_recv.at[a])
        route(a, head, qblk, info, pick, tab)

    h = [
        res_ref[:, n * 512:(n + 1) * 512].astype(F32) + part[n, yy].astype(F32) for n in range(4)
    ]
    for d in (1, 3, 2):
        y2 = lax.rem(yy + d, 4)
        wait_bytes(got.at[:, y2], recv1.at[y2])
        h = [h[n] + got[n, y2].astype(F32) for n in range(4)]
    square = sum(jnp.sum(v * v, axis=1, keepdims=True) for v in h)
    rs = lax.rsqrt(square * (1.0 / D) + 1e-6)
    for n in range(4):
        hid[:, n * 512:(n + 1) * 512] = h[n]
    for a, f in enumerate(FEATURES):
        here = lines[a].at[rows32(place[a])]
        here[...] = (hid[:, f] * rs * gain_ref[:, f]).astype(BF16)
        for h, q in peers[a]:
            remote(here, here, line_send.at[a], line_recv.at[a], h, q)
    pl.semaphore_wait(all_sem, 3)
    for r in range(2):
        block = pl.ds(r * 256, 256)
        for a in range(3):
            if r == 0:
                wait_bytes(lines[a].at[pl.ds(0, 96)], line_recv.at[a])
            outbox[a][block] = dot(pick[a, block], lines[a][...]).astype(BF16)
            if r == 0:
                pltpu.make_async_copy(outbox[a].at[rows16(0)], inbox[a].at[rows16(0)], recv3.at[a, 0]).start()

            def dispatch(m, carry, a=a, r=r):
                h, q = partner(a, head, qblk, m, 1)
                remote(outbox[a].at[rows16(m)], inbox[a].at[rows16(m)], send3.at[a], recv3.at[a, r], h, q)
                return carry

            lax.fori_loop(max(r * 16, 1), r * 16 + 16, dispatch, 0, unroll=True)

    for a in range(3):
        sort[a] = one_hot(source(a, head, qblk, iota((256, 256), 1)) == iota((256, 256), 0))
        unsort[a] = one_hot(source(a, head, qblk, iota((256, 256), 0)) == iota((256, 256), 1))
        route_back(a, tab, mix)
    for c in w_copies:
        c.wait()

    def one_round(r, carry):
        block = pl.ds(pl.multiple_of(r * 256, 256), 256)
        for a, f in enumerate(FEATURES):
            wait_bytes(inbox[a].at[block], recv3.at[a, r])
            x_buf[:, f] = dot(sort[a], inbox[a][block]).astype(BF16)
        gate = dot(x_buf[...], wg[...])
        up = dot(x_buf[...], wu[...])
        hidden = (gate / (1.0 + jnp.exp(-gate)) * up).astype(BF16)
        y_buf[...] = dot(hidden, wd[...]).astype(BF16)
        for a, f in enumerate(FEATURES):
            ybox[a][block] = dot(unsort[a], y_buf[:, f]).astype(BF16)

        def send_back(m, carry):
            for a in range(3):
                h, q = partner(a, head, qblk, m, -1)
                remote(ybox[a].at[rows16(m)], backbox[a].at[rows16(m)], send4.at[a], recv4.at[a, r], h, q)
            return carry

        @pl.when(r == 0)
        def _():
            for a in range(3):
                pltpu.make_async_copy(ybox[a].at[rows16(0)], backbox[a].at[rows16(0)], recv4.at[a, 0]).start()

        @pl.when(r != 0)
        def _():
            send_back(r * 16, 0)

        lax.fori_loop(0, 15, lambda j, carry: send_back(r * 16 + 1 + j, carry), 0, unroll=True)
        return carry

    lax.fori_loop(0, 2, one_round, 0)

    def mixed(a, r):
        block = slice(r * 256, (r + 1) * 256)
        wait_bytes(backbox[a].at[block], recv4.at[a, r])
        return dot(mix[a, 0, :, block], backbox[a][block]) + dot(mix[a, 1, :, block], backbox[a][block])

    first = [mixed(a, 0) for a in range(3)]
    for a in range(3):
        sums[a][...] = (first[a] + mixed(a, 1)).astype(BF16)
        for d, (h, q) in zip((1, 3, 2), peers[a]):
            remote(sums[a].at[rows32(lax.rem(place[a] + d, 4))], others[a].at[rows32(place[a])],
                   sum_send.at[a], sum_recv.at[a], h, q)
    for a, f in enumerate(FEATURES):
        v = hid[:, f] + sums[a][rows32(place[a])].astype(F32)
        wait_bytes(others[a].at[pl.ds(0, 96)], sum_recv.at[a])
        for d in (1, 3, 2):
            v += others[a][rows32(lax.rem(place[a] + d, 4))].astype(F32)
        out_ref[:, f] = v.astype(BF16)
    wait_bytes(kv.at[pl.ds(0, 7)], kv_send)
    wait_bytes(q_buf.at[pl.ds(0, 3)], q_send)
    wait_bytes(w_buf.at[:, pl.ds(0, 768)], w_send)
    wait_bytes(part.at[:, pl.ds(0, 3)], send1)
    wait_bytes(info.at[:, pl.ds(0, 3)], info_send)
    for a in range(3):
        wait_bytes(lines[a].at[pl.ds(0, 96)], line_send.at[a])
        wait_bytes(outbox[a].at[pl.ds(0, 31 * 16)], send3.at[a])
        wait_bytes(ybox[a].at[pl.ds(0, 31 * 16)], send4.at[a])
        wait_bytes(sums[a].at[pl.ds(0, 96)], sum_send.at[a])


def per_device(
    residual, queries, key_cache, value_cache, visible_len, out_weight, norm_gain,
    expert_ids, route_weights, w_gate, w_up, w_down,
):
    vmem, hbm = pl.BlockSpec(memory_space=pltpu.VMEM), pl.BlockSpec(memory_space=pl.ANY)
    dma, scratch = pltpu.SemaphoreType.DMA, pltpu.VMEM
    return pl.pallas_call(
        layer_kernel,
        out_shape=jax.ShapeDtypeStruct((32, D), BF16),
        in_specs=[hbm, hbm, hbm, hbm, hbm, hbm, hbm, hbm, hbm, hbm, hbm, hbm],
        out_specs=vmem,
        scratch_shapes=[
            scratch((1, 512), jnp.int32),
            scratch((32, D), BF16),
            scratch((1, D), F32),
            scratch((8, 32), jnp.int32),
            scratch((8, 32), F32),
            dma((5,)),
            scratch((8, 2, 256, HD), BF16),
            scratch((4, 4, 32, 2 * HD), BF16),
            scratch((4, HD, 256), BF16),
            scratch((4, 1024, 512), BF16),
            scratch((HD, 512), BF16),
            scratch((1, 1024), F32),
            scratch((1, 1024), F32),
            scratch((HD, 1024), F32),
            scratch((4, 128, 2 * HD), BF16),
            scratch((128, 512), F32),
            scratch((4, 4, 32, 512), BF16),
            scratch((4, 4, 32, 512), BF16),
            dma, dma, dma, dma((8,)), dma, dma((4,)), dma, dma((4, 4)), dma((4, 4)), dma((4, 4)), dma((4, 4, 2)), dma, dma((4,)),
            scratch((D, FF), BF16),
            scratch((D, FF), BF16),
            scratch((FF, D), BF16),
            scratch((32, D), F32),
            scratch((16, 128), F32),
            scratch((3, 4, 16, 128), F32),
            scratch((3, 512, 128), BF16),
            scratch((3, 3, 32, 128), F32),
            scratch((3, 2, 128, 512), BF16),
            scratch((3, 256, 256), BF16),
            scratch((3, 256, 256), BF16),
            scratch((256, D), BF16),
            scratch((256, D), BF16),
            *[scratch((rows, w), BF16) for rows in (128, 512, 512, 512, 512, 128, 128) for w in WIDTH],
            dma((3,)), dma, dma((3,)), dma((3,)), dma((3,)), dma((3,)), dma((3, 2)), dma((3,)), dma((3, 2)), dma((3,)), dma((3,)),
            pltpu.SemaphoreType.REGULAR, pltpu.SemaphoreType.REGULAR,
        ],
        compiler_params=pltpu.CompilerParams(
            collective_id=0, has_side_effects=True, vmem_limit_bytes=VMEM_LIMIT
        ),
        name="layer",
    )(
        queries.reshape(4, 4, 32, 2 * HD), key_cache, value_cache, visible_len.reshape(1, -1), residual,
        norm_gain.reshape(1, -1), expert_ids.T, route_weights.T, out_weight, w_gate, w_up, w_down,
    )


def solution(mesh):
    in_specs = (
        P(("qblk", "head"), None),
        P("qblk", "head"),
        P(None, "qblk", None),
        P(None, "qblk", None),
        P("qblk"),
        P("head", None),
        P(),
        P(("qblk", "head"), None),
        P(("qblk", "head"), None),
        P(("head", "qblk"), None, None),
        P(("head", "qblk"), None, None),
        P(("head", "qblk"), None, None),
    )
    return jax.shard_map(
        per_device, mesh=mesh, in_specs=in_specs, out_specs=P(("qblk", "head"), None),
        check_vma=False,
    )
```
